1024 devices in a mesh: gx: 16 (over z_lo), gy: 8 (over y, core), gz: 8 (over z_hi, x).
Axes of the slice: x: 4, y: 4, z: 32 (z_hi: 2, z_lo: 16; z = z_hi * 16 + z_lo), core: 2. Of those that a mesh axis runs over, the one named last changes fastest.
Arguments:
- iterate: float32 [4, 128, 64, 1024], P(None, 'gx', 'gy', 'gz'), may hold values from -4 to 4
- forcing: float32 [4, 128, 64, 1024], P(None, 'gx', 'gy', 'gz'), may hold values from -6 to 6
- viscosity: float32 [3, 128, 64, 1024], P(None, 'gx', 'gy', 'gz'), may hold values from 0.1 to 10
Outputs:
- updated: float32 [4, 128, 64, 1024], P(None, 'gx', 'gy', 'gz')
The draws below stay inside these ranges and needn't reach their ends.
All inputs are finite; a program needn't handle non-finite values.
Results may differ from the reference program's by a relative error of at most 0.00002.
Values sent between devices are 32-bit elements; how exact they have to be, the bound alone decides.
No kernel may reach another device: no remote copies, remote signals or barrier semaphores. Data moves between devices by JAX's collectives and lax.ppermute only.
A program may use at most 64 MiB of HBM per device.

```python
import math
import jax
import jax.numpy as jnp

NX = 128
NY = 64
NZ = 1024


def block_scale(rng, extent, pieces, least, largest):
    loudness, own = 1.0, jax.random.fold_in(rng, 6)
    for axis_at, blocks in pieces:
        draws = jnp.exp(jax.random.uniform(jax.random.fold_in(own, axis_at), (blocks,), jnp.float32, least / len(pieces), largest / len(pieces)))
        loudness = loudness * jnp.repeat(draws, extent[axis_at] // blocks).reshape([-1 if axis == axis_at else 1 for axis in range(len(extent))])
    return loudness


def bell_draw(stream_key, shape, spread, bound, shards=(), held_as=jnp.bfloat16):
    array = spread * jax.random.normal(stream_key, shape, jnp.float32)
    if shards:
        array = array * block_scale(stream_key, shape, shards, -0.22, 0.18)
    return jnp.clip(array, -bound, bound).astype(held_as)


def setup_inputs(seed: int = 0) -> dict:
    seeds = jax.random.split(jax.random.key(seed), 4)
    return {
        "iterate": bell_draw(seeds[0], (4, NX, NY, NZ), 0.5, 4.0, ((1, 16), (2, 8), (3, 8)), jnp.float32),
        "forcing": bell_draw(seeds[1], (4, NX, NY, NZ), 1.0, 6.0, ((1, 16), (2, 8), (3, 8)), jnp.float32),
        "viscosity": jnp.clip(jnp.exp(math.log(10.0) - 4.6051702 * jax.random.uniform(seeds[2], (3, NX, NY, NZ), jnp.float32) ** block_scale(seeds[2], (3, NX, NY, NZ), ((1, 16), (2, 8), (3, 8)), -0.2, 0.2)), 0.1, 10.0),
    }


VELOCITY_DAMPING = 0.6
PRESSURE_DAMPING = 0.5


def beside(source, axis_num, offset):
    window = [slice(1, source.shape[i] - 1) for i in range(3)]
    window[axis_num] = slice(1 + offset, source.shape[axis_num] - 1 + offset)
    return source[tuple(window)]


def velocity_residual(padded, viscous, forcing, spacing):
    pressure = padded[3]
    residuals = []
    diagonals = []
    for c in range(3):
        moving = padded[c]
        eta_face = viscous[c]
        center = beside(moving, 0, 0)
        eta_center = beside(eta_face, 0, 0)
        summed = jnp.zeros_like(center)
        diagonal = jnp.zeros_like(center)
        for d in range(3):
            for s in (-1, 1):
                weight = 0.5 * (eta_center + beside(eta_face, d, s))
                summed = summed + weight * (center - beside(moving, d, s))
                diagonal = diagonal + weight
        gradient = (beside(pressure, 0, 0) - beside(pressure, c, -1)) / spacing
        residuals.append(forcing[c] - summed / (spacing * spacing) - gradient)
        diagonals.append(diagonal / (spacing * spacing))
    return jnp.stack(residuals), jnp.stack(diagonals)


def divergence(padded_velocity, spacing):
    summed = beside(padded_velocity[0], 0, 1) - beside(padded_velocity[0], 0, 0)
    for c in range(1, 3):
        summed = summed + (beside(padded_velocity[c], c, 1) - beside(padded_velocity[c], 0, 0))
    return summed / spacing


def cell_viscosity(viscous):
    summed = beside(viscous[0], 0, 0) + beside(viscous[0], 0, 1)
    for c in range(1, 3):
        summed = summed + beside(viscous[c], 0, 0) + beside(viscous[c], c, 1)
    return summed / 6.0


def pad_one(values):
    return jnp.pad(values, ((0, 0), (1, 1), (1, 1), (1, 1)))


def smooth(iterate, forcing, viscosity, spacing):
    viscous = pad_one(viscosity)
    residuals, diagonals = velocity_residual(pad_one(iterate), viscous, forcing, spacing)
    velocity = iterate[:3] + VELOCITY_DAMPING * residuals / diagonals
    mass_resid = forcing[3] + divergence(pad_one(velocity), spacing)
    pressure = iterate[3] - PRESSURE_DAMPING * cell_viscosity(viscous) * mass_resid
    return jnp.concatenate([velocity, pressure[None]], axis=0)


def residual(iterate, forcing, viscosity, spacing):
    padded = pad_one(iterate)
    residuals = velocity_residual(padded, pad_one(viscosity), forcing, spacing)[0]
    mass_resid = forcing[3] + divergence(padded[:3], spacing)
    return jnp.concatenate([residuals, mass_resid[None]], axis=0)


def restrict(values):
    extents = values.shape
    blocks = values.reshape(extents[0], extents[1] // 2, 2, extents[2] // 2, 2, extents[3] // 2, 2)
    return blocks.mean(axis=(2, 4, 6))


def prolong(values):
    return jnp.repeat(jnp.repeat(jnp.repeat(values, 2, axis=1), 2, axis=2), 2, axis=3)


def reference(iterate, forcing, viscosity):
    viscous_mid = restrict(viscosity)
    viscous_low = restrict(viscous_mid)
    finest = smooth(iterate, forcing, viscosity, 1.0)
    forcing_mid = restrict(residual(finest, forcing, viscosity, 1.0))
    middle = smooth(jnp.zeros_like(forcing_mid), forcing_mid, viscous_mid, 2.0)
    forcing_low = restrict(residual(middle, forcing_mid, viscous_mid, 2.0))
    lowest = smooth(jnp.zeros_like(forcing_low), forcing_low, viscous_low, 4.0)
    middle = smooth(middle + prolong(lowest), forcing_mid, viscous_mid, 2.0)
    finest = smooth(finest + prolong(middle), forcing, viscosity, 1.0)
    return finest
```

```python
import functools

import jax
import jax.numpy as jnp
from jax import lax
from jax.experimental import pallas as pl
from jax.experimental.pallas import tpu as pltpu
from jax.sharding import PartitionSpec as P

F32 = jnp.float32
BX, BY, BZ = 8, 8, 128
XL, XH = 2, 4
NL = BX + XL + XH
ROWS, LANES = 16, 256
ML = 14
VMEM = pl.BlockSpec(memory_space=pltpu.VMEM)
SMEM = pl.BlockSpec(memory_space=pltpu.SMEM)
PARAMS = pltpu.CompilerParams(vmem_limit_bytes=20 * 1024 * 1024)


def call(kernel, outs, scratch, *args):
    specs = [SMEM if a.dtype == jnp.int32 else VMEM for a in args]
    return pl.pallas_call(
        kernel,
        out_shape=[jax.ShapeDtypeStruct(s, F32) for s in outs],
        in_specs=specs,
        out_specs=[VMEM] * len(outs),
        scratch_shapes=[pltpu.VMEM(s, F32) for s in scratch],
        compiler_params=PARAMS,
    )(*args)


def iota(shape, dim):
    return lax.broadcasted_iota(jnp.int32, shape, dim)


def up(a, dim, by=1):
    return pltpu.roll(a, a.shape[dim] - by, dim)


def down(a, dim, by=1):
    return pltpu.roll(a, by, dim)


def lane_roll(a, by):
    by = by % a.shape[1]
    return pltpu.roll(a, by, 1) if by else a


def pack_z(place, iterate, forcing, viscosity, own, first, second):
    lane = iota((BY, BZ), 1) // 16
    odd = jnp.full((BY, BZ), place[3], jnp.int32) == 1
    at = 0
    for source, count in ((iterate, 4), (forcing, 4), (viscosity, 3)):
        for f in range(count):
            low = jnp.zeros((BY, BZ), F32)
            high = jnp.zeros((BY, BZ), F32)
            for x in range(BX):
                a = source[f, x]
                own[at, x] = a
                mine = lane == x
                low = jnp.where(mine, lane_roll(a, 16 * x - 112), low)
                high = jnp.where(mine, lane_roll(a, 16 * x), high)
            first[at] = jnp.where(odd, low, high)
            second[at] = jnp.where(odd, high, low)
            at += 1


def strips(place, first, second, f):
    odd = jnp.full((BY, BZ), place[3], jnp.int32) == 1
    a, b = first[f], second[f]
    return jnp.where(odd, b, a), jnp.where(odd, a, b)


def pack_x(place, own, first, second, to_up, to_down):
    lane = iota((BY, BZ), 1)

    def field(f, carry):
        low, high = strips(place, first, second, f)
        for i in range(XL):
            to_up[f, i] = own[f, BX - XL + i]
        to_up[f, XL] = jnp.where(lane >= 96, low, lane_roll(high, -32))
        for i in range(XH):
            to_down[f, i] = own[f, i]
        to_down[f, XH] = jnp.where(lane < 64, low, lane_roll(high, 64))
        return carry

    lax.fori_loop(0, 11, field, 0)


def pack_y(place, own, first, second, from_low, from_high, to_up, to_down):
    def field(f, carry):
        low, high = strips(place, first, second, f)
        tiles = [from_low[f, i] for i in range(XL)]
        tiles += [own[f, i] for i in range(BX)]
        tiles += [from_high[f, i] for i in range(XH)]
        tiles += [low, high, from_low[f, XL], from_high[f, XH]]
        for i, tile in enumerate(tiles):
            to_up[f, i] = tile[BY - XL :, :]
            to_down[f, i] = tile[:XH, :]
        return carry

    lax.fori_loop(0, 11, field, 0)


def inside_yz(place, rows, lanes, ny, nz, end_y, low_y, end_z, low_z, by, bz):
    y = iota((rows, lanes), 0)
    z = iota((rows, lanes), 1)
    held = ((y < end_y) | (y >= rows - low_y)) & ((z < end_z) | (z >= lanes - low_z))
    y = jnp.where(y < end_y, y, y - rows) + place[1] * by
    z = jnp.where(z < end_z, z, z - lanes) + place[2] * bz
    good = held & (y >= 0) & (y < ny) & (z >= 0) & (z < nz)
    return jnp.where(good, 1, 0)


def inside(yz, x, nx):
    ok = jnp.where((x >= 0) & (x < nx), 1, 0)
    return (yz * ok) != 0


def neighbours(low, mid, high, by=1):
    return (low, high, down(mid, 0, by), up(mid, 0, by), down(mid, 1, by), up(mid, 1, by))


def total(values):
    out = values[0]
    for v in values[1:]:
        out = out + v
    return out


def couple(e, es, vs):
    return e * total(vs) + total([a * b for a, b in zip(es, vs)])


def fine_mask_args(place, sizes):
    return inside_yz(place, ROWS, LANES, sizes[1], sizes[2], BY + XH, XL, BZ + 16, 16, BY, BZ)


def compact_matrix():
    a = iota((LANES, BZ), 0) // 2
    return jnp.where(a == iota((LANES, BZ), 1), 0.125, 0.0).astype(jnp.bfloat16)


def spread_matrix():
    a = iota((BZ, LANES), 1) // 2
    return jnp.where(a == iota((BZ, LANES), 0), 1.0, 0.0).astype(jnp.bfloat16)


def exact_dot(a, matrix):
    high = a.astype(jnp.bfloat16)
    rest = a - high.astype(F32)
    mid = rest.astype(jnp.bfloat16)
    low = (rest - mid.astype(F32)).astype(jnp.bfloat16)
    dot = functools.partial(jnp.dot, preferred_element_type=F32)
    return dot(high, matrix) + (dot(mid, matrix) + dot(low, matrix))


def fine_level(sizes, place, own, first, second, from_low, from_high, y_low, y_high, full, to_down, to_up, it, packed, rsum, tsum):
    lane = iota((ROWS, BZ), 1)

    def assemble(dest, at, f):
        low, high = strips(place, first, second, f)
        packed[0, 0:BY] = low
        packed[1, 0:BY] = high
        packed[2, 0:BY] = from_low[f, XL]
        packed[3, 0:BY] = from_high[f, XH]
        blank = jnp.zeros((2, BZ), F32)
        for i in range(4):
            packed[i, BY : BY + XH] = y_high[f, NL + i]
            packed[i, 12:14] = blank
            packed[i, 14:16] = y_low[f, NL + i]
        tiles = [packed[i] for i in range(4)]
        for l in range(NL):
            x = l - XL
            if x < 0:
                body = from_low[f, l]
                a, b = lane_roll(tiles[2], 16 - 16 * l), lane_roll(tiles[2], -(64 + 16 * l))
            elif x < BX:
                body = own[f, x]
                a, b = lane_roll(tiles[0], 112 - 16 * x), lane_roll(tiles[1], -16 * x)
            else:
                body = from_high[f, x - BX]
                a, b = lane_roll(tiles[3], 112 - 16 * (x - BX)), lane_roll(tiles[3], -(64 + 16 * (x - BX)))
            dest[at, l, 0:BY, 0:BZ] = body
            dest[at, l, BY : BY + XH, 0:BZ] = y_high[f, l]
            dest[at, l, 12:14, 0:BZ] = blank
            dest[at, l, 14:16, 0:BZ] = y_low[f, l]
            dest[at, l, :, BZ:] = jnp.where(lane >= 112, a, jnp.where(lane < 16, b, 0.0))

    def first_fields(f, carry):
        assemble(it, f, f)
        return carry

    def other_fields(f, carry):
        assemble(full, f, f)
        return carry

    lax.fori_loop(0, 4, first_fields, 0)
    lax.fori_loop(4, 11, other_fields, 0)

    yz = fine_mask_args(place, sizes)
    for i in range(4):
        full[i, 0] = jnp.zeros((ROWS, LANES), F32)
        full[i, NL - 1] = jnp.zeros((ROWS, LANES), F32)
    full[3, NL - 2] = jnp.zeros((ROWS, LANES), F32)

    def velocities(l, carry):
        good = inside(yz, place[0] * BX + l - XL, sizes[0])
        p = it[3, l]
        for c in range(3):
            u, e = it[c, l], full[8 + c, l]
            us = neighbours(it[c, l - 1], u, it[c, l + 1])
            es = neighbours(full[8 + c, l - 1], e, full[8 + c, l + 1])
            diag = 6.0 * e + total(es)
            before = it[3, l - 1] if c == 0 else down(p, c - 1)
            push = 1.2 * (full[4 + c, l] - (p - before)) + 0.6 * couple(e, es, us)
            full[c, l] = jnp.where(good, 0.4 * u + push / diag, 0.0)
        return carry

    lax.fori_loop(1, NL - 1, velocities, 0)

    def outflow(l):
        v, w = full[1, l], full[2, l]
        return (full[0, l + 1] - full[0, l]) + (up(v, 0) - v) + (up(w, 1) - w)

    def pressures(l, carry):
        good = inside(yz, place[0] * BX + l - XL, sizes[0])
        ev, ew = full[9, l], full[10, l]
        cell = (full[8, l] + full[8, l + 1]) + (ev + up(ev, 0)) + (ew + up(ew, 1))
        full[3, l] = jnp.where(good, it[3, l] - (0.5 / 6.0) * cell * (full[7, l] + outflow(l)), 0.0)
        return carry

    lax.fori_loop(1, NL - 2, pressures, 0)

    def layer_residual(c, l):
        u, e = full[c, l], full[8 + c, l]
        us = neighbours(full[c, l - 1], u, full[c, l + 1])
        es = neighbours(full[8 + c, l - 1], e, full[8 + c, l + 1])
        diag = 6.0 * e + total(es)
        p = full[3, l]
        before = full[3, l - 1] if c == 0 else down(p, c - 1)
        return full[4 + c, l] - (p - before) - 0.5 * (diag * u - couple(e, es, us))

    def residuals(m, carry):
        l = XL + 2 * m
        for c in range(3):
            rsum[c, m] = layer_residual(c, l) + layer_residual(c, l + 1)
        rsum[3, m] = (full[7, l] + outflow(l)) + (full[7, l + 1] + outflow(l + 1))
        return carry

    lax.fori_loop(0, 5, residuals, 0)
    for i in range(4):
        rsum[i, 5] = jnp.zeros((ROWS, LANES), F32)
    for c in range(3):
        for m in range(6):
            rsum[4 + c, m] = full[8 + c, XL + 2 * m] + full[8 + c, XL + 2 * m + 1]

    matrix = compact_matrix()
    for f in range(7):
        tsum[6 * f : 6 * f + 6] = exact_dot(rsum[f].reshape(6 * ROWS, LANES), matrix).reshape(6, ROWS, BZ)
    for f in range(7):
        for m in range(6):
            i = 6 * f + m
            a = tsum[i, pl.ds(0, 8, stride=2), :] + tsum[i, pl.ds(1, 8, stride=2), :]
            to_down[f, m] = a
            if m < 4:
                to_up[f, m] = a


def pack_y_mid(own, from_low, from_high, to_down, to_up):
    def field(f, carry):
        tiles = [from_low[f, i] for i in range(4)]
        tiles += [own[f, i] for i in range(4)]
        tiles += [from_high[f, i] for i in range(6)]
        for i, tile in enumerate(tiles):
            to_down[f, i] = tile
            to_up[f, i] = tile[:4, :]
        return carry

    lax.fori_loop(0, 7, field, 0)


def coarse_levels(sizes, place, fine, own, y_low, y_high, out, mid, um, dm, f2, e2, low, sm, twice, spread, g, un):
    blank = jnp.zeros((2, BZ), F32)

    def assemble(f, carry):
        for l in range(ML):
            mid[f, l, 0:4] = own[f, l, 0:4]
            mid[f, l, 4:10] = y_high[f, l, 0:6]
            mid[f, l, 10:12] = blank
            mid[f, l, 12:16] = y_low[f, l]
        return carry

    lax.fori_loop(0, 7, assemble, 0)

    shape = (ROWS, BZ)
    yz = inside_yz(place, ROWS, BZ, sizes[1] // 2, sizes[2] // 2, 10, 4, BZ // 2 + 8, 8, BY // 2, BZ // 2)
    row_even = iota(shape, 0) % 2 == 0
    lane_even = iota(shape, 1) % 2 == 0

    def mid_inside(l):
        return inside(yz, place[0] * (BX // 2) + l - 4, sizes[0] // 2)

    def first_velocities(l, carry):
        good = mid_inside(l)
        for c in range(3):
            e = mid[4 + c, l]
            diag = 6.0 * e + total(neighbours(mid[4 + c, l - 1], e, mid[4 + c, l + 1]))
            dm[c, l] = diag
            um[c, l] = jnp.where(good, 4.8 * mid[c, l] / diag, 0.0)
        return carry

    lax.fori_loop(1, 13, first_velocities, 0)

    def outflow(v, l):
        b, w = v[1, l], v[2, l]
        return (v[0, l + 1] - v[0, l]) + (up(b, 0) - b) + (up(w, 1) - w)

    def mid_cell(l):
        ev, ew = mid[5, l], mid[6, l]
        return (mid[4, l] + mid[4, l + 1]) + (ev + up(ev, 0)) + (ew + up(ew, 1))

    def first_pressures(l, carry):
        q = mid[3, l] + 0.5 * outflow(um, l)
        um[3, l] = jnp.where(mid_inside(l), (-0.5 / 6.0) * mid_cell(l) * q, 0.0)
        return carry

    lax.fori_loop(1, 12, first_pressures, 0)

    def expand(a):
        a = a + up(a, 0)
        a = jnp.where(row_even, a, down(a, 0))
        a = a + up(a, 1)
        return 0.125 * jnp.where(lane_even, a, down(a, 1))

    def layer_residual(c, l):
        u, e = um[c, l], mid[4 + c, l]
        us = neighbours(um[c, l - 1], u, um[c, l + 1])
        es = neighbours(mid[4 + c, l - 1], e, mid[4 + c, l + 1])
        p = um[3, l]
        before = um[3, l - 1] if c == 0 else down(p, c - 1)
        return mid[c, l] - 0.5 * (p - before) - 0.125 * (dm[c, l] * u - couple(e, es, us))

    def residuals(k, carry):
        l = 2 + 2 * k
        for c in range(3):
            f2[c, k] = expand(layer_residual(c, l) + layer_residual(c, l + 1))
        f2[3, k] = expand((mid[3, l] + 0.5 * outflow(um, l)) + (mid[3, l + 1] + 0.5 * outflow(um, l + 1)))
        return carry

    lax.fori_loop(0, 5, residuals, 0)

    def low_viscosity(k, carry):
        for c in range(3):
            e2[c, k] = expand(mid[4 + c, 2 * k] + mid[4 + c, 2 * k + 1])
        return carry

    lax.fori_loop(0, 7, low_viscosity, 0)

    def low_inside(k):
        return inside(yz, place[0] * (BX // 4) + k - 1, sizes[0] // 4)

    def low_velocities(k, carry):
        good = low_inside(k)
        for c in range(3):
            e = e2[c, k + 1]
            diag = 6.0 * e + total(neighbours(e2[c, k], e, e2[c, k + 2], 2))
            low[c, k] = jnp.where(good, 19.2 * f2[c, k] / diag, 0.0)
        return carry

    lax.fori_loop(0, 5, low_velocities, 0)

    def low_pressures(k, carry):
        v, w, ev, ew = low[1, k], low[2, k], e2[1, k + 1], e2[2, k + 1]
        flow = (low[0, k + 1] - low[0, k]) + (up(v, 0, 2) - v) + (up(w, 1, 2) - w)
        cell = (e2[0, k + 1] + e2[0, k + 2]) + (ev + up(ev, 0, 2)) + (ew + up(ew, 1, 2))
        low[3, k] = jnp.where(low_inside(k), (-0.5 / 6.0) * cell * (f2[3, k] + 0.25 * flow), 0.0)
        return carry

    lax.fori_loop(0, 4, low_pressures, 0)

    def corrected(k, carry):
        for i in range(3):
            um[i, 2 * k + 2] = um[i, 2 * k + 2] + low[i, k]
            um[i, 2 * k + 3] = um[i, 2 * k + 3] + low[i, k]
        return carry

    lax.fori_loop(0, 5, corrected, 0)
    for k in range(4):
        um[3, 2 * k + 2] = um[3, 2 * k + 2] + low[3, k]
        um[3, 2 * k + 3] = um[3, 2 * k + 3] + low[3, k]

    def second_velocities(l, carry):
        good = mid_inside(l)
        p = um[3, l]
        for c in range(3):
            u, e = um[c, l], mid[4 + c, l]
            us = neighbours(um[c, l - 1], u, um[c, l + 1])
            es = neighbours(mid[4 + c, l - 1], e, mid[4 + c, l + 1])
            before = um[3, l - 1] if c == 0 else down(p, c - 1)
            push = 4.8 * (mid[c, l] - 0.5 * (p - before)) + 0.6 * couple(e, es, us)
            sm[c, l] = jnp.where(good, 0.4 * u + push / dm[c, l], 0.0)
        return carry

    lax.fori_loop(3, 10, second_velocities, 0)

    def second_pressures(l, carry):
        q = mid[3, l] + 0.5 * outflow(sm, l)
        sm[3, l] = jnp.where(mid_inside(l), um[3, l] - (0.5 / 6.0) * mid_cell(l) * q, 0.0)
        return carry

    lax.fori_loop(3, 9, second_pressures, 0)

    last_row = iota((8, BZ), 0) == 7
    for i in range(4):
        for m in range(6):
            a = sm[i, 3 + m]
            a = jnp.where(last_row, a[8:16], a[0:8])
            twice[6 * i + m, pl.ds(0, 8, stride=2), :] = a
            twice[6 * i + m, pl.ds(1, 8, stride=2), :] = a
    matrix = spread_matrix()
    for i in range(4):
        wide = exact_dot(twice[6 * i : 6 * i + 6].reshape(6 * ROWS, BZ), matrix)
        spread[i] = wide.reshape(6, ROWS, LANES)

    for i in range(4):
        for j in range(11):
            g[i, j] = fine[i, j + 1] + spread[i, (j + 1) // 2]

    fyz = fine_mask_args(place, sizes)

    def last_velocities(x, carry):
        good = inside(fyz, place[0] * BX + x, sizes[0])
        p = g[3, x + 1]
        for c in range(3):
            u, e = g[c, x + 1], fine[8 + c, x + XL]
            us = neighbours(g[c, x], u, g[c, x + 2])
            es = neighbours(fine[8 + c, x + XL - 1], e, fine[8 + c, x + XL + 1])
            diag = 6.0 * e + total(es)
            before = g[3, x] if c == 0 else down(p, c - 1)
            push = 1.2 * (fine[4 + c, x + XL] - (p - before)) + 0.6 * couple(e, es, us)
            un[c, x] = jnp.where(good, 0.4 * u + push / diag, 0.0)
        return carry

    lax.fori_loop(0, 9, last_velocities, 0)

    def last_pressures(x, carry):
        l = x + XL
        ev, ew = fine[9, l], fine[10, l]
        cell = (fine[8, l] + fine[8, l + 1]) + (ev + up(ev, 0)) + (ew + up(ew, 1))
        p = g[3, x + 1] - (0.5 / 6.0) * cell * (fine[7, l] + outflow(un, x))
        out[3, x] = p[0:BY, 0:BZ]
        for c in range(3):
            out[c, x] = un[c, x, 0:BY, 0:BZ]
        return carry

    lax.fori_loop(0, BX, last_pressures, 0)


def per_device(sizes, iterate, forcing, viscosity):
    nx, ny, nz = (lax.axis_size(a) for a in ("gx", "gy", "gz"))
    at = [lax.axis_index(a) for a in ("gx", "gy", "gz")]
    place = jnp.stack(at + [at[2] % 2]).astype(jnp.int32)

    def swap(a, axis, count, start):
        pairs = []
        for i in range(start, count - 1, 2):
            pairs += [(i, i + 1), (i + 1, i)]
        return lax.ppermute(a, axis, pairs)

    def to_next(a, axis, count):
        return lax.ppermute(a, axis, [(i, i + 1) for i in range(count - 1)])

    def to_previous(a, axis, count):
        return lax.ppermute(a, axis, [(i + 1, i) for i in range(count - 1)])

    tile = (BY, BZ)
    own, first, second = call(
        pack_z, [(11, BX) + tile, (11,) + tile, (11,) + tile], [], place, iterate, forcing, viscosity
    )
    first = swap(first, "gz", nz, 1)
    second = swap(second, "gz", nz, 0)

    upward, downward = call(pack_x, [(11, XL + 1) + tile, (11, XH + 1) + tile], [], place, own, first, second)
    x_low = to_next(upward, "gx", nx)
    x_high = to_previous(downward, "gx", nx)

    upward, downward = call(
        pack_y, [(11, NL + 4, XL, BZ), (11, NL + 4, XH, BZ)], [], place, own, first, second, x_low, x_high
    )
    y_low = to_next(upward, "gy", ny)
    y_high = to_previous(downward, "gy", ny)

    fine, downward, upward = call(
        functools.partial(fine_level, sizes),
        [(11, NL, ROWS, LANES), (7, 6) + tile, (7, 4) + tile],
        [(4, NL, ROWS, LANES), (4, ROWS, BZ), (7, 6, ROWS, LANES), (42, ROWS, BZ)],
        place, own, first, second, x_low, x_high, y_low, y_high,
    )
    x_low = to_next(upward, "gx", nx)
    x_high = to_previous(downward, "gx", nx)

    downward, upward = call(pack_y_mid, [(7, ML) + tile, (7, ML, 4, BZ)], [], downward, x_low, x_high)
    y_low = to_next(upward, "gy", ny)
    y_high = to_previous(downward, "gy", ny)

    wide = (ROWS, BZ)
    (updated,) = call(
        functools.partial(coarse_levels, sizes),
        [(4, BX) + tile],
        [
            (7, ML) + wide, (4, ML) + wide, (3, ML) + wide, (4, 5) + wide, (3, 7) + wide, (4, 5) + wide,
            (4, ML) + wide, (24,) + wide, (4, 6, ROWS, LANES), (4, 11, ROWS, LANES), (3, 9, ROWS, LANES),
        ],
        place, fine, downward, y_low, y_high,
    )
    return updated


def solution(mesh):
    spec = P(None, "gx", "gy", "gz")
    sizes = (mesh.shape["gx"] * BX, mesh.shape["gy"] * BY, mesh.shape["gz"] * BZ)
    return jax.shard_map(
        functools.partial(per_device, sizes), mesh=mesh, in_specs=(spec,) * 3, out_specs=spec, check_vma=False
    )
```

```python
import functools

import jax
import jax.numpy as jnp
from jax import lax
from jax.experimental import pallas as pl
from jax.experimental.pallas import tpu as pltpu
from jax.sharding import PartitionSpec as P

F32 = jnp.float32
BX, BY, BZ = 8, 8, 128
XL, XH = 2, 4
NL = BX + XL + XH
ROWS, LANES = 16, 256
ML = 14
VMEM = pl.BlockSpec(memory_space=pltpu.VMEM)
SMEM = pl.BlockSpec(memory_space=pltpu.SMEM)
HBM = pl.BlockSpec(memory_space=pltpu.HBM)
UNROLL = True
PARAMS = pltpu.CompilerParams(vmem_limit_bytes=20 * 1024 * 1024)


def call(kernel, outs, scratch, *args, space=VMEM):
    specs = [SMEM if a.dtype == jnp.int32 else space for a in args]
    return pl.pallas_call(
        kernel,
        out_shape=[jax.ShapeDtypeStruct(s, F32) for s in outs],
        in_specs=specs,
        out_specs=[VMEM] * len(outs),
        scratch_shapes=[pltpu.VMEM(s, F32) if isinstance(s, tuple) else s for s in scratch],
        compiler_params=PARAMS,
    )(*args)


def loop(start, stop, body, carry):
    return lax.fori_loop(start, stop, body, carry, unroll=UNROLL)


def iota(shape, dim):
    return lax.broadcasted_iota(jnp.int32, shape, dim)


def up(a, dim, by=1):
    return pltpu.roll(a, a.shape[dim] - by, dim)


def down(a, dim, by=1):
    return pltpu.roll(a, by, dim)


def lane_roll(a, by):
    by = by % a.shape[1]
    return pltpu.roll(a, by, 1) if by else a


def pack_z(place, iterate, forcing, viscosity, own, first, second, sems):
    parts = ((iterate, 0, 4), (forcing, 4, 4), (viscosity, 8, 3))
    copies = [
        pltpu.make_async_copy(source, own.at[at : at + count], sems.at[i])
        for i, (source, at, count) in enumerate(parts)
    ]
    for copy in copies:
        copy.start()
    lane = iota((BY, BZ), 1) // 16
    odd = jnp.full((BY, BZ), place[3], jnp.int32) == 1
    for copy, (_, at, count) in zip(copies, parts):
        copy.wait()
        for f in range(at, at + count):
            low = jnp.zeros((BY, BZ), F32)
            high = jnp.zeros((BY, BZ), F32)
            for x in range(BX):
                a = own[f, x]
                mine = lane == x
                low = jnp.where(mine, lane_roll(a, 16 * x - 112), low)
                high = jnp.where(mine, lane_roll(a, 16 * x), high)
            first[f] = jnp.where(odd, low, high)
            second[f] = jnp.where(odd, high, low)


def strips(place, first, second, f):
    odd = jnp.full((BY, BZ), place[3], jnp.int32) == 1
    a, b = first[f], second[f]
    return jnp.where(odd, b, a), jnp.where(odd, a, b)


def pack_x(place, own, first, second, to_up, to_down):
    lane = iota((BY, BZ), 1)
    for f in range(11):
        low, high = strips(place, first, second, f)
        for i in range(XL):
            to_up[f, i] = own[f, BX - XL + i]
        to_up[f, XL] = jnp.where(lane >= 96, low, lane_roll(high, -32))
        for i in range(XH):
            to_down[f, i] = own[f, i]
        to_down[f, XH] = jnp.where(lane < 64, low, lane_roll(high, 64))


def pack_y(place, own, first, second, from_low, from_high, to_up, to_down):
    def field(f, carry):
        low, high = strips(place, first, second, f)
        tiles = [from_low[f, i] for i in range(XL)]
        tiles += [own[f, i] for i in range(BX)]
        tiles += [from_high[f, i] for i in range(XH)]
        tiles += [low, high, from_low[f, XL], from_high[f, XH]]
        for i, tile in enumerate(tiles):
            to_up[f, i] = tile[BY - XL :, :]
            to_down[f, i] = tile[:XH, :]
        return carry

    loop(0, 11, field, 0)


def inside_yz(place, rows, lanes, ny, nz, end_y, low_y, end_z, low_z, by, bz):
    y = iota((rows, lanes), 0)
    z = iota((rows, lanes), 1)
    held = ((y < end_y) | (y >= rows - low_y)) & ((z < end_z) | (z >= lanes - low_z))
    y = jnp.where(y < end_y, y, y - rows) + place[1] * by
    z = jnp.where(z < end_z, z, z - lanes) + place[2] * bz
    good = held & (y >= 0) & (y < ny) & (z >= 0) & (z < nz)
    return jnp.where(good, 1, 0)


def inside(yz, x, nx):
    ok = jnp.where((x >= 0) & (x < nx), 1, 0)
    return (yz * ok) != 0


def neighbours(low, mid, high, by=1):
    return (low, high, down(mid, 0, by), up(mid, 0, by), down(mid, 1, by), up(mid, 1, by))


def total(values):
    out = values[0]
    for v in values[1:]:
        out = out + v
    return out


def couple(e, es, vs):
    return e * total(vs) + total([a * b for a, b in zip(es, vs)])


def fine_mask_args(place, sizes):
    return inside_yz(place, ROWS, LANES, sizes[1], sizes[2], BY + XH, XL, BZ + 16, 16, BY, BZ)


def compact_matrix():
    a = iota((LANES, BZ), 0) // 2
    return jnp.where(a == iota((LANES, BZ), 1), 0.125, 0.0).astype(jnp.bfloat16)


def spread_matrix():
    a = iota((BZ, LANES), 1) // 2
    return jnp.where(a == iota((BZ, LANES), 0), 1.0, 0.0).astype(jnp.bfloat16)


def exact_dot(a, matrix):
    high = a.astype(jnp.bfloat16)
    rest = a - high.astype(F32)
    mid = rest.astype(jnp.bfloat16)
    low = (rest - mid.astype(F32)).astype(jnp.bfloat16)
    dot = functools.partial(jnp.dot, preferred_element_type=F32)
    return dot(high, matrix) + (dot(mid, matrix) + dot(low, matrix))


def kept(place, sizes):
    low = jnp.where(place[1] > 0, 1.0, 0.0).astype(F32)
    high = jnp.where(place[1] < sizes[1] // BY - 1, 1.0, 0.0).astype(F32)
    return low, high


def side_lanes(l, tiles):
    lane = iota((BY, BZ), 1)
    x = l - XL
    if x < 0:
        a, b = lane_roll(tiles[2], 16 - 16 * l), lane_roll(tiles[2], -(64 + 16 * l))
    elif x < BX:
        a, b = lane_roll(tiles[0], 112 - 16 * x), lane_roll(tiles[1], -16 * x)
    else:
        a, b = lane_roll(tiles[3], 112 - 16 * (x - BX)), lane_roll(tiles[3], -(64 + 16 * (x - BX)))
    return jnp.where(lane >= 112, a, jnp.where(lane < 16, b, 0.0))


def assemble_own(place, own, first, second, from_low, from_high, half):
    for f in range(11):
        low, high = strips(place, first, second, f)
        tiles = [low, high, from_low[f, XL], from_high[f, XH]]
        for l in range(NL):
            x = l - XL
            if x < 0:
                body = from_low[f, l]
            elif x < BX:
                body = own[f, x]
            else:
                body = from_high[f, x - BX]
            half[f, l, :, 0:BZ] = body
            half[f, l, :, BZ:] = side_lanes(l, tiles)


def fine_level(sizes, place, half, y_low, y_high, grid, full, to_down, to_up, rows, rsum, tsum):
    keep_low, keep_high = kept(place, sizes)

    def halo_rows(f, carry):
        for i in range(NL + 4):
            rows[i, 0:XH] = y_high[f, i] * keep_high
            rows[i, XH:6] = jnp.zeros((2, BZ), F32)
            rows[i, 6:8] = y_low[f, i] * keep_low
        tiles = [rows[NL + i] for i in range(4)]
        for l in range(NL):
            grid[f, l, 0:BY] = half[f, l]
            grid[f, l, BY:, 0:BZ] = rows[l]
            grid[f, l, BY:, BZ:] = side_lanes(l, tiles)
        return carry

    loop(0, 11, halo_rows, 0)

    yz = fine_mask_args(place, sizes)
    for i in range(4):
        full[i, 0] = jnp.zeros((ROWS, LANES), F32)
        full[i, NL - 1] = jnp.zeros((ROWS, LANES), F32)
    full[3, NL - 2] = jnp.zeros((ROWS, LANES), F32)

    def velocities(l, carry):
        good = inside(yz, place[0] * BX + l - XL, sizes[0])
        p = grid[3, l]
        for c in range(3):
            u, e = grid[c, l], grid[8 + c, l]
            us = neighbours(grid[c, l - 1], u, grid[c, l + 1])
            es = neighbours(grid[8 + c, l - 1], e, grid[8 + c, l + 1])
            diag = 6.0 * e + total(es)
            before = grid[3, l - 1] if c == 0 else down(p, c - 1)
            push = 1.2 * (grid[4 + c, l] - (p - before)) + 0.6 * couple(e, es, us)
            full[c, l] = jnp.where(good, 0.4 * u + push / diag, 0.0)
        return carry

    loop(1, NL - 1, velocities, 0)

    def outflow(l):
        v, w = full[1, l], full[2, l]
        return (full[0, l + 1] - full[0, l]) + (up(v, 0) - v) + (up(w, 1) - w)

    def pressures(l, carry):
        good = inside(yz, place[0] * BX + l - XL, sizes[0])
        ev, ew = grid[9, l], grid[10, l]
        cell = (grid[8, l] + grid[8, l + 1]) + (ev + up(ev, 0)) + (ew + up(ew, 1))
        full[3, l] = jnp.where(good, grid[3, l] - (0.5 / 6.0) * cell * (grid[7, l] + outflow(l)), 0.0)
        return carry

    loop(1, NL - 2, pressures, 0)

    def layer_residual(c, l):
        u, e = full[c, l], grid[8 + c, l]
        us = neighbours(full[c, l - 1], u, full[c, l + 1])
        es = neighbours(grid[8 + c, l - 1], e, grid[8 + c, l + 1])
        diag = 6.0 * e + total(es)
        p = full[3, l]
        before = full[3, l - 1] if c == 0 else down(p, c - 1)
        return grid[4 + c, l] - (p - before) - 0.5 * (diag * u - couple(e, es, us))

    def residuals(m, carry):
        l = XL + 2 * m
        for c in range(3):
            rsum[c, m] = layer_residual(c, l) + layer_residual(c, l + 1)
        rsum[3, m] = (grid[7, l] + outflow(l)) + (grid[7, l + 1] + outflow(l + 1))
        return carry

    loop(0, 5, residuals, 0)
    for i in range(4):
        rsum[i, 5] = jnp.zeros((ROWS, LANES), F32)
    for c in range(3):
        for m in range(6):
            rsum[4 + c, m] = grid[8 + c, XL + 2 * m] + grid[8 + c, XL + 2 * m + 1]

    matrix = compact_matrix()
    for f in range(7):
        tsum[6 * f : 6 * f + 6] = exact_dot(rsum[f].reshape(6 * ROWS, LANES), matrix).reshape(6, ROWS, BZ)
    for f in range(7):
        for m in range(6):
            i = 6 * f + m
            a = tsum[i, pl.ds(0, 8, stride=2), :] + tsum[i, pl.ds(1, 8, stride=2), :]
            to_down[f, m] = a
            if m < 4:
                to_up[f, m] = a


def pack_y_mid(own, from_low, from_high, to_down, to_up):
    for f in range(7):
        tiles = [from_low[f, i] for i in range(4)]
        tiles += [own[f, i] for i in range(4)]
        tiles += [from_high[f, i] for i in range(6)]
        for i, tile in enumerate(tiles):
            to_down[f, 6 * i : 6 * i + 6] = tile[:6, :]
            to_up[f, i] = tile[:4, :]
        to_down[f, 6 * ML :] = jnp.zeros((4, BZ), F32)


def coarse_levels(sizes, place, grid, fine, own, y_low, y_high, out, mid, um, dm, f2, e2, low, sm, twice, spread, g, un):
    blank = jnp.zeros((2, BZ), F32)
    keep_low, keep_high = kept(place, sizes)

    def assemble(f, carry):
        for l in range(ML):
            mid[f, l, 0:4] = own[f, l]
            mid[f, l, 4:10] = y_high[f, 6 * l : 6 * l + 6] * keep_high
            mid[f, l, 10:12] = blank
            mid[f, l, 12:16] = y_low[f, l] * keep_low
        return carry

    loop(0, 7, assemble, 0)

    shape = (ROWS, BZ)
    yz = inside_yz(place, ROWS, BZ, sizes[1] // 2, sizes[2] // 2, 10, 4, BZ // 2 + 8, 8, BY // 2, BZ // 2)
    row_even = iota(shape, 0) % 2 == 0
    lane_even = iota(shape, 1) % 2 == 0

    def mid_inside(l):
        return inside(yz, place[0] * (BX // 2) + l - 4, sizes[0] // 2)

    def first_velocities(l, carry):
        good = mid_inside(l)
        for c in range(3):
            e = mid[4 + c, l]
            diag = 6.0 * e + total(neighbours(mid[4 + c, l - 1], e, mid[4 + c, l + 1]))
            dm[c, l] = diag
            um[c, l] = jnp.where(good, 4.8 * mid[c, l] / diag, 0.0)
        return carry

    loop(1, 13, first_velocities, 0)

    def outflow(v, l):
        b, w = v[1, l], v[2, l]
        return (v[0, l + 1] - v[0, l]) + (up(b, 0) - b) + (up(w, 1) - w)

    def mid_cell(l):
        ev, ew = mid[5, l], mid[6, l]
        return (mid[4, l] + mid[4, l + 1]) + (ev + up(ev, 0)) + (ew + up(ew, 1))

    def first_pressures(l, carry):
        q = mid[3, l] + 0.5 * outflow(um, l)
        um[3, l] = jnp.where(mid_inside(l), (-0.5 / 6.0) * mid_cell(l) * q, 0.0)
        return carry

    loop(1, 12, first_pressures, 0)

    def expand(a):
        a = a + up(a, 0)
        a = jnp.where(row_even, a, down(a, 0))
        a = a + up(a, 1)
        return 0.125 * jnp.where(lane_even, a, down(a, 1))

    def layer_residual(c, l):
        u, e = um[c, l], mid[4 + c, l]
        us = neighbours(um[c, l - 1], u, um[c, l + 1])
        es = neighbours(mid[4 + c, l - 1], e, mid[4 + c, l + 1])
        p = um[3, l]
        before = um[3, l - 1] if c == 0 else down(p, c - 1)
        return mid[c, l] - 0.5 * (p - before) - 0.125 * (dm[c, l] * u - couple(e, es, us))

    def residuals(k, carry):
        l = 2 + 2 * k
        for c in range(3):
            f2[c, k] = expand(layer_residual(c, l) + layer_residual(c, l + 1))
        f2[3, k] = expand((mid[3, l] + 0.5 * outflow(um, l)) + (mid[3, l + 1] + 0.5 * outflow(um, l + 1)))
        return carry

    loop(0, 5, residuals, 0)

    def low_viscosity(k, carry):
        for c in range(3):
            e2[c, k] = expand(mid[4 + c, 2 * k] + mid[4 + c, 2 * k + 1])
        return carry

    loop(0, 7, low_viscosity, 0)

    def low_inside(k):
        return inside(yz, place[0] * (BX // 4) + k - 1, sizes[0] // 4)

    def low_velocities(k, carry):
        good = low_inside(k)
        for c in range(3):
            e = e2[c, k + 1]
            diag = 6.0 * e + total(neighbours(e2[c, k], e, e2[c, k + 2], 2))
            low[c, k] = jnp.where(good, 19.2 * f2[c, k] / diag, 0.0)
        return carry

    loop(0, 5, low_velocities, 0)

    def low_pressures(k, carry):
        v, w, ev, ew = low[1, k], low[2, k], e2[1, k + 1], e2[2, k + 1]
        flow = (low[0, k + 1] - low[0, k]) + (up(v, 0, 2) - v) + (up(w, 1, 2) - w)
        cell = (e2[0, k + 1] + e2[0, k + 2]) + (ev + up(ev, 0, 2)) + (ew + up(ew, 1, 2))
        low[3, k] = jnp.where(low_inside(k), (-0.5 / 6.0) * cell * (f2[3, k] + 0.25 * flow), 0.0)
        return carry

    loop(0, 4, low_pressures, 0)

    def corrected(k, carry):
        for i in range(3):
            um[i, 2 * k + 2] = um[i, 2 * k + 2] + low[i, k]
            um[i, 2 * k + 3] = um[i, 2 * k + 3] + low[i, k]
        return carry

    loop(0, 5, corrected, 0)
    for k in range(4):
        um[3, 2 * k + 2] = um[3, 2 * k + 2] + low[3, k]
        um[3, 2 * k + 3] = um[3, 2 * k + 3] + low[3, k]

    def second_velocities(l, carry):
        good = mid_inside(l)
        p = um[3, l]
        for c in range(3):
            u, e = um[c, l], mid[4 + c, l]
            us = neighbours(um[c, l - 1], u, um[c, l + 1])
            es = neighbours(mid[4 + c, l - 1], e, mid[4 + c, l + 1])
            before = um[3, l - 1] if c == 0 else down(p, c - 1)
            push = 4.8 * (mid[c, l] - 0.5 * (p - before)) + 0.6 * couple(e, es, us)
            sm[c, l] = jnp.where(good, 0.4 * u + push / dm[c, l], 0.0)
        return carry

    loop(3, 10, second_velocities, 0)

    def second_pressures(l, carry):
        q = mid[3, l] + 0.5 * outflow(sm, l)
        sm[3, l] = jnp.where(mid_inside(l), um[3, l] - (0.5 / 6.0) * mid_cell(l) * q, 0.0)
        return carry

    loop(3, 9, second_pressures, 0)

    last_row = iota((8, BZ), 0) == 7
    for i in range(4):
        for m in range(6):
            a = sm[i, 3 + m]
            a = jnp.where(last_row, a[8:16], a[0:8])
            twice[6 * i + m, pl.ds(0, 8, stride=2), :] = a
            twice[6 * i + m, pl.ds(1, 8, stride=2), :] = a
    matrix = spread_matrix()
    for i in range(4):
        wide = exact_dot(twice[6 * i : 6 * i + 6].reshape(6 * ROWS, BZ), matrix)
        spread[i] = wide.reshape(6, ROWS, LANES)

    for i in range(4):
        for j in range(11):
            g[i, j] = fine[i, j + 1] + spread[i, (j + 1) // 2]

    fyz = fine_mask_args(place, sizes)

    def last_velocities(x, carry):
        good = inside(fyz, place[0] * BX + x, sizes[0])
        p = g[3, x + 1]
        for c in range(3):
            u, e = g[c, x + 1], grid[8 + c, x + XL]
            us = neighbours(g[c, x], u, g[c, x + 2])
            es = neighbours(grid[8 + c, x + XL - 1], e, grid[8 + c, x + XL + 1])
            diag = 6.0 * e + total(es)
            before = g[3, x] if c == 0 else down(p, c - 1)
            push = 1.2 * (grid[4 + c, x + XL] - (p - before)) + 0.6 * couple(e, es, us)
            un[c, x] = jnp.where(good, 0.4 * u + push / diag, 0.0)
        return carry

    loop(0, 9, last_velocities, 0)

    def last_pressures(x, carry):
        l = x + XL
        ev, ew = grid[9, l], grid[10, l]
        cell = (grid[8, l] + grid[8, l + 1]) + (ev + up(ev, 0)) + (ew + up(ew, 1))
        p = g[3, x + 1] - (0.5 / 6.0) * cell * (grid[7, l] + outflow(un, x))
        out[3, x] = p[0:BY, 0:BZ]
        for c in range(3):
            out[c, x] = un[c, x, 0:BY, 0:BZ]
        return carry

    loop(0, BX, last_pressures, 0)


GRID = (11, NL, ROWS, LANES)
FINE_OUT = [GRID, (4, NL, ROWS, LANES), (7, 6, BY, BZ), (7, 4, BY, BZ)]
FINE_SCRATCH = [(NL + 4, BY, BZ), (7, 6, ROWS, LANES), (42, ROWS, BZ)]
WIDE = (ROWS, BZ)
COARSE_SCRATCH = [
    (7, ML) + WIDE, (4, ML) + WIDE, (3, ML) + WIDE, (4, 5) + WIDE, (3, 7) + WIDE, (4, 5) + WIDE,
    (4, ML) + WIDE, (24,) + WIDE, (4, 6, ROWS, LANES), (4, 11, ROWS, LANES), (3, 9, ROWS, LANES),
]


def per_device(sizes, iterate, forcing, viscosity):
    nx, ny, nz = (lax.axis_size(a) for a in ("gx", "gy", "gz"))
    at = [lax.axis_index(a) for a in ("gx", "gy", "gz")]
    place = jnp.stack(at + [at[2] % 2]).astype(jnp.int32)

    def swap(a, axis, count, start):
        pairs = []
        for i in range(start, count - 1, 2):
            pairs += [(i, i + 1), (i + 1, i)]
        return lax.ppermute(a, axis, pairs)

    def around(a, axis, count, by):
        return lax.ppermute(a, axis, [(i, (i + by) % count) for i in range(count)])

    def to_next(a, axis, count):
        return lax.ppermute(a, axis, [(i, i + 1) for i in range(count - 1)])

    def to_previous(a, axis, count):
        return lax.ppermute(a, axis, [(i + 1, i) for i in range(count - 1)])

    iterate, forcing, viscosity = (
        pltpu.with_memory_space_constraint(a, pltpu.HBM) for a in (iterate, forcing, viscosity)
    )
    tile = (BY, BZ)
    own, first, second = call(
        pack_z, [(11, BX) + tile, (11,) + tile, (11,) + tile], [pltpu.SemaphoreType.DMA((3,))],
        place, iterate, forcing, viscosity, space=HBM,
    )
    first = swap(first, "gz", nz, 1)
    second = swap(second, "gz", nz, 0)

    upward, downward = call(pack_x, [(11, XL + 1) + tile, (11, XH + 1) + tile], [], place, own, first, second)
    x_low = to_next(upward, "gx", nx)
    x_high = to_previous(downward, "gx", nx)

    upward, downward = call(
        pack_y, [(11, NL + 4, XL, BZ), (11, NL + 4, XH, BZ)], [], place, own, first, second, x_low, x_high
    )
    y_low = around(upward, "gy", ny, 1)
    y_high = around(downward, "gy", ny, -1)
    (half,) = call(assemble_own, [(11, NL, BY, LANES)], [], place, own, first, second, x_low, x_high)

    grid, fine, downward, upward = call(
        functools.partial(fine_level, sizes), FINE_OUT, FINE_SCRATCH, place, half, y_low, y_high
    )
    x_low = to_next(upward, "gx", nx)
    x_high = to_previous(downward, "gx", nx)

    downward, upward = call(pack_y_mid, [(7, 6 * ML + 4, BZ), (7, ML, 4, BZ)], [], downward, x_low, x_high)
    y_low = around(upward, "gy", ny, 1)
    y_high = around(downward, "gy", ny, -1)

    (updated,) = call(
        functools.partial(coarse_levels, sizes), [(4, BX) + tile], COARSE_SCRATCH,
        place, grid, fine, upward, y_low, y_high,
    )
    return updated


def solution(mesh):
    spec = P(None, "gx", "gy", "gz")
    sizes = (mesh.shape["gx"] * BX, mesh.shape["gy"] * BY, mesh.shape["gz"] * BZ)
    return jax.shard_map(
        functools.partial(per_device, sizes), mesh=mesh, in_specs=(spec,) * 3, out_specs=spec, check_vma=False
    )
```

```python
import functools

import jax
import jax.numpy as jnp
from jax import lax
from jax.experimental import pallas as pl
from jax.experimental.pallas import tpu as pltpu
from jax.sharding import PartitionSpec as P

F32 = jnp.float32
BX, BY, BZ = 8, 8, 128
XL, XH = 2, 4
NL = BX + XL + XH
ROWS, LANES = 16, 256
ML = 14
VMEM = pl.BlockSpec(memory_space=pltpu.VMEM)
SMEM = pl.BlockSpec(memory_space=pltpu.SMEM)
HBM = pl.BlockSpec(memory_space=pltpu.HBM)
UNROLL = True
PARAMS = pltpu.CompilerParams(vmem_limit_bytes=20 * 1024 * 1024)


def call(kernel, outs, scratch, *args, space=VMEM):
    specs = [SMEM if a.dtype == jnp.int32 else space for a in args]
    return pl.pallas_call(
        kernel,
        out_shape=[jax.ShapeDtypeStruct(s, F32) for s in outs],
        in_specs=specs,
        out_specs=[VMEM] * len(outs),
        scratch_shapes=[pltpu.VMEM(s, F32) if isinstance(s, tuple) else s for s in scratch],
        compiler_params=PARAMS,
    )(*args)


def loop(start, stop, body, carry):
    return lax.fori_loop(start, stop, body, carry, unroll=UNROLL)


def iota(shape, dim):
    return lax.broadcasted_iota(jnp.int32, shape, dim)


def up(a, dim, by=1):
    return pltpu.roll(a, a.shape[dim] - by, dim)


def down(a, dim, by=1):
    return pltpu.roll(a, by, dim)


def lane_roll(a, by):
    by = by % a.shape[1]
    return pltpu.roll(a, by, 1) if by else a


def pack_z(place, iterate, forcing, viscosity, own, first, second, sems):
    parts = ((iterate, 0, 4), (forcing, 4, 4), (viscosity, 8, 3))
    copies = [
        pltpu.make_async_copy(source, own.at[at : at + count], sems.at[i])
        for i, (source, at, count) in enumerate(parts)
    ]
    for copy in copies:
        copy.start()
    lane = iota((BY, BZ), 1) // 16
    odd = jnp.full((BY, BZ), place[3], jnp.int32) == 1
    for copy, (_, at, count) in zip(copies, parts):
        copy.wait()
        for f in range(at, at + count):
            low = jnp.zeros((BY, BZ), F32)
            high = jnp.zeros((BY, BZ), F32)
            for x in range(BX):
                a = own[f, x]
                mine = lane == x
                low = jnp.where(mine, lane_roll(a, 16 * x - 112), low)
                high = jnp.where(mine, lane_roll(a, 16 * x), high)
            first[f] = jnp.where(odd, low, high)
            second[f] = jnp.where(odd, high, low)


def strips(place, first, second, f):
    odd = jnp.full((BY, BZ), place[3], jnp.int32) == 1
    a, b = first[f], second[f]
    return jnp.where(odd, b, a), jnp.where(odd, a, b)


def pack_x(place, own, first, second, to_up, to_down):
    lane = iota((BY, BZ), 1)
    for f in range(11):
        low, high = strips(place, first, second, f)
        for i in range(XL):
            to_up[f, i] = own[f, BX - XL + i]
        to_up[f, XL] = jnp.where(lane >= 96, low, lane_roll(high, -32))
        for i in range(XH):
            to_down[f, i] = own[f, i]
        to_down[f, XH] = jnp.where(lane < 64, low, lane_roll(high, 64))


def pack_y(place, own, first, second, from_low, from_high, to_up, to_down):
    def field(f, carry):
        low, high = strips(place, first, second, f)
        tiles = [from_low[f, i] for i in range(XL)]
        tiles += [own[f, i] for i in range(BX)]
        tiles += [from_high[f, i] for i in range(XH)]
        tiles += [low, high, from_low[f, XL], from_high[f, XH]]
        for i, tile in enumerate(tiles):
            to_up[f, i] = tile[BY - XL :, :]
            to_down[f, i] = tile[:XH, :]
        return carry

    loop(0, 11, field, 0)


def inside_yz(place, rows, lanes, ny, nz, end_y, low_y, end_z, low_z, by, bz):
    y = iota((rows, lanes), 0)
    z = iota((rows, lanes), 1)
    held = ((y < end_y) | (y >= rows - low_y)) & ((z < end_z) | (z >= lanes - low_z))
    y = jnp.where(y < end_y, y, y - rows) + place[1] * by
    z = jnp.where(z < end_z, z, z - lanes) + place[2] * bz
    good = held & (y >= 0) & (y < ny) & (z >= 0) & (z < nz)
    return jnp.where(good, 1, 0)


def inside(yz, x, nx):
    ok = jnp.where((x >= 0) & (x < nx), 1, 0)
    return (yz * ok) != 0


def neighbours(low, mid, high, by=1):
    return (low, high, down(mid, 0, by), up(mid, 0, by), down(mid, 1, by), up(mid, 1, by))


def total(values):
    out = values[0]
    for v in values[1:]:
        out = out + v
    return out


def couple(e, es, vs):
    return e * total(vs) + total([a * b for a, b in zip(es, vs)])


def fine_mask_args(place, sizes):
    return inside_yz(place, ROWS, LANES, sizes[1], sizes[2], BY + XH, XL, BZ + 16, 16, BY, BZ)


def compact_matrix():
    a = iota((LANES, BZ), 0) // 2
    return jnp.where(a == iota((LANES, BZ), 1), 0.125, 0.0).astype(jnp.bfloat16)


def spread_matrix():
    a = iota((BZ, LANES), 1) // 2
    return jnp.where(a == iota((BZ, LANES), 0), 1.0, 0.0).astype(jnp.bfloat16)


def exact_dot(a, matrix):
    high = a.astype(jnp.bfloat16)
    rest = a - high.astype(F32)
    mid = rest.astype(jnp.bfloat16)
    low = (rest - mid.astype(F32)).astype(jnp.bfloat16)
    dot = functools.partial(jnp.dot, preferred_element_type=F32)
    return dot(high, matrix) + (dot(mid, matrix) + dot(low, matrix))


def kept(place, sizes):
    low = jnp.where(place[1] > 0, 1.0, 0.0).astype(F32)
    high = jnp.where(place[1] < sizes[1] // BY - 1, 1.0, 0.0).astype(F32)
    return low, high


def side_lanes(l, tiles):
    lane = iota((BY, BZ), 1)
    x = l - XL
    if x < 0:
        a, b = lane_roll(tiles[2], 16 - 16 * l), lane_roll(tiles[2], -(64 + 16 * l))
    elif x < BX:
        a, b = lane_roll(tiles[0], 112 - 16 * x), lane_roll(tiles[1], -16 * x)
    else:
        a, b = lane_roll(tiles[3], 112 - 16 * (x - BX)), lane_roll(tiles[3], -(64 + 16 * (x - BX)))
    return jnp.where(lane >= 112, a, jnp.where(lane < 16, b, 0.0))


def assemble_own(place, own, first, second, from_low, from_high, half):
    for f in range(11):
        low, high = strips(place, first, second, f)
        tiles = [low, high, from_low[f, XL], from_high[f, XH]]
        for l in range(NL):
            x = l - XL
            if x < 0:
                body = from_low[f, l]
            elif x < BX:
                body = own[f, x]
            else:
                body = from_high[f, x - BX]
            half[f, l, :, 0:BZ] = body
            half[f, l, :, BZ:] = side_lanes(l, tiles)


def pair_sums(e, high):
    return e + high, e + down(e, 0), e + up(e, 0), e + down(e, 1), e + up(e, 1)


def weigh(weights, values):
    return total([a * b for a, b in zip(weights, values)])


def fine_level(sizes, place, half, y_low, y_high, whole, full, to_down, to_up, rows, rsum, tsum):
    keep_low, keep_high = kept(place, sizes)

    def halo_rows(f, carry):
        for i in range(NL + 4):
            rows[i, 0:XH] = y_high[f, i] * keep_high
            rows[i, XH:6] = jnp.zeros((2, BZ), F32)
            rows[i, 6:8] = y_low[f, i] * keep_low
        tiles = [rows[NL + i] for i in range(4)]
        for l in range(NL):
            whole[f, l, 0:BY] = half[f, l]
            whole[f, l, BY:, 0:BZ] = rows[l]
            whole[f, l, BY:, BZ:] = side_lanes(l, tiles)
        return carry

    loop(0, 11, halo_rows, 0)

    def grid(f, l):
        return whole[f, l]

    yz = fine_mask_args(place, sizes)
    for i in range(4):
        full[i, 0] = jnp.zeros((ROWS, LANES), F32)
        full[i, NL - 1] = jnp.zeros((ROWS, LANES), F32)
    full[3, NL - 2] = jnp.zeros((ROWS, LANES), F32)

    def weights(c, l):
        e = grid(8 + c, l)
        return (e + grid(8 + c, l - 1),) + pair_sums(e, grid(8 + c, l + 1))

    def velocities(l, carry):
        good = inside(yz, place[0] * BX + l - XL, sizes[0])
        p = grid(3, l)
        for c in range(3):
            u = grid(c, l)
            us = neighbours(grid(c, l - 1), u, grid(c, l + 1))
            ks = weights(c, l)
            before = grid(3, l - 1) if c == 0 else down(p, c - 1)
            push = 1.2 * (grid(4 + c, l) - (p - before)) + 0.6 * weigh(ks, us)
            full[c, l] = jnp.where(good, 0.4 * u + push / total(ks), 0.0)
        return carry

    loop(1, NL - 1, velocities, 0)

    def outflow(l):
        v, w = full[1, l], full[2, l]
        return (full[0, l + 1] - full[0, l]) + (up(v, 0) - v) + (up(w, 1) - w)

    def pressures(l, carry):
        good = inside(yz, place[0] * BX + l - XL, sizes[0])
        ev, ew = grid(9, l), grid(10, l)
        cell = (grid(8, l) + grid(8, l + 1)) + (ev + up(ev, 0)) + (ew + up(ew, 1))
        full[3, l] = jnp.where(good, grid(3, l) - (0.5 / 6.0) * cell * (grid(7, l) + outflow(l)), 0.0)
        return carry

    loop(1, NL - 2, pressures, 0)

    def layer_residual(c, l):
        u = full[c, l]
        us = neighbours(full[c, l - 1], u, full[c, l + 1])
        ks = weights(c, l)
        p = full[3, l]
        before = full[3, l - 1] if c == 0 else down(p, c - 1)
        return grid(4 + c, l) - (p - before) - 0.5 * (total(ks) * u - weigh(ks, us))

    def residuals(m, carry):
        l = XL + 2 * m
        for c in range(3):
            rsum[c, m] = layer_residual(c, l) + layer_residual(c, l + 1)
        rsum[3, m] = (grid(7, l) + outflow(l)) + (grid(7, l + 1) + outflow(l + 1))
        return carry

    loop(0, 5, residuals, 0)
    for i in range(4):
        rsum[i, 5] = jnp.zeros((ROWS, LANES), F32)
    for c in range(3):
        for m in range(6):
            rsum[4 + c, m] = grid(8 + c, XL + 2 * m) + grid(8 + c, XL + 2 * m + 1)

    matrix = compact_matrix()
    for f in range(7):
        tsum[6 * f : 6 * f + 6] = exact_dot(rsum[f].reshape(6 * ROWS, LANES), matrix).reshape(6, ROWS, BZ)
    for f in range(7):
        for m in range(6):
            i = 6 * f + m
            a = tsum[i, pl.ds(0, 8, stride=2), :] + tsum[i, pl.ds(1, 8, stride=2), :]
            to_down[f, m] = a
            if m < 4:
                to_up[f, m] = a


def sizes_of(c):
    return (ROWS if c == 1 else BY), (LANES if c == 2 else BZ)


def last_terms(sizes, place, whole, fine, sums, base, inv, cells, pbase):
    fyz = fine_mask_args(place, sizes)

    def grid(f, l):
        return whole[f, l]

    for x in range(9):
        l = x + XL
        good = inside(fyz, place[0] * BX + x, sizes[0])
        p = fine[3, l]
        for c in range(3):
            u, e = fine[c, l], grid(8 + c, l)
            us = neighbours(fine[c, l - 1], u, fine[c, l + 1])
            xp, ym, yp, zm, zp = pair_sums(e, grid(8 + c, l + 1))
            ks = (e + grid(8 + c, l - 1), xp, ym, yp, zm, zp)
            before = fine[3, l - 1] if c == 0 else down(p, c - 1)
            push = 1.2 * (grid(4 + c, l) - (p - before)) + 0.6 * weigh(ks, us)
            over = 1.0 / total(ks)
            rows, lanes = sizes_of(c)
            for i, k in enumerate(ks):
                sums[c, i, x, 0:rows, 0:lanes] = (0.6 * k)[0:rows, 0:lanes]
            base[c, x, 0:rows, 0:lanes] = jnp.where(good, 0.4 * u + push * over, 0.0)[0:rows, 0:lanes]
            inv[c, x, 0:rows, 0:lanes] = jnp.where(good, over, 0.0)[0:rows, 0:lanes]
            if x < BX and c == 0:
                cell = e + grid(8, l + 1)
            elif x < BX:
                cell = cell + (yp if c == 1 else zp)
        if x < BX:
            cell = (0.5 / 6.0) * cell
            cells[x] = cell[0:BY, 0:BZ]
            pbase[x] = (p - cell * grid(7, l))[0:BY, 0:BZ]


def pack_y_mid(own, from_low, from_high, to_down, to_up):
    for f in range(7):
        tiles = [from_low[f, i] for i in range(4)]
        tiles += [own[f, i] for i in range(4)]
        tiles += [from_high[f, i] for i in range(6)]
        for i, tile in enumerate(tiles):
            to_down[f, 6 * i : 6 * i + 6] = tile[:6, :]
            to_up[f, i] = tile[:4, :]
        to_down[f, 6 * ML :] = jnp.zeros((4, BZ), F32)


def coarse_levels(
    sizes, place, last_sums, base, inv, cells, pbase, own, y_low, y_high, out,
    mid, sums, um, over, dm, f2, e2, low, sm, twice, spread, un,
):
    blank = jnp.zeros((2, BZ), F32)
    keep_low, keep_high = kept(place, sizes)

    def assemble(f, carry):
        for l in range(ML):
            mid[f, l, 0:4] = own[f, l]
            mid[f, l, 4:10] = y_high[f, 6 * l : 6 * l + 6] * keep_high
            mid[f, l, 10:12] = blank
            mid[f, l, 12:16] = y_low[f, l] * keep_low
        return carry

    loop(0, 7, assemble, 0)

    shape = (ROWS, BZ)
    yz = inside_yz(place, ROWS, BZ, sizes[1] // 2, sizes[2] // 2, 10, 4, BZ // 2 + 8, 8, BY // 2, BZ // 2)
    row_even = iota(shape, 0) % 2 == 0
    lane_even = iota(shape, 1) % 2 == 0

    def mid_inside(l):
        return inside(yz, place[0] * (BX // 2) + l - 4, sizes[0] // 2)

    for c in range(3):
        sums[c, 0, 1] = mid[4 + c, 0] + mid[4 + c, 1]

    def first_velocities(l, carry):
        good = mid_inside(l)
        for c in range(3):
            xp, ym, yp, zm, zp = pair_sums(mid[4 + c, l], mid[4 + c, l + 1])
            diag = total([sums[c, 0, l], xp, ym, yp, zm, zp])
            sums[c, 0, l + 1] = xp
            sums[c, 1, l] = ym
            sums[c, 2, l] = yp
            sums[c, 3, l] = zm
            sums[c, 4, l] = zp
            dm[c, l] = diag
            inverse = 1.0 / diag
            over[c, l] = inverse
            um[c, l] = jnp.where(good, 4.8 * mid[c, l] * inverse, 0.0)
        return carry

    loop(1, 13, first_velocities, 0)

    def weights(c, l):
        return (sums[c, 0, l], sums[c, 0, l + 1]) + tuple(sums[c, i, l] for i in range(1, 5))

    def outflow(v, l):
        b, w = v[1, l], v[2, l]
        return (v[0, l + 1] - v[0, l]) + (up(b, 0) - b) + (up(w, 1) - w)

    def mid_cell(l):
        return sums[0, 0, l + 1] + sums[1, 2, l] + sums[2, 4, l]

    def first_pressures(l, carry):
        q = mid[3, l] + 0.5 * outflow(um, l)
        um[3, l] = jnp.where(mid_inside(l), (-0.5 / 6.0) * mid_cell(l) * q, 0.0)
        return carry

    loop(1, 12, first_pressures, 0)

    def expand(a):
        a = a + up(a, 0)
        a = jnp.where(row_even, a, down(a, 0))
        a = a + up(a, 1)
        return 0.125 * jnp.where(lane_even, a, down(a, 1))

    def layer_residual(c, l):
        u = um[c, l]
        us = neighbours(um[c, l - 1], u, um[c, l + 1])
        p = um[3, l]
        before = um[3, l - 1] if c == 0 else down(p, c - 1)
        return mid[c, l] - 0.5 * (p - before) - 0.125 * (dm[c, l] * u - weigh(weights(c, l), us))

    def residuals(k, carry):
        l = 2 + 2 * k
        for c in range(3):
            f2[c, k] = expand(layer_residual(c, l) + layer_residual(c, l + 1))
        f2[3, k] = expand((mid[3, l] + 0.5 * outflow(um, l)) + (mid[3, l + 1] + 0.5 * outflow(um, l + 1)))
        return carry

    loop(0, 5, residuals, 0)

    def low_viscosity(k, carry):
        for c in range(3):
            e2[c, k] = expand(mid[4 + c, 2 * k] + mid[4 + c, 2 * k + 1])
        return carry

    loop(0, 7, low_viscosity, 0)

    def low_inside(k):
        return inside(yz, place[0] * (BX // 4) + k - 1, sizes[0] // 4)

    def low_velocities(k, carry):
        good = low_inside(k)
        for c in range(3):
            e = e2[c, k + 1]
            diag = 6.0 * e + total(neighbours(e2[c, k], e, e2[c, k + 2], 2))
            low[c, k] = jnp.where(good, 19.2 * f2[c, k] / diag, 0.0)
        return carry

    loop(0, 5, low_velocities, 0)

    def low_pressures(k, carry):
        v, w, ev, ew = low[1, k], low[2, k], e2[1, k + 1], e2[2, k + 1]
        flow = (low[0, k + 1] - low[0, k]) + (up(v, 0, 2) - v) + (up(w, 1, 2) - w)
        cell = (e2[0, k + 1] + e2[0, k + 2]) + (ev + up(ev, 0, 2)) + (ew + up(ew, 1, 2))
        low[3, k] = jnp.where(low_inside(k), (-0.5 / 6.0) * cell * (f2[3, k] + 0.25 * flow), 0.0)
        return carry

    loop(0, 4, low_pressures, 0)

    def corrected(k, carry):
        for i in range(3):
            um[i, 2 * k + 2] = um[i, 2 * k + 2] + low[i, k]
            um[i, 2 * k + 3] = um[i, 2 * k + 3] + low[i, k]
        return carry

    loop(0, 5, corrected, 0)
    for k in range(4):
        um[3, 2 * k + 2] = um[3, 2 * k + 2] + low[3, k]
        um[3, 2 * k + 3] = um[3, 2 * k + 3] + low[3, k]

    def second_velocities(l, carry):
        good = mid_inside(l)
        p = um[3, l]
        for c in range(3):
            u = um[c, l]
            us = neighbours(um[c, l - 1], u, um[c, l + 1])
            before = um[3, l - 1] if c == 0 else down(p, c - 1)
            push = 4.8 * (mid[c, l] - 0.5 * (p - before)) + 0.6 * weigh(weights(c, l), us)
            sm[c, l] = jnp.where(good, 0.4 * u + push * over[c, l], 0.0)
        return carry

    loop(3, 10, second_velocities, 0)

    def second_pressures(l, carry):
        q = mid[3, l] + 0.5 * outflow(sm, l)
        sm[3, l] = jnp.where(mid_inside(l), um[3, l] - (0.5 / 6.0) * mid_cell(l) * q, 0.0)
        return carry

    loop(3, 9, second_pressures, 0)

    last_row = iota((8, BZ), 0) == 7
    for i in range(4):
        for m in range(6):
            a = sm[i, 3 + m]
            a = jnp.where(last_row, a[8:16], a[0:8])
            twice[6 * i + m, pl.ds(0, 8, stride=2), :] = a
            twice[6 * i + m, pl.ds(1, 8, stride=2), :] = a
    matrix = spread_matrix()
    for i in range(4):
        wide = exact_dot(twice[6 * i : 6 * i + 6].reshape(6 * ROWS, BZ), matrix)
        spread[i] = wide.reshape(6, ROWS, LANES)

    for m in range(1, 6):
        p = spread[3, m]
        for c in range(3):
            rows, lanes = sizes_of(c)
            z = spread[c, m]
            sides = (down(z, 0), up(z, 0), down(z, 1), up(z, 1))
            for x in (2 * m - 2, 2 * m - 1):
                if x > BX:
                    continue
                zs = (spread[c, (x + 1) // 2], spread[c, (x + 3) // 2]) + sides
                push = weigh([last_sums[c, i, x, 0:rows, 0:lanes] for i in range(6)], [v[0:rows, 0:lanes] for v in zs])
                if c > 0:
                    push = push - 1.2 * (p - down(p, c - 1))[0:rows, 0:lanes]
                elif x % 2 == 0:
                    push = push - 1.2 * (p - spread[3, m - 1])[0:rows, 0:lanes]
                u = base[c, x, 0:rows, 0:lanes] + 0.4 * z[0:rows, 0:lanes] + inv[c, x, 0:rows, 0:lanes] * push
                un[c, x, 0:rows, 0:lanes] = u
                if x < BX:
                    out[c, x] = u[0:BY, 0:BZ]

    for x in range(BX):
        v, w = un[1, x, :, 0:BZ], un[2, x, 0:BY, :]
        flow = un[0, x + 1, 0:BY, 0:BZ] - un[0, x, 0:BY, 0:BZ]
        flow = flow + (up(v, 0) - v)[0:BY] + (up(w, 1) - w)[:, 0:BZ]
        out[3, x] = pbase[x] + spread[3, (x + 2) // 2, 0:BY, 0:BZ] - cells[x] * flow


WIDE, TILE, HUGE = (ROWS, BZ), (BY, BZ), (ROWS, LANES)
HALF = (11, NL, BY, LANES)
FINE_OUT = [(11, NL) + HUGE, (4, NL) + HUGE, (7, 6) + TILE, (7, 4) + TILE]
FINE_SCRATCH = [(NL + 4,) + TILE, (7, 6) + HUGE, (42,) + WIDE]
LAST_OUT = [(3, 6, 9) + HUGE, (3, 9) + HUGE, (3, 9) + HUGE, (BX,) + TILE, (BX,) + TILE]
COARSE_SCRATCH = [
    (7, ML) + WIDE, (3, 5, ML) + WIDE, (4, ML) + WIDE, (3, ML) + WIDE, (3, ML) + WIDE, (4, 5) + WIDE, (3, 7) + WIDE,
    (4, 5) + WIDE, (4, ML) + WIDE, (24,) + WIDE, (4, 6) + HUGE, (3, 9) + HUGE,
]


def per_device(sizes, iterate, forcing, viscosity):
    nx, ny, nz = (lax.axis_size(a) for a in ("gx", "gy", "gz"))
    at = [lax.axis_index(a) for a in ("gx", "gy", "gz")]
    place = jnp.stack(at + [at[2] % 2]).astype(jnp.int32)

    def swap(a, axis, count, start):
        pairs = []
        for i in range(start, count - 1, 2):
            pairs += [(i, i + 1), (i + 1, i)]
        return lax.ppermute(a, axis, pairs)

    def around(a, axis, count, by):
        return lax.ppermute(a, axis, [(i, (i + by) % count) for i in range(count)])

    def to_next(a, axis, count):
        return lax.ppermute(a, axis, [(i, i + 1) for i in range(count - 1)])

    def to_previous(a, axis, count):
        return lax.ppermute(a, axis, [(i + 1, i) for i in range(count - 1)])

    iterate, forcing, viscosity = (
        pltpu.with_memory_space_constraint(a, pltpu.HBM) for a in (iterate, forcing, viscosity)
    )
    tile = (BY, BZ)
    own, first, second = call(
        pack_z, [(11, BX) + tile, (11,) + tile, (11,) + tile], [pltpu.SemaphoreType.DMA((3,))],
        place, iterate, forcing, viscosity, space=HBM,
    )
    first = swap(first, "gz", nz, 1)
    second = swap(second, "gz", nz, 0)

    upward, downward = call(pack_x, [(11, XL + 1) + tile, (11, XH + 1) + tile], [], place, own, first, second)
    x_low = to_next(upward, "gx", nx)
    x_high = to_previous(downward, "gx", nx)

    upward, downward = call(
        pack_y, [(11, NL + 4, XL, BZ), (11, NL + 4, XH, BZ)], [], place, own, first, second, x_low, x_high
    )
    y_low = around(upward, "gy", ny, 1)
    y_high = around(downward, "gy", ny, -1)
    (half,) = call(assemble_own, [HALF], [], place, own, first, second, x_low, x_high)

    whole, fine, downward, upward = call(
        functools.partial(fine_level, sizes), FINE_OUT, FINE_SCRATCH, place, half, y_low, y_high
    )
    x_low = to_next(upward, "gx", nx)
    x_high = to_previous(downward, "gx", nx)

    downward, upward = call(pack_y_mid, [(7, 6 * ML + 4, BZ), (7, ML, 4, BZ)], [], downward, x_low, x_high)
    y_low = around(upward, "gy", ny, 1)
    y_high = around(downward, "gy", ny, -1)

    terms = call(functools.partial(last_terms, sizes), LAST_OUT, [], place, whole, fine)
    (updated,) = call(
        functools.partial(coarse_levels, sizes), [(4, BX) + tile], COARSE_SCRATCH,
        place, *terms, upward, y_low, y_high,
    )
    return updated


def solution(mesh):
    spec = P(None, "gx", "gy", "gz")
    sizes = (mesh.shape["gx"] * BX, mesh.shape["gy"] * BY, mesh.shape["gz"] * BZ)
    return jax.shard_map(
        functools.partial(per_device, sizes), mesh=mesh, in_specs=(spec,) * 3, out_specs=spec, check_vma=False
    )
```

```python
import functools

import jax
import jax.numpy as jnp
from jax import lax
from jax.experimental import pallas as pl
from jax.experimental.pallas import tpu as pltpu
from jax.sharding import PartitionSpec as P

F32 = jnp.float32
BX, BY, BZ = 8, 8, 128
XL, XH = 2, 4
NL = BX + XL + XH
ROWS, LANES = 16, 256
ML = 14
VMEM = pl.BlockSpec(memory_space=pltpu.VMEM)
SMEM = pl.BlockSpec(memory_space=pltpu.SMEM)
HBM = pl.BlockSpec(memory_space=pltpu.HBM)
UNROLL = True
PARAMS = pltpu.CompilerParams(vmem_limit_bytes=20 * 1024 * 1024)


def call(kernel, outs, scratch, *args, space=VMEM):
    specs = [SMEM if a.dtype == jnp.int32 else space for a in args]
    return pl.pallas_call(
        kernel,
        out_shape=[jax.ShapeDtypeStruct(s, F32) for s in outs],
        in_specs=specs,
        out_specs=[VMEM] * len(outs),
        scratch_shapes=[pltpu.VMEM(s, F32) if isinstance(s, tuple) else s for s in scratch],
        compiler_params=PARAMS,
    )(*args)


def loop(start, stop, body, carry):
    return lax.fori_loop(start, stop, body, carry, unroll=UNROLL)


def iota(shape, dim):
    return lax.broadcasted_iota(jnp.int32, shape, dim)


def up(a, dim, by=1):
    return pltpu.roll(a, a.shape[dim] - by, dim)


def down(a, dim, by=1):
    return pltpu.roll(a, by, dim)


def lane_roll(a, by):
    by = by % a.shape[1]
    return pltpu.roll(a, by, 1) if by else a


def fine_above(f, dim):
    own = f % 4 == dim and f != 3
    return (3, 2, 3)[f // 4] + own if f % 4 < 3 else (3, 2)[f // 4]


def fine_below(f):
    return 1 if 4 <= f < 8 else 2


def mid_above(f, dim):
    return (4, 5)[f // 4] + (f % 4 == dim and f != 3)


def mid_below(f):
    return (3, 4)[f // 4]


def offsets(entries):
    table, at = {}, 0
    for key, rows in entries:
        table[key] = at
        at += rows
    return table, -(-at // 8) * 8


FINE, MID = range(11), range(7)
X_UP, X_UP_TILES = offsets(
    [((f, x), 1) for f in FINE for x in range(BX - fine_below(f), BX)] + [((f, "z"), 1) for f in FINE]
)
X_DOWN, X_DOWN_TILES = offsets(
    [((f, x), 1) for f in FINE for x in range(fine_above(f, 0))] + [((f, "z"), 1) for f in FINE]
)
FINE_LAYERS = {
    f: [x + XL for x in range(-fine_below(f), BX + fine_above(f, 0))] + list(range(NL, NL + 4)) for f in FINE
}
Y_UP, Y_UP_ROWS = offsets([((f, l), fine_below(f)) for f in FINE for l in FINE_LAYERS[f]])
Y_DOWN, Y_DOWN_ROWS = offsets([((f, l), fine_above(f, 1)) for f in FINE for l in FINE_LAYERS[f]])
MX_UP, MX_UP_ROWS = offsets([((f, m), mid_above(f, 1)) for f in MID for m in range(4 - mid_below(f), 4)])
MX_DOWN, MX_DOWN_ROWS = offsets([((f, m), mid_above(f, 1)) for f in MID for m in range(mid_above(f, 0))])
MID_LAYERS = {f: [m + 4 for m in range(-mid_below(f), 4 + mid_above(f, 0))] for f in MID}
MY_UP, MY_UP_ROWS = offsets([((f, l), mid_below(f)) for f in MID for l in MID_LAYERS[f]])
MY_DOWN, MY_DOWN_ROWS = offsets([((f, l), mid_above(f, 1)) for f in MID for l in MID_LAYERS[f]])


def pack_z(place, iterate, forcing, viscosity, own, first, second, sems):
    parts = ((iterate, 0, 4), (forcing, 4, 4), (viscosity, 8, 3))
    copies = [
        pltpu.make_async_copy(source, own.at[at : at + count], sems.at[i])
        for i, (source, at, count) in enumerate(parts)
    ]
    for copy in copies:
        copy.start()
    lane = iota((BY, BZ), 1) // 16
    odd = jnp.full((BY, BZ), place[3], jnp.int32) == 1
    for copy, (_, at, count) in zip(copies, parts):
        copy.wait()
        for f in range(at, at + count):
            low = jnp.zeros((BY, BZ), F32)
            high = jnp.zeros((BY, BZ), F32)
            for x in range(BX):
                a = own[f, x]
                mine = lane == x
                low = jnp.where(mine, lane_roll(a, 16 * x - 112), low)
                high = jnp.where(mine, lane_roll(a, 16 * x), high)
            first[f] = jnp.where(odd, low, high)
            second[f] = jnp.where(odd, high, low)


def strips(place, first, second, f):
    odd = jnp.full((BY, BZ), place[3], jnp.int32) == 1
    a, b = first[f], second[f]
    return jnp.where(odd, b, a), jnp.where(odd, a, b)


def pack_x(place, own, first, second, to_up, to_down):
    lane = iota((BY, BZ), 1)
    for f in FINE:
        low, high = strips(place, first, second, f)
        to_up[X_UP[f, "z"]] = jnp.where(lane >= 96, low, lane_roll(high, -32))
        to_down[X_DOWN[f, "z"]] = jnp.where(lane < 64, low, lane_roll(high, 64))
        for x in range(BX - fine_below(f), BX):
            to_up[X_UP[f, x]] = own[f, x]
        for x in range(fine_above(f, 0)):
            to_down[X_DOWN[f, x]] = own[f, x]


def fine_tile(own, from_low, from_high, f, l):
    x = l - XL
    if 0 <= x < BX:
        return own[f, x]
    if x < 0:
        return from_low[X_UP[f, BX + x]] if -x <= fine_below(f) else None
    return from_high[X_DOWN[f, x - BX]] if x - BX < fine_above(f, 0) else None


def strip_tiles(place, first, second, from_low, from_high, f):
    low, high = strips(place, first, second, f)
    return [low, high, from_low[X_UP[f, "z"]], from_high[X_DOWN[f, "z"]]]


def pack_y(place, own, first, second, from_low, from_high, to_up, to_down):
    for f in FINE:
        sides = strip_tiles(place, first, second, from_low, from_high, f)
        below, above = fine_below(f), fine_above(f, 1)
        for l in FINE_LAYERS[f]:
            tile = sides[l - NL] if l >= NL else fine_tile(own, from_low, from_high, f, l)
            at = Y_UP[f, l]
            to_up[at : at + below] = tile[BY - below :, :]
            at = Y_DOWN[f, l]
            to_down[at : at + above] = tile[:above, :]


def inside_yz(place, rows, lanes, ny, nz, end_y, low_y, end_z, low_z, by, bz):
    y = iota((rows, lanes), 0)
    z = iota((rows, lanes), 1)
    held = ((y < end_y) | (y >= rows - low_y)) & ((z < end_z) | (z >= lanes - low_z))
    y = jnp.where(y < end_y, y, y - rows) + place[1] * by
    z = jnp.where(z < end_z, z, z - lanes) + place[2] * bz
    good = held & (y >= 0) & (y < ny) & (z >= 0) & (z < nz)
    return jnp.where(good, 1, 0)


def inside(yz, x, nx):
    ok = jnp.where((x >= 0) & (x < nx), 1, 0)
    return (yz * ok) != 0


def neighbours(low, mid, high, by=1):
    return (low, high, down(mid, 0, by), up(mid, 0, by), down(mid, 1, by), up(mid, 1, by))


def total(values):
    out = values[0]
    for v in values[1:]:
        out = out + v
    return out


def couple(e, es, vs):
    return e * total(vs) + total([a * b for a, b in zip(es, vs)])


def fine_mask_args(place, sizes):
    return inside_yz(place, ROWS, LANES, sizes[1], sizes[2], BY + XH, XL, BZ + 16, 16, BY, BZ)


def compact_matrix():
    a = iota((LANES, BZ), 0) // 2
    return jnp.where(a == iota((LANES, BZ), 1), 0.125, 0.0).astype(jnp.bfloat16)


def spread_matrix():
    a = iota((BZ, LANES), 1) // 2
    return jnp.where(a == iota((BZ, LANES), 0), 1.0, 0.0).astype(jnp.bfloat16)


def exact_dot(a, matrix):
    high = a.astype(jnp.bfloat16)
    rest = a - high.astype(F32)
    mid = rest.astype(jnp.bfloat16)
    low = (rest - mid.astype(F32)).astype(jnp.bfloat16)
    dot = functools.partial(jnp.dot, preferred_element_type=F32)
    return dot(high, matrix) + (dot(mid, matrix) + dot(low, matrix))


def kept(place, sizes):
    low = jnp.where(place[1] > 0, 1.0, 0.0).astype(F32)
    high = jnp.where(place[1] < sizes[1] // BY - 1, 1.0, 0.0).astype(F32)
    return low, high


def side_lanes(l, tiles):
    lane = iota((BY, BZ), 1)
    x = l - XL
    if x < 0:
        a, b = lane_roll(tiles[2], 16 - 16 * l), lane_roll(tiles[2], -(64 + 16 * l))
    elif x < BX:
        a, b = lane_roll(tiles[0], 112 - 16 * x), lane_roll(tiles[1], -16 * x)
    else:
        a, b = lane_roll(tiles[3], 112 - 16 * (x - BX)), lane_roll(tiles[3], -(64 + 16 * (x - BX)))
    return jnp.where(lane >= 112, a, jnp.where(lane < 16, b, 0.0))


def assemble_own(place, own, first, second, from_low, from_high, half):
    for f in FINE:
        sides = strip_tiles(place, first, second, from_low, from_high, f)
        for l in range(NL):
            body = fine_tile(own, from_low, from_high, f, l)
            half[f, l, :, 0:BZ] = jnp.zeros((BY, BZ), F32) if body is None else body
            half[f, l, :, BZ:] = side_lanes(l, sides)


def pair_sums(e, high):
    return e + high, e + down(e, 0), e + up(e, 0), e + down(e, 1), e + up(e, 1)


def weigh(weights, values):
    return total([a * b for a, b in zip(weights, values)])


def fine_level(sizes, place, half, y_low, y_high, whole, full, middle, to_down, to_up, rows, rsum, tsum):
    keep_low, keep_high = kept(place, sizes)

    for f in FINE:
        below, above = fine_below(f), fine_above(f, 1)
        for l in FINE_LAYERS[f]:
            rows[f, l] = jnp.zeros((BY, BZ), F32)
            at = Y_DOWN[f, l]
            rows[f, l, 0:above] = y_high[at : at + above] * keep_high
            at = Y_UP[f, l]
            rows[f, l, BY - below :] = y_low[at : at + below] * keep_low
        sides = [rows[f, NL + i] for i in range(4)]
        for l in range(NL):
            whole[f, l, 0:BY] = half[f, l]
            whole[f, l, BY:, 0:BZ] = rows[f, l] if l in FINE_LAYERS[f] else jnp.zeros((BY, BZ), F32)
            whole[f, l, BY:, BZ:] = side_lanes(l, sides)

    def grid(f, l):
        return whole[f, l]

    yz = fine_mask_args(place, sizes)
    for i in range(4):
        full[i, 0] = jnp.zeros((ROWS, LANES), F32)
        full[i, NL - 1] = jnp.zeros((ROWS, LANES), F32)
    full[3, NL - 2] = jnp.zeros((ROWS, LANES), F32)

    def weights(c, l):
        e = grid(8 + c, l)
        return (e + grid(8 + c, l - 1),) + pair_sums(e, grid(8 + c, l + 1))

    def velocities(l, carry):
        good = inside(yz, place[0] * BX + l - XL, sizes[0])
        p = grid(3, l)
        for c in range(3):
            u = grid(c, l)
            us = neighbours(grid(c, l - 1), u, grid(c, l + 1))
            ks = weights(c, l)
            before = grid(3, l - 1) if c == 0 else down(p, c - 1)
            push = 1.2 * (grid(4 + c, l) - (p - before)) + 0.6 * weigh(ks, us)
            full[c, l] = jnp.where(good, 0.4 * u + push / total(ks), 0.0)
        return carry

    loop(1, NL - 1, velocities, 0)

    def outflow(l):
        v, w = full[1, l], full[2, l]
        return (full[0, l + 1] - full[0, l]) + (up(v, 0) - v) + (up(w, 1) - w)

    def pressures(l, carry):
        good = inside(yz, place[0] * BX + l - XL, sizes[0])
        ev, ew = grid(9, l), grid(10, l)
        cell = (grid(8, l) + grid(8, l + 1)) + (ev + up(ev, 0)) + (ew + up(ew, 1))
        full[3, l] = jnp.where(good, grid(3, l) - (0.5 / 6.0) * cell * (grid(7, l) + outflow(l)), 0.0)
        return carry

    loop(1, NL - 2, pressures, 0)

    def layer_residual(c, l):
        u = full[c, l]
        us = neighbours(full[c, l - 1], u, full[c, l + 1])
        ks = weights(c, l)
        p = full[3, l]
        before = full[3, l - 1] if c == 0 else down(p, c - 1)
        return grid(4 + c, l) - (p - before) - 0.5 * (total(ks) * u - weigh(ks, us))

    def residuals(m, carry):
        l = XL + 2 * m
        for c in range(3):
            rsum[c, m] = layer_residual(c, l) + layer_residual(c, l + 1)
        rsum[3, m] = (grid(7, l) + outflow(l)) + (grid(7, l + 1) + outflow(l + 1))
        return carry

    loop(0, 5, residuals, 0)
    for i in range(4):
        rsum[i, 5] = jnp.zeros((ROWS, LANES), F32)
    for c in range(3):
        for m in range(6):
            rsum[4 + c, m] = grid(8 + c, XL + 2 * m) + grid(8 + c, XL + 2 * m + 1)

    matrix = compact_matrix()
    for f in range(7):
        tsum[6 * f : 6 * f + 6] = exact_dot(rsum[f].reshape(6 * ROWS, LANES), matrix).reshape(6, ROWS, BZ)
    for f in MID:
        rows_sent = mid_above(f, 1)
        for m in range(mid_above(f, 0)):
            i = 6 * f + m
            a = tsum[i, pl.ds(0, 8, stride=2), :] + tsum[i, pl.ds(1, 8, stride=2), :]
            at = MX_DOWN[f, m]
            to_down[at : at + rows_sent] = a[:rows_sent]
            if m < 4:
                middle[f, m] = a
            if (f, m) in MX_UP:
                at = MX_UP[f, m]
                to_up[at : at + rows_sent] = a[:rows_sent]


def sizes_of(c):
    return (ROWS if c == 1 else BY), (LANES if c == 2 else BZ)


def last_terms(sizes, place, whole, fine, sums, base, inv, cells, pbase):
    fyz = fine_mask_args(place, sizes)

    def grid(f, l):
        return whole[f, l]

    for x in range(9):
        l = x + XL
        good = inside(fyz, place[0] * BX + x, sizes[0])
        p = fine[3, l]
        for c in range(3):
            u, e = fine[c, l], grid(8 + c, l)
            us = neighbours(fine[c, l - 1], u, fine[c, l + 1])
            xp, ym, yp, zm, zp = pair_sums(e, grid(8 + c, l + 1))
            ks = (e + grid(8 + c, l - 1), xp, ym, yp, zm, zp)
            before = fine[3, l - 1] if c == 0 else down(p, c - 1)
            push = 1.2 * (grid(4 + c, l) - (p - before)) + 0.6 * weigh(ks, us)
            over = 1.0 / total(ks)
            rows, lanes = sizes_of(c)
            for i, k in enumerate(ks):
                sums[c, i, x, 0:rows, 0:lanes] = (0.6 * k)[0:rows, 0:lanes]
            base[c, x, 0:rows, 0:lanes] = jnp.where(good, 0.4 * u + push * over, 0.0)[0:rows, 0:lanes]
            inv[c, x, 0:rows, 0:lanes] = jnp.where(good, over, 0.0)[0:rows, 0:lanes]
            if x < BX and c == 0:
                cell = e + grid(8, l + 1)
            elif x < BX:
                cell = cell + (yp if c == 1 else zp)
        if x < BX:
            cell = (0.5 / 6.0) * cell
            cells[x] = cell[0:BY, 0:BZ]
            pbase[x] = (p - cell * grid(7, l))[0:BY, 0:BZ]


def pack_y_mid(own, from_low, from_high, to_down, to_up, rows):
    for f in MID:
        below, above = mid_below(f), mid_above(f, 1)
        for l in range(ML):
            if l not in MID_LAYERS[f]:
                rows[f, l] = jnp.zeros((4, BZ), F32)
                continue
            m = l - 4
            if m < 0:
                at = MX_UP[f, 4 + m]
                tile = from_low[at : at + above]
            elif m < 4:
                tile = own[f, m, 0:above]
            else:
                at = MX_DOWN[f, m - 4]
                tile = from_high[at : at + above]
            at = MY_DOWN[f, l]
            to_down[at : at + above] = tile
            at = MY_UP[f, l]
            to_up[at : at + below] = tile[4 - below : 4]
            rows[f, l] = tile[0:4]


def coarse_levels(
    sizes, place, last_sums, base, inv, cells, pbase, own, y_low, y_high, out,
    mid, sums, um, over, dm, f2, e2, low, sm, twice, spread, un,
):
    keep_low, keep_high = kept(place, sizes)
    for f in MID:
        below, above = mid_below(f), mid_above(f, 1)
        for l in range(ML):
            mid[f, l] = jnp.zeros((ROWS, BZ), F32)
            mid[f, l, 0:4] = own[f, l]
            if l in MID_LAYERS[f]:
                at = MY_DOWN[f, l]
                mid[f, l, 4 : 4 + above] = y_high[at : at + above] * keep_high
                at = MY_UP[f, l]
                mid[f, l, ROWS - below :] = y_low[at : at + below] * keep_low

    shape = (ROWS, BZ)
    yz = inside_yz(place, ROWS, BZ, sizes[1] // 2, sizes[2] // 2, 10, 4, BZ // 2 + 8, 8, BY // 2, BZ // 2)
    row_even = iota(shape, 0) % 2 == 0
    lane_even = iota(shape, 1) % 2 == 0

    def mid_inside(l):
        return inside(yz, place[0] * (BX // 2) + l - 4, sizes[0] // 2)

    for c in range(3):
        sums[c, 0, 1] = mid[4 + c, 0] + mid[4 + c, 1]

    def first_velocities(l, carry):
        good = mid_inside(l)
        for c in range(3):
            xp, ym, yp, zm, zp = pair_sums(mid[4 + c, l], mid[4 + c, l + 1])
            diag = total([sums[c, 0, l], xp, ym, yp, zm, zp])
            sums[c, 0, l + 1] = xp
            sums[c, 1, l] = ym
            sums[c, 2, l] = yp
            sums[c, 3, l] = zm
            sums[c, 4, l] = zp
            dm[c, l] = diag
            inverse = 1.0 / diag
            over[c, l] = inverse
            um[c, l] = jnp.where(good, 4.8 * mid[c, l] * inverse, 0.0)
        return carry

    loop(1, 13, first_velocities, 0)

    def weights(c, l):
        return (sums[c, 0, l], sums[c, 0, l + 1]) + tuple(sums[c, i, l] for i in range(1, 5))

    def outflow(v, l):
        b, w = v[1, l], v[2, l]
        return (v[0, l + 1] - v[0, l]) + (up(b, 0) - b) + (up(w, 1) - w)

    def mid_cell(l):
        return sums[0, 0, l + 1] + sums[1, 2, l] + sums[2, 4, l]

    def first_pressures(l, carry):
        q = mid[3, l] + 0.5 * outflow(um, l)
        um[3, l] = jnp.where(mid_inside(l), (-0.5 / 6.0) * mid_cell(l) * q, 0.0)
        return carry

    loop(1, 12, first_pressures, 0)

    def expand(a):
        a = a + up(a, 0)
        a = jnp.where(row_even, a, down(a, 0))
        a = a + up(a, 1)
        return 0.125 * jnp.where(lane_even, a, down(a, 1))

    def layer_residual(c, l):
        u = um[c, l]
        us = neighbours(um[c, l - 1], u, um[c, l + 1])
        p = um[3, l]
        before = um[3, l - 1] if c == 0 else down(p, c - 1)
        return mid[c, l] - 0.5 * (p - before) - 0.125 * (dm[c, l] * u - weigh(weights(c, l), us))

    def residuals(k, carry):
        l = 2 + 2 * k
        for c in range(3):
            f2[c, k] = expand(layer_residual(c, l) + layer_residual(c, l + 1))
        f2[3, k] = expand((mid[3, l] + 0.5 * outflow(um, l)) + (mid[3, l + 1] + 0.5 * outflow(um, l + 1)))
        return carry

    loop(0, 5, residuals, 0)

    def low_viscosity(k, carry):
        for c in range(3):
            e2[c, k] = expand(mid[4 + c, 2 * k] + mid[4 + c, 2 * k + 1])
        return carry

    loop(0, 7, low_viscosity, 0)

    def low_inside(k):
        return inside(yz, place[0] * (BX // 4) + k - 1, sizes[0] // 4)

    def low_velocities(k, carry):
        good = low_inside(k)
        for c in range(3):
            e = e2[c, k + 1]
            diag = 6.0 * e + total(neighbours(e2[c, k], e, e2[c, k + 2], 2))
            low[c, k] = jnp.where(good, 19.2 * f2[c, k] / diag, 0.0)
        return carry

    loop(0, 5, low_velocities, 0)

    def low_pressures(k, carry):
        v, w, ev, ew = low[1, k], low[2, k], e2[1, k + 1], e2[2, k + 1]
        flow = (low[0, k + 1] - low[0, k]) + (up(v, 0, 2) - v) + (up(w, 1, 2) - w)
        cell = (e2[0, k + 1] + e2[0, k + 2]) + (ev + up(ev, 0, 2)) + (ew + up(ew, 1, 2))
        low[3, k] = jnp.where(low_inside(k), (-0.5 / 6.0) * cell * (f2[3, k] + 0.25 * flow), 0.0)
        return carry

    loop(0, 4, low_pressures, 0)

    def corrected(k, carry):
        for i in range(3):
            um[i, 2 * k + 2] = um[i, 2 * k + 2] + low[i, k]
            um[i, 2 * k + 3] = um[i, 2 * k + 3] + low[i, k]
        return carry

    loop(0, 5, corrected, 0)
    for k in range(4):
        um[3, 2 * k + 2] = um[3, 2 * k + 2] + low[3, k]
        um[3, 2 * k + 3] = um[3, 2 * k + 3] + low[3, k]

    def second_velocities(l, carry):
        good = mid_inside(l)
        p = um[3, l]
        for c in range(3):
            u = um[c, l]
            us = neighbours(um[c, l - 1], u, um[c, l + 1])
            before = um[3, l - 1] if c == 0 else down(p, c - 1)
            push = 4.8 * (mid[c, l] - 0.5 * (p - before)) + 0.6 * weigh(weights(c, l), us)
            sm[c, l] = jnp.where(good, 0.4 * u + push * over[c, l], 0.0)
        return carry

    loop(3, 10, second_velocities, 0)

    def second_pressures(l, carry):
        q = mid[3, l] + 0.5 * outflow(sm, l)
        sm[3, l] = jnp.where(mid_inside(l), um[3, l] - (0.5 / 6.0) * mid_cell(l) * q, 0.0)
        return carry

    loop(3, 9, second_pressures, 0)

    last_row = iota((8, BZ), 0) == 7
    for i in range(4):
        for m in range(6):
            a = sm[i, 3 + m]
            a = jnp.where(last_row, a[8:16], a[0:8])
            twice[6 * i + m, pl.ds(0, 8, stride=2), :] = a
            twice[6 * i + m, pl.ds(1, 8, stride=2), :] = a
    matrix = spread_matrix()
    for i in range(4):
        wide = exact_dot(twice[6 * i : 6 * i + 6].reshape(6 * ROWS, BZ), matrix)
        spread[i] = wide.reshape(6, ROWS, LANES)

    for m in range(1, 6):
        p = spread[3, m]
        for c in range(3):
            rows, lanes = sizes_of(c)
            z = spread[c, m]
            sides = (down(z, 0), up(z, 0), down(z, 1), up(z, 1))
            for x in (2 * m - 2, 2 * m - 1):
                if x > BX:
                    continue
                zs = (spread[c, (x + 1) // 2], spread[c, (x + 3) // 2]) + sides
                push = weigh([last_sums[c, i, x, 0:rows, 0:lanes] for i in range(6)], [v[0:rows, 0:lanes] for v in zs])
                if c > 0:
                    push = push - 1.2 * (p - down(p, c - 1))[0:rows, 0:lanes]
                elif x % 2 == 0:
                    push = push - 1.2 * (p - spread[3, m - 1])[0:rows, 0:lanes]
                u = base[c, x, 0:rows, 0:lanes] + 0.4 * z[0:rows, 0:lanes] + inv[c, x, 0:rows, 0:lanes] * push
                un[c, x, 0:rows, 0:lanes] = u
                if x < BX:
                    out[c, x] = u[0:BY, 0:BZ]

    for x in range(BX):
        v, w = un[1, x, :, 0:BZ], un[2, x, 0:BY, :]
        flow = un[0, x + 1, 0:BY, 0:BZ] - un[0, x, 0:BY, 0:BZ]
        flow = flow + (up(v, 0) - v)[0:BY] + (up(w, 1) - w)[:, 0:BZ]
        out[3, x] = pbase[x] + spread[3, (x + 2) // 2, 0:BY, 0:BZ] - cells[x] * flow


WIDE, TILE, HUGE = (ROWS, BZ), (BY, BZ), (ROWS, LANES)
HALF = (11, NL, BY, LANES)
FINE_OUT = [(11, NL) + HUGE, (4, NL) + HUGE, (7, 4) + TILE, (MX_DOWN_ROWS, BZ), (MX_UP_ROWS, BZ)]
FINE_SCRATCH = [(11, NL + 4) + TILE, (7, 6) + HUGE, (42,) + WIDE]
LAST_OUT = [(3, 6, 9) + HUGE, (3, 9) + HUGE, (3, 9) + HUGE, (BX,) + TILE, (BX,) + TILE]
COARSE_SCRATCH = [
    (7, ML) + WIDE, (3, 5, ML) + WIDE, (4, ML) + WIDE, (3, ML) + WIDE, (3, ML) + WIDE, (4, 5) + WIDE, (3, 7) + WIDE,
    (4, 5) + WIDE, (4, ML) + WIDE, (24,) + WIDE, (4, 6) + HUGE, (3, 9) + HUGE,
]


def per_device(sizes, iterate, forcing, viscosity):
    nx, ny, nz = (lax.axis_size(a) for a in ("gx", "gy", "gz"))
    at = [lax.axis_index(a) for a in ("gx", "gy", "gz")]
    place = jnp.stack(at + [at[2] % 2]).astype(jnp.int32)

    def swap(a, axis, count, start):
        pairs = []
        for i in range(start, count - 1, 2):
            pairs += [(i, i + 1), (i + 1, i)]
        return lax.ppermute(a, axis, pairs)

    def around(a, axis, count, by):
        return lax.ppermute(a, axis, [(i, (i + by) % count) for i in range(count)])

    def to_next(a, axis, count):
        return lax.ppermute(a, axis, [(i, i + 1) for i in range(count - 1)])

    def to_previous(a, axis, count):
        return lax.ppermute(a, axis, [(i + 1, i) for i in range(count - 1)])

    iterate, forcing, viscosity = (
        pltpu.with_memory_space_constraint(a, pltpu.HBM) for a in (iterate, forcing, viscosity)
    )
    tile = (BY, BZ)
    own, first, second = call(
        pack_z, [(11, BX) + tile, (11,) + tile, (11,) + tile], [pltpu.SemaphoreType.DMA((3,))],
        place, iterate, forcing, viscosity, space=HBM,
    )
    first = swap(first, "gz", nz, 1)
    second = swap(second, "gz", nz, 0)

    upward, downward = call(pack_x, [(X_UP_TILES,) + tile, (X_DOWN_TILES,) + tile], [], place, own, first, second)
    x_low = to_next(upward, "gx", nx)
    x_high = to_previous(downward, "gx", nx)

    upward, downward = call(
        pack_y, [(Y_UP_ROWS, BZ), (Y_DOWN_ROWS, BZ)], [], place, own, first, second, x_low, x_high
    )
    y_low = around(upward, "gy", ny, 1)
    y_high = around(downward, "gy", ny, -1)
    (half,) = call(assemble_own, [HALF], [], place, own, first, second, x_low, x_high)

    whole, fine, middle, downward, upward = call(
        functools.partial(fine_level, sizes), FINE_OUT, FINE_SCRATCH, place, half, y_low, y_high
    )
    x_low = to_next(upward, "gx", nx)
    x_high = to_previous(downward, "gx", nx)

    downward, upward, middle = call(
        pack_y_mid, [(MY_DOWN_ROWS, BZ), (MY_UP_ROWS, BZ), (7, ML, 4, BZ)], [], middle, x_low, x_high
    )
    y_low = around(upward, "gy", ny, 1)
    y_high = around(downward, "gy", ny, -1)

    terms = call(functools.partial(last_terms, sizes), LAST_OUT, [], place, whole, fine)
    (updated,) = call(
        functools.partial(coarse_levels, sizes), [(4, BX) + tile], COARSE_SCRATCH,
        place, *terms, middle, y_low, y_high,
    )
    return updated


def solution(mesh):
    spec = P(None, "gx", "gy", "gz")
    sizes = (mesh.shape["gx"] * BX, mesh.shape["gy"] * BY, mesh.shape["gz"] * BZ)
    return jax.shard_map(
        functools.partial(per_device, sizes), mesh=mesh, in_specs=(spec,) * 3, out_specs=spec, check_vma=False
    )
```

```python
import functools

import jax
import jax.numpy as jnp
from jax import lax
from jax.experimental import pallas as pl
from jax.experimental.pallas import tpu as pltpu
from jax.sharding import PartitionSpec as P

F32 = jnp.float32
BX, BY, BZ = 8, 8, 128
XL, XH = 2, 4
NL = BX + XL + XH
ROWS, LANES = 16, 256
ML = 14
VMEM = pl.BlockSpec(memory_space=pltpu.VMEM)
HBM = pl.BlockSpec(memory_space=pltpu.HBM)
UNROLL = True
PARAMS = pltpu.CompilerParams(vmem_limit_bytes=20 * 1024 * 1024)


def call(kernel, outs, scratch, *args, space=VMEM):
    specs = [VMEM if a.dtype == jnp.int32 else space for a in args]
    return pl.pallas_call(
        kernel,
        out_shape=[jax.ShapeDtypeStruct(s, F32) for s in outs],
        in_specs=specs,
        out_specs=[VMEM] * len(outs),
        scratch_shapes=[pltpu.VMEM(s, F32) if isinstance(s, tuple) else s for s in scratch],
        compiler_params=PARAMS,
    )(*args)


def loop(start, stop, body, carry):
    return lax.fori_loop(start, stop, body, carry, unroll=UNROLL)


def iota(shape, dim):
    return lax.broadcasted_iota(jnp.int32, shape, dim)


def up(a, dim, by=1):
    return pltpu.roll(a, a.shape[dim] - by, dim)


def down(a, dim, by=1):
    return pltpu.roll(a, by, dim)


def lane_roll(a, by):
    by = by % a.shape[1]
    return pltpu.roll(a, by, 1) if by else a


def fine_above(f, dim):
    own = f % 4 == dim and f != 3
    return (3, 2, 3)[f // 4] + own if f % 4 < 3 else (3, 2)[f // 4]


def fine_below(f):
    return 1 if 4 <= f < 8 else 2


def mid_above(f, dim):
    return (4, 5)[f // 4] + (f % 4 == dim and f != 3)


def mid_below(f):
    return (3, 4)[f // 4]


def offsets(entries):
    table, at = {}, 0
    for key, rows in entries:
        table[key] = at
        at += rows
    return table, -(-at // 8) * 8


FINE, MID = range(11), range(7)
X_UP, X_UP_TILES = offsets(
    [((f, x), 1) for f in FINE for x in range(BX - fine_below(f), BX)] + [((f, "z"), 1) for f in FINE]
)
X_DOWN, X_DOWN_TILES = offsets(
    [((f, x), 1) for f in FINE for x in range(fine_above(f, 0))] + [((f, "z"), 1) for f in FINE]
)
FINE_LAYERS = {
    f: [x + XL for x in range(-fine_below(f), BX + fine_above(f, 0))] + list(range(NL, NL + 4)) for f in FINE
}
Y_UP, Y_UP_ROWS = offsets([((f, l), fine_below(f)) for f in FINE for l in FINE_LAYERS[f]])
Y_DOWN, Y_DOWN_ROWS = offsets([((f, l), fine_above(f, 1)) for f in FINE for l in FINE_LAYERS[f]])
MX_UP, MX_UP_ROWS = offsets([((f, m), mid_above(f, 1)) for f in MID for m in range(4 - mid_below(f), 4)])
MX_DOWN, MX_DOWN_ROWS = offsets([((f, m), mid_above(f, 1)) for f in MID for m in range(mid_above(f, 0))])
MID_LAYERS = {f: [m + 4 for m in range(-mid_below(f), 4 + mid_above(f, 0))] for f in MID}
MY_UP, MY_UP_ROWS = offsets([((f, l), mid_below(f)) for f in MID for l in MID_LAYERS[f]])
MY_DOWN, MY_DOWN_ROWS = offsets([((f, l), mid_above(f, 1)) for f in MID for l in MID_LAYERS[f]])


def pack_z(place, iterate, forcing, viscosity, own, first, second, sems):
    parts = ((iterate, 0, 4), (forcing, 4, 4), (viscosity, 8, 3))
    copies = [
        pltpu.make_async_copy(source, own.at[at : at + count], sems.at[i])
        for i, (source, at, count) in enumerate(parts)
    ]
    for copy in copies:
        copy.start()
    lane = iota((BY, BZ), 1) // 16
    odd = place[3] == 1
    for copy, (_, at, count) in zip(copies, parts):
        copy.wait()
        for f in range(at, at + count):
            low = jnp.zeros((BY, BZ), F32)
            high = jnp.zeros((BY, BZ), F32)
            for x in range(BX):
                a = own[f, x]
                mine = lane == x
                low = jnp.where(mine, lane_roll(a, 16 * x - 112), low)
                high = jnp.where(mine, lane_roll(a, 16 * x), high)
            first[f] = jnp.where(odd, low, high)
            second[f] = jnp.where(odd, high, low)


def strips(place, first, second, f):
    odd = place[3] == 1
    a, b = first[f], second[f]
    return jnp.where(odd, b, a), jnp.where(odd, a, b)


def pack_x(place, own, first, second, to_up, to_down):
    lane = iota((BY, BZ), 1)
    for f in FINE:
        low, high = strips(place, first, second, f)
        to_up[X_UP[f, "z"]] = jnp.where(lane >= 96, low, lane_roll(high, -32))
        to_down[X_DOWN[f, "z"]] = jnp.where(lane < 64, low, lane_roll(high, 64))
        for x in range(BX - fine_below(f), BX):
            to_up[X_UP[f, x]] = own[f, x]
        for x in range(fine_above(f, 0)):
            to_down[X_DOWN[f, x]] = own[f, x]


def fine_tile(own, from_low, from_high, f, l):
    x = l - XL
    if 0 <= x < BX:
        return own[f, x]
    if x < 0:
        return from_low[X_UP[f, BX + x]] if -x <= fine_below(f) else None
    return from_high[X_DOWN[f, x - BX]] if x - BX < fine_above(f, 0) else None


def strip_tiles(place, first, second, from_low, from_high, f):
    low, high = strips(place, first, second, f)
    return [low, high, from_low[X_UP[f, "z"]], from_high[X_DOWN[f, "z"]]]


def pack_y(place, own, first, second, from_low, from_high, to_up, to_down):
    for f in FINE:
        sides = strip_tiles(place, first, second, from_low, from_high, f)
        below, above = fine_below(f), fine_above(f, 1)
        for l in FINE_LAYERS[f]:
            tile = sides[l - NL] if l >= NL else fine_tile(own, from_low, from_high, f, l)
            at = Y_UP[f, l]
            to_up[at : at + below] = tile[BY - below :, :]
            at = Y_DOWN[f, l]
            to_down[at : at + above] = tile[:above, :]


def widen(tile, rows, lanes):
    tile = jnp.concatenate([tile] * (rows // BY), axis=0) if rows > BY else tile
    return jnp.concatenate([tile] * (lanes // BZ), axis=1) if lanes > BZ else tile


def inside_yz(place, rows, lanes, ny, nz, end_y, low_y, end_z, low_z, by, bz):
    y = iota((rows, lanes), 0)
    z = iota((rows, lanes), 1)
    held = ((y < end_y) | (y >= rows - low_y)) & ((z < end_z) | (z >= lanes - low_z))
    y = jnp.where(y < end_y, y, y - rows) + widen(place[1] * by, rows, lanes)
    z = jnp.where(z < end_z, z, z - lanes) + widen(place[2] * bz, rows, lanes)
    return jnp.where(held & (y >= 0) & (y < ny) & (z >= 0) & (z < nz), 1, 0)


def inside(yz, x, nx):
    ok = jnp.where((x >= 0) & (x < nx), 1, 0)
    return (yz * widen(ok, *yz.shape)) != 0


def neighbours(low, mid, high, by=1):
    return (low, high, down(mid, 0, by), up(mid, 0, by), down(mid, 1, by), up(mid, 1, by))


def total(values):
    out = values[0]
    for v in values[1:]:
        out = out + v
    return out


def couple(e, es, vs):
    return e * total(vs) + total([a * b for a, b in zip(es, vs)])


def fine_mask_args(place, sizes):
    return inside_yz(place, ROWS, LANES, sizes[1], sizes[2], BY + XH, XL, BZ + 16, 16, BY, BZ)


def compact_matrix():
    a = iota((LANES, BZ), 0) // 2
    return jnp.where(a == iota((LANES, BZ), 1), 0.125, 0.0).astype(jnp.bfloat16)


def spread_matrix():
    a = iota((BZ, LANES), 1) // 2
    return jnp.where(a == iota((BZ, LANES), 0), 1.0, 0.0).astype(jnp.bfloat16)


def exact_dot(a, matrix):
    high = a.astype(jnp.bfloat16)
    rest = a - high.astype(F32)
    mid = rest.astype(jnp.bfloat16)
    low = (rest - mid.astype(F32)).astype(jnp.bfloat16)
    dot = functools.partial(jnp.dot, preferred_element_type=F32)
    return dot(high, matrix) + (dot(mid, matrix) + dot(low, matrix))


def kept(place, sizes):
    low = jnp.where(place[1] > 0, 1.0, 0.0)
    high = jnp.where(place[1] < sizes[1] // BY - 1, 1.0, 0.0)
    return low, high


def side_lanes(l, tiles):
    lane = iota((BY, BZ), 1)
    x = l - XL
    if x < 0:
        a, b = lane_roll(tiles[2], 16 - 16 * l), lane_roll(tiles[2], -(64 + 16 * l))
    elif x < BX:
        a, b = lane_roll(tiles[0], 112 - 16 * x), lane_roll(tiles[1], -16 * x)
    else:
        a, b = lane_roll(tiles[3], 112 - 16 * (x - BX)), lane_roll(tiles[3], -(64 + 16 * (x - BX)))
    return jnp.where(lane >= 112, a, jnp.where(lane < 16, b, 0.0))


def assemble_own(place, own, first, second, from_low, from_high, half):
    for f in FINE:
        sides = strip_tiles(place, first, second, from_low, from_high, f)
        for l in range(NL):
            body = fine_tile(own, from_low, from_high, f, l)
            half[f, l, :, 0:BZ] = jnp.zeros((BY, BZ), F32) if body is None else body
            half[f, l, :, BZ:] = side_lanes(l, sides)


def pair_sums(e, high):
    return e + high, e + down(e, 0), e + up(e, 0), e + down(e, 1), e + up(e, 1)


def weigh(weights, values):
    return total([a * b for a, b in zip(weights, values)])


def fine_level(sizes, place, half, y_low, y_high, whole, full, middle, to_down, to_up, rows, rsum, tsum):
    keep_low, keep_high = kept(place, sizes)

    for f in FINE:
        below, above = fine_below(f), fine_above(f, 1)
        for l in FINE_LAYERS[f]:
            rows[f, l] = jnp.zeros((BY, BZ), F32)
            at = Y_DOWN[f, l]
            rows[f, l, 0:above] = y_high[at : at + above] * keep_high[:above]
            at = Y_UP[f, l]
            rows[f, l, BY - below :] = y_low[at : at + below] * keep_low[:below]
        sides = [rows[f, NL + i] for i in range(4)]
        for l in range(NL):
            whole[f, l, 0:BY] = half[f, l]
            whole[f, l, BY:, 0:BZ] = rows[f, l] if l in FINE_LAYERS[f] else jnp.zeros((BY, BZ), F32)
            whole[f, l, BY:, BZ:] = side_lanes(l, sides)

    def grid(f, l):
        return whole[f, l]

    yz = fine_mask_args(place, sizes)
    for i in range(4):
        full[i, 0] = jnp.zeros((ROWS, LANES), F32)
        full[i, NL - 1] = jnp.zeros((ROWS, LANES), F32)
    full[3, NL - 2] = jnp.zeros((ROWS, LANES), F32)

    def weights(c, l):
        e = grid(8 + c, l)
        return (e + grid(8 + c, l - 1),) + pair_sums(e, grid(8 + c, l + 1))

    def velocities(l, carry):
        good = inside(yz, place[0] * BX + l - XL, sizes[0])
        p = grid(3, l)
        for c in range(3):
            u = grid(c, l)
            us = neighbours(grid(c, l - 1), u, grid(c, l + 1))
            ks = weights(c, l)
            before = grid(3, l - 1) if c == 0 else down(p, c - 1)
            push = 1.2 * (grid(4 + c, l) - (p - before)) + 0.6 * weigh(ks, us)
            full[c, l] = jnp.where(good, 0.4 * u + push / total(ks), 0.0)
        return carry

    loop(1, NL - 1, velocities, 0)

    def outflow(l):
        v, w = full[1, l], full[2, l]
        return (full[0, l + 1] - full[0, l]) + (up(v, 0) - v) + (up(w, 1) - w)

    def pressures(l, carry):
        good = inside(yz, place[0] * BX + l - XL, sizes[0])
        ev, ew = grid(9, l), grid(10, l)
        cell = (grid(8, l) + grid(8, l + 1)) + (ev + up(ev, 0)) + (ew + up(ew, 1))
        full[3, l] = jnp.where(good, grid(3, l) - (0.5 / 6.0) * cell * (grid(7, l) + outflow(l)), 0.0)
        return carry

    loop(1, NL - 2, pressures, 0)

    def layer_residual(c, l):
        u = full[c, l]
        us = neighbours(full[c, l - 1], u, full[c, l + 1])
        ks = weights(c, l)
        p = full[3, l]
        before = full[3, l - 1] if c == 0 else down(p, c - 1)
        return grid(4 + c, l) - (p - before) - 0.5 * (total(ks) * u - weigh(ks, us))

    def residuals(m, carry):
        l = XL + 2 * m
        for c in range(3):
            rsum[c, m] = layer_residual(c, l) + layer_residual(c, l + 1)
        rsum[3, m] = (grid(7, l) + outflow(l)) + (grid(7, l + 1) + outflow(l + 1))
        return carry

    loop(0, 5, residuals, 0)
    for i in range(4):
        rsum[i, 5] = jnp.zeros((ROWS, LANES), F32)
    for c in range(3):
        for m in range(6):
            rsum[4 + c, m] = grid(8 + c, XL + 2 * m) + grid(8 + c, XL + 2 * m + 1)

    matrix = compact_matrix()
    for f in range(7):
        tsum[6 * f : 6 * f + 6] = exact_dot(rsum[f].reshape(6 * ROWS, LANES), matrix).reshape(6, ROWS, BZ)
    for f in MID:
        rows_sent = mid_above(f, 1)
        for m in range(mid_above(f, 0)):
            i = 6 * f + m
            a = tsum[i, pl.ds(0, 8, stride=2), :] + tsum[i, pl.ds(1, 8, stride=2), :]
            at = MX_DOWN[f, m]
            to_down[at : at + rows_sent] = a[:rows_sent]
            if m < 4:
                middle[f, m] = a
            if (f, m) in MX_UP:
                at = MX_UP[f, m]
                to_up[at : at + rows_sent] = a[:rows_sent]


def sizes_of(c):
    return (ROWS if c == 1 else BY), (LANES if c == 2 else BZ)


def last_terms(sizes, place, whole, fine, sums, base, inv, cells, pbase):
    fyz = fine_mask_args(place, sizes)

    def grid(f, l):
        return whole[f, l]

    for x in range(9):
        l = x + XL
        good = inside(fyz, place[0] * BX + x, sizes[0])
        p = fine[3, l]
        for c in range(3):
            u, e = fine[c, l], grid(8 + c, l)
            us = neighbours(fine[c, l - 1], u, fine[c, l + 1])
            xp, ym, yp, zm, zp = pair_sums(e, grid(8 + c, l + 1))
            ks = (e + grid(8 + c, l - 1), xp, ym, yp, zm, zp)
            before = fine[3, l - 1] if c == 0 else down(p, c - 1)
            push = 1.2 * (grid(4 + c, l) - (p - before)) + 0.6 * weigh(ks, us)
            over = 1.0 / total(ks)
            rows, lanes = sizes_of(c)
            for i, k in enumerate(ks):
                sums[c, i, x, 0:rows, 0:lanes] = (0.6 * k)[0:rows, 0:lanes]
            base[c, x, 0:rows, 0:lanes] = jnp.where(good, 0.4 * u + push * over, 0.0)[0:rows, 0:lanes]
            inv[c, x, 0:rows, 0:lanes] = jnp.where(good, over, 0.0)[0:rows, 0:lanes]
            if x < BX and c == 0:
                cell = e + grid(8, l + 1)
            elif x < BX:
                cell = cell + (yp if c == 1 else zp)
        if x < BX:
            cell = (0.5 / 6.0) * cell
            cells[x] = cell[0:BY, 0:BZ]
            pbase[x] = (p - cell * grid(7, l))[0:BY, 0:BZ]


def pack_y_mid(own, from_low, from_high, to_down, to_up, rows):
    for f in MID:
        below, above = mid_below(f), mid_above(f, 1)
        for l in range(ML):
            if l not in MID_LAYERS[f]:
                rows[f, l] = jnp.zeros((4, BZ), F32)
                continue
            m = l - 4
            if m < 0:
                at = MX_UP[f, 4 + m]
                tile = from_low[at : at + above]
            elif m < 4:
                tile = own[f, m, 0:above]
            else:
                at = MX_DOWN[f, m - 4]
                tile = from_high[at : at + above]
            at = MY_DOWN[f, l]
            to_down[at : at + above] = tile
            at = MY_UP[f, l]
            to_up[at : at + below] = tile[4 - below : 4]
            rows[f, l] = tile[0:4]


def coarse_levels(
    sizes, place, last_sums, base, inv, cells, pbase, own, y_low, y_high, out,
    mid, sums, um, over, dm, f2, e2, low, sm, twice, spread, un,
):
    keep_low, keep_high = kept(place, sizes)
    for f in MID:
        below, above = mid_below(f), mid_above(f, 1)
        for l in range(ML):
            mid[f, l] = jnp.zeros((ROWS, BZ), F32)
            mid[f, l, 0:4] = own[f, l]
            if l in MID_LAYERS[f]:
                at = MY_DOWN[f, l]
                mid[f, l, 4 : 4 + above] = y_high[at : at + above] * keep_high[:above]
                at = MY_UP[f, l]
                mid[f, l, ROWS - below :] = y_low[at : at + below] * keep_low[:below]

    shape = (ROWS, BZ)
    yz = inside_yz(place, ROWS, BZ, sizes[1] // 2, sizes[2] // 2, 10, 4, BZ // 2 + 8, 8, BY // 2, BZ // 2)
    row_even = iota(shape, 0) % 2 == 0
    lane_even = iota(shape, 1) % 2 == 0

    def mid_inside(l):
        return inside(yz, place[0] * (BX // 2) + l - 4, sizes[0] // 2)

    for c in range(3):
        sums[c, 0, 1] = mid[4 + c, 0] + mid[4 + c, 1]

    def first_velocities(l, carry):
        good = mid_inside(l)
        for c in range(3):
            xp, ym, yp, zm, zp = pair_sums(mid[4 + c, l], mid[4 + c, l + 1])
            diag = total([sums[c, 0, l], xp, ym, yp, zm, zp])
            sums[c, 0, l + 1] = xp
            sums[c, 1, l] = ym
            sums[c, 2, l] = yp
            sums[c, 3, l] = zm
            sums[c, 4, l] = zp
            dm[c, l] = diag
            inverse = 1.0 / diag
            over[c, l] = inverse
            um[c, l] = jnp.where(good, 4.8 * mid[c, l] * inverse, 0.0)
        return carry

    loop(1, 13, first_velocities, 0)

    def weights(c, l):
        return (sums[c, 0, l], sums[c, 0, l + 1]) + tuple(sums[c, i, l] for i in range(1, 5))

    def outflow(v, l):
        b, w = v[1, l], v[2, l]
        return (v[0, l + 1] - v[0, l]) + (up(b, 0) - b) + (up(w, 1) - w)

    def mid_cell(l):
        return sums[0, 0, l + 1] + sums[1, 2, l] + sums[2, 4, l]

    def first_pressures(l, carry):
        q = mid[3, l] + 0.5 * outflow(um, l)
        um[3, l] = jnp.where(mid_inside(l), (-0.5 / 6.0) * mid_cell(l) * q, 0.0)
        return carry

    loop(1, 12, first_pressures, 0)

    def expand(a):
        a = a + up(a, 0)
        a = jnp.where(row_even, a, down(a, 0))
        a = a + up(a, 1)
        return 0.125 * jnp.where(lane_even, a, down(a, 1))

    def layer_residual(c, l):
        u = um[c, l]
        us = neighbours(um[c, l - 1], u, um[c, l + 1])
        p = um[3, l]
        before = um[3, l - 1] if c == 0 else down(p, c - 1)
        return mid[c, l] - 0.5 * (p - before) - 0.125 * (dm[c, l] * u - weigh(weights(c, l), us))

    def residuals(k, carry):
        l = 2 + 2 * k
        for c in range(3):
            f2[c, k] = expand(layer_residual(c, l) + layer_residual(c, l + 1))
        f2[3, k] = expand((mid[3, l] + 0.5 * outflow(um, l)) + (mid[3, l + 1] + 0.5 * outflow(um, l + 1)))
        return carry

    loop(0, 5, residuals, 0)

    def low_viscosity(k, carry):
        for c in range(3):
            e2[c, k] = expand(mid[4 + c, 2 * k] + mid[4 + c, 2 * k + 1])
        return carry

    loop(0, 7, low_viscosity, 0)

    def low_inside(k):
        return inside(yz, place[0] * (BX // 4) + k - 1, sizes[0] // 4)

    def low_velocities(k, carry):
        good = low_inside(k)
        for c in range(3):
            e = e2[c, k + 1]
            diag = 6.0 * e + total(neighbours(e2[c, k], e, e2[c, k + 2], 2))
            low[c, k] = jnp.where(good, 19.2 * f2[c, k] / diag, 0.0)
        return carry

    loop(0, 5, low_velocities, 0)

    def low_pressures(k, carry):
        v, w, ev, ew = low[1, k], low[2, k], e2[1, k + 1], e2[2, k + 1]
        flow = (low[0, k + 1] - low[0, k]) + (up(v, 0, 2) - v) + (up(w, 1, 2) - w)
        cell = (e2[0, k + 1] + e2[0, k + 2]) + (ev + up(ev, 0, 2)) + (ew + up(ew, 1, 2))
        low[3, k] = jnp.where(low_inside(k), (-0.5 / 6.0) * cell * (f2[3, k] + 0.25 * flow), 0.0)
        return carry

    loop(0, 4, low_pressures, 0)

    def corrected(k, carry):
        for i in range(3):
            um[i, 2 * k + 2] = um[i, 2 * k + 2] + low[i, k]
            um[i, 2 * k + 3] = um[i, 2 * k + 3] + low[i, k]
        return carry

    loop(0, 5, corrected, 0)
    for k in range(4):
        um[3, 2 * k + 2] = um[3, 2 * k + 2] + low[3, k]
        um[3, 2 * k + 3] = um[3, 2 * k + 3] + low[3, k]

    def second_velocities(l, carry):
        good = mid_inside(l)
        p = um[3, l]
        for c in range(3):
            u = um[c, l]
            us = neighbours(um[c, l - 1], u, um[c, l + 1])
            before = um[3, l - 1] if c == 0 else down(p, c - 1)
            push = 4.8 * (mid[c, l] - 0.5 * (p - before)) + 0.6 * weigh(weights(c, l), us)
            sm[c, l] = jnp.where(good, 0.4 * u + push * over[c, l], 0.0)
        return carry

    loop(3, 10, second_velocities, 0)

    def second_pressures(l, carry):
        q = mid[3, l] + 0.5 * outflow(sm, l)
        sm[3, l] = jnp.where(mid_inside(l), um[3, l] - (0.5 / 6.0) * mid_cell(l) * q, 0.0)
        return carry

    loop(3, 9, second_pressures, 0)

    last_row = iota((8, BZ), 0) == 7
    for i in range(4):
        for m in range(6):
            a = sm[i, 3 + m]
            a = jnp.where(last_row, a[8:16], a[0:8])
            twice[6 * i + m, pl.ds(0, 8, stride=2), :] = a
            twice[6 * i + m, pl.ds(1, 8, stride=2), :] = a
    matrix = spread_matrix()
    for i in range(4):
        wide = exact_dot(twice[6 * i : 6 * i + 6].reshape(6 * ROWS, BZ), matrix)
        spread[i] = wide.reshape(6, ROWS, LANES)

    for m in range(1, 6):
        p = spread[3, m]
        for c in range(3):
            rows, lanes = sizes_of(c)
            z = spread[c, m]
            sides = (down(z, 0), up(z, 0), down(z, 1), up(z, 1))
            for x in (2 * m - 2, 2 * m - 1):
                if x > BX:
                    continue
                zs = (spread[c, (x + 1) // 2], spread[c, (x + 3) // 2]) + sides
                push = weigh([last_sums[c, i, x, 0:rows, 0:lanes] for i in range(6)], [v[0:rows, 0:lanes] for v in zs])
                if c > 0:
                    push = push - 1.2 * (p - down(p, c - 1))[0:rows, 0:lanes]
                elif x % 2 == 0:
                    push = push - 1.2 * (p - spread[3, m - 1])[0:rows, 0:lanes]
                u = base[c, x, 0:rows, 0:lanes] + 0.4 * z[0:rows, 0:lanes] + inv[c, x, 0:rows, 0:lanes] * push
                un[c, x, 0:rows, 0:lanes] = u
                if x < BX:
                    out[c, x] = u[0:BY, 0:BZ]

    for x in range(BX):
        v, w = un[1, x, :, 0:BZ], un[2, x, 0:BY, :]
        flow = un[0, x + 1, 0:BY, 0:BZ] - un[0, x, 0:BY, 0:BZ]
        flow = flow + (up(v, 0) - v)[0:BY] + (up(w, 1) - w)[:, 0:BZ]
        out[3, x] = pbase[x] + spread[3, (x + 2) // 2, 0:BY, 0:BZ] - cells[x] * flow


WIDE, TILE, HUGE = (ROWS, BZ), (BY, BZ), (ROWS, LANES)
HALF = (11, NL, BY, LANES)
FINE_OUT = [(11, NL) + HUGE, (4, NL) + HUGE, (7, 4) + TILE, (MX_DOWN_ROWS, BZ), (MX_UP_ROWS, BZ)]
FINE_SCRATCH = [(11, NL + 4) + TILE, (7, 6) + HUGE, (42,) + WIDE]
LAST_OUT = [(3, 6, 9) + HUGE, (3, 9) + HUGE, (3, 9) + HUGE, (BX,) + TILE, (BX,) + TILE]
COARSE_SCRATCH = [
    (7, ML) + WIDE, (3, 5, ML) + WIDE, (4, ML) + WIDE, (3, ML) + WIDE, (3, ML) + WIDE, (4, 5) + WIDE, (3, 7) + WIDE,
    (4, 5) + WIDE, (4, ML) + WIDE, (24,) + WIDE, (4, 6) + HUGE, (3, 9) + HUGE,
]


def per_device(sizes, iterate, forcing, viscosity):
    nx, ny, nz = (lax.axis_size(a) for a in ("gx", "gy", "gz"))
    at = [lax.axis_index(a) for a in ("gx", "gy", "gz")]
    place = jnp.stack([jnp.full((BY, BZ), a, jnp.int32) for a in at + [at[2] % 2]])

    def swap(a, axis, count, start):
        pairs = []
        for i in range(start, count - 1, 2):
            pairs += [(i, i + 1), (i + 1, i)]
        return lax.ppermute(a, axis, pairs)

    def around(a, axis, count, by):
        return lax.ppermute(a, axis, [(i, (i + by) % count) for i in range(count)])

    def to_next(a, axis, count):
        return lax.ppermute(a, axis, [(i, i + 1) for i in range(count - 1)])

    def to_previous(a, axis, count):
        return lax.ppermute(a, axis, [(i + 1, i) for i in range(count - 1)])

    iterate, forcing, viscosity = (
        pltpu.with_memory_space_constraint(a, pltpu.HBM) for a in (iterate, forcing, viscosity)
    )
    tile = (BY, BZ)
    own, first, second = call(
        pack_z, [(11, BX) + tile, (11,) + tile, (11,) + tile], [pltpu.SemaphoreType.DMA((3,))],
        place, iterate, forcing, viscosity, space=HBM,
    )
    first = swap(first, "gz", nz, 1)
    second = swap(second, "gz", nz, 0)

    upward, downward = call(pack_x, [(X_UP_TILES,) + tile, (X_DOWN_TILES,) + tile], [], place, own, first, second)
    x_low = to_next(upward, "gx", nx)
    x_high = to_previous(downward, "gx", nx)

    upward, downward = call(
        pack_y, [(Y_UP_ROWS, BZ), (Y_DOWN_ROWS, BZ)], [], place, own, first, second, x_low, x_high
    )
    y_low = around(upward, "gy", ny, 1)
    y_high = around(downward, "gy", ny, -1)
    (half,) = call(assemble_own, [HALF], [], place, own, first, second, x_low, x_high)

    whole, fine, middle, downward, upward = call(
        functools.partial(fine_level, sizes), FINE_OUT, FINE_SCRATCH, place, half, y_low, y_high
    )
    x_low = to_next(upward, "gx", nx)
    x_high = to_previous(downward, "gx", nx)

    downward, upward, middle = call(
        pack_y_mid, [(MY_DOWN_ROWS, BZ), (MY_UP_ROWS, BZ), (7, ML, 4, BZ)], [], middle, x_low, x_high
    )
    y_low = around(upward, "gy", ny, 1)
    y_high = around(downward, "gy", ny, -1)

    terms = call(functools.partial(last_terms, sizes), LAST_OUT, [], place, whole, fine)
    (updated,) = call(
        functools.partial(coarse_levels, sizes), [(4, BX) + tile], COARSE_SCRATCH,
        place, *terms, middle, y_low, y_high,
    )
    return updated


def solution(mesh):
    spec = P(None, "gx", "gy", "gz")
    sizes = (mesh.shape["gx"] * BX, mesh.shape["gy"] * BY, mesh.shape["gz"] * BZ)
    return jax.shard_map(
        functools.partial(per_device, sizes), mesh=mesh, in_specs=(spec,) * 3, out_specs=spec, check_vma=False
    )
```

```python
import functools

import jax
import jax.numpy as jnp
from jax import lax
from jax.experimental import pallas as pl
from jax.experimental.pallas import tpu as pltpu
from jax.sharding import PartitionSpec as P

F32 = jnp.float32
BX, BY, BZ = 8, 8, 128
XL, XH = 2, 4
NL = BX + XL + XH
ROWS, LANES = 16, 256
ML = 14
VMEM = pl.BlockSpec(memory_space=pltpu.VMEM)
HBM = pl.BlockSpec(memory_space=pltpu.HBM)
UNROLL = True
PARAMS = pltpu.CompilerParams(vmem_limit_bytes=20 * 1024 * 1024)


def call(kernel, outs, scratch, *args, space=VMEM):
    specs = [VMEM if a.dtype == jnp.int32 else space for a in args]
    return pl.pallas_call(
        kernel,
        out_shape=[jax.ShapeDtypeStruct(s, F32) for s in outs],
        in_specs=specs,
        out_specs=[VMEM] * len(outs),
        scratch_shapes=[pltpu.VMEM(s, F32) if isinstance(s, tuple) else s for s in scratch],
        compiler_params=PARAMS,
    )(*args)


def loop(start, stop, body, carry):
    return lax.fori_loop(start, stop, body, carry, unroll=UNROLL)


def iota(shape, dim):
    return lax.broadcasted_iota(jnp.int32, shape, dim)


def up(a, dim, by=1):
    return pltpu.roll(a, a.shape[dim] - by, dim)


def down(a, dim, by=1):
    return pltpu.roll(a, by, dim)


def lane_roll(a, by):
    by = by % a.shape[1]
    return pltpu.roll(a, by, 1) if by else a


def fine_above(f, dim):
    own = f % 4 == dim and f != 3
    return (3, 2, 3)[f // 4] + own if f % 4 < 3 else (3, 2)[f // 4]


def fine_below(f):
    return 1 if 4 <= f < 8 else 2


def mid_above(f, dim):
    return (4, 5)[f // 4] + (f % 4 == dim and f != 3)


def mid_below(f):
    return (3, 4)[f // 4]


def offsets(entries, unit=8):
    table, at = {}, 0
    for key, rows in entries:
        table[key] = at
        at += rows
    return table, -(-at // unit) * unit


FINE, MID = range(11), range(7)
X_UP = [(f, x) for f in FINE for x in range(BX - fine_below(f), BX)]
X_DOWN = [(f, x) for f in FINE for x in range(fine_above(f, 0))]
EARLY_UP, EARLY_DOWN = 18, 24
X_UP_EARLY, X_UP_EARLY_TILES = offsets([(key, 1) for key in X_UP[:EARLY_UP]], 8)
X_DOWN_EARLY, X_DOWN_EARLY_TILES = offsets([(key, 1) for key in X_DOWN[:EARLY_DOWN]], 1)
X_UP_LATE, X_UP_LATE_TILES = offsets([((f, "z"), 1) for f in FINE] + [(key, 1) for key in X_UP[EARLY_UP:]], 1)
X_DOWN_LATE, X_DOWN_LATE_TILES = offsets([((f, "z"), 1) for f in FINE] + [(key, 1) for key in X_DOWN[EARLY_DOWN:]], 1)
FINE_LAYERS = {
    f: [x + XL for x in range(-fine_below(f), BX + fine_above(f, 0))] + list(range(NL, NL + 4)) for f in FINE
}
Y_UP, Y_UP_ROWS = offsets([((f, l), fine_below(f)) for f in FINE for l in FINE_LAYERS[f]])
Y_DOWN, Y_DOWN_ROWS = offsets([((f, l), fine_above(f, 1)) for f in FINE for l in FINE_LAYERS[f]])
MX_UP, MX_UP_ROWS = offsets([((f, m), mid_above(f, 1)) for f in MID for m in range(4 - mid_below(f), 4)])
MX_DOWN, MX_DOWN_ROWS = offsets([((f, m), mid_above(f, 1)) for f in MID for m in range(mid_above(f, 0))])
MID_LAYERS = {f: [m + 4 for m in range(-mid_below(f), 4 + mid_above(f, 0))] for f in MID}
MY_UP, MY_UP_ROWS = offsets([((f, l), mid_below(f)) for f in MID for l in MID_LAYERS[f]])
MY_DOWN, MY_DOWN_ROWS = offsets([((f, l), mid_above(f, 1)) for f in MID for l in MID_LAYERS[f]])


def pack_z(place, iterate, forcing, viscosity, own, first, second, sems):
    parts = ((iterate, 0, 4), (forcing, 4, 4), (viscosity, 8, 3))
    copies = [
        pltpu.make_async_copy(source, own.at[at : at + count], sems.at[i])
        for i, (source, at, count) in enumerate(parts)
    ]
    for copy in copies:
        copy.start()
    lane = iota((BY, BZ), 1) // 16
    odd = place[3] == 1
    for copy, (_, at, count) in zip(copies, parts):
        copy.wait()
        for f in range(at, at + count):
            low = jnp.zeros((BY, BZ), F32)
            high = jnp.zeros((BY, BZ), F32)
            for x in range(BX):
                a = own[f, x]
                mine = lane == x
                low = jnp.where(mine, lane_roll(a, 16 * x - 112), low)
                high = jnp.where(mine, lane_roll(a, 16 * x), high)
            first[f] = jnp.where(odd, low, high)
            second[f] = jnp.where(odd, high, low)


def strips(place, first, second, f):
    odd = place[3] == 1
    a, b = first[f], second[f]
    return jnp.where(odd, b, a), jnp.where(odd, a, b)


def fill(message, table, own):
    for key, at in table.items():
        if key[1] != "z":
            message[at] = own[key]
    for at in range(len(table), message.shape[0]):
        message[at] = jnp.zeros((BY, BZ), F32)


def pack_x_early(own, to_up, to_down):
    fill(to_up, X_UP_EARLY, own)
    fill(to_down, X_DOWN_EARLY, own)


def pack_x_late(place, own, first, second, to_up, to_down):
    lane = iota((BY, BZ), 1)
    for f in FINE:
        low, high = strips(place, first, second, f)
        to_up[X_UP_LATE[f, "z"]] = jnp.where(lane >= 96, low, lane_roll(high, -32))
        to_down[X_DOWN_LATE[f, "z"]] = jnp.where(lane < 64, low, lane_roll(high, 64))
    fill(to_up, X_UP_LATE, own)
    fill(to_down, X_DOWN_LATE, own)


def fine_tile(own, halos, f, l):
    x = l - XL
    if 0 <= x < BX:
        return own[f, x]
    low_early, high_early, low_late, high_late = halos
    key = (f, BX + x) if x < 0 else (f, x - BX)
    early, late = (low_early, low_late) if x < 0 else (high_early, high_late)
    table, rest = (X_UP_EARLY, X_UP_LATE) if x < 0 else (X_DOWN_EARLY, X_DOWN_LATE)
    if key in table:
        return early[table[key]]
    return late[rest[key]] if key in rest else None


def strip_tiles(place, first, second, halos, f):
    low, high = strips(place, first, second, f)
    return [low, high, halos[2][X_UP_LATE[f, "z"]], halos[3][X_DOWN_LATE[f, "z"]]]


def pack_y(place, own, first, second, low_early, high_early, low_late, high_late, to_up, to_down):
    halos = (low_early, high_early, low_late, high_late)
    for f in FINE:
        sides = strip_tiles(place, first, second, halos, f)
        below, above = fine_below(f), fine_above(f, 1)
        for l in FINE_LAYERS[f]:
            tile = sides[l - NL] if l >= NL else fine_tile(own, halos, f, l)
            at = Y_UP[f, l]
            to_up[at : at + below] = tile[BY - below :, :]
            at = Y_DOWN[f, l]
            to_down[at : at + above] = tile[:above, :]


def widen(tile, rows, lanes):
    tile = jnp.concatenate([tile] * (rows // BY), axis=0) if rows > BY else tile
    return jnp.concatenate([tile] * (lanes // BZ), axis=1) if lanes > BZ else tile


def inside_yz(place, rows, lanes, ny, nz, end_y, low_y, end_z, low_z, by, bz):
    y = iota((rows, lanes), 0)
    z = iota((rows, lanes), 1)
    held = ((y < end_y) | (y >= rows - low_y)) & ((z < end_z) | (z >= lanes - low_z))
    y = jnp.where(y < end_y, y, y - rows) + widen(place[1] * by, rows, lanes)
    z = jnp.where(z < end_z, z, z - lanes) + widen(place[2] * bz, rows, lanes)
    return jnp.where(held & (y >= 0) & (y < ny) & (z >= 0) & (z < nz), 1, 0)


def inside(yz, x, nx):
    ok = jnp.where((x >= 0) & (x < nx), 1, 0)
    return (yz * widen(ok, *yz.shape)) != 0


def neighbours(low, mid, high, by=1):
    return (low, high, down(mid, 0, by), up(mid, 0, by), down(mid, 1, by), up(mid, 1, by))


def total(values):
    out = values[0]
    for v in values[1:]:
        out = out + v
    return out


def couple(e, es, vs):
    return e * total(vs) + total([a * b for a, b in zip(es, vs)])


def fine_mask_args(place, sizes):
    return inside_yz(place, ROWS, LANES, sizes[1], sizes[2], BY + XH, XL, BZ + 16, 16, BY, BZ)


def compact_matrix():
    a = iota((LANES, BZ), 0) // 2
    return jnp.where(a == iota((LANES, BZ), 1), 0.125, 0.0).astype(jnp.bfloat16)


def spread_matrix():
    a = iota((BZ, LANES), 1) // 2
    return jnp.where(a == iota((BZ, LANES), 0), 1.0, 0.0).astype(jnp.bfloat16)


def exact_dot(a, matrix):
    high = a.astype(jnp.bfloat16)
    rest = a - high.astype(F32)
    mid = rest.astype(jnp.bfloat16)
    low = (rest - mid.astype(F32)).astype(jnp.bfloat16)
    dot = functools.partial(jnp.dot, preferred_element_type=F32)
    return dot(high, matrix) + (dot(mid, matrix) + dot(low, matrix))


def kept(place, sizes):
    low = jnp.where(place[1] > 0, 1.0, 0.0)
    high = jnp.where(place[1] < sizes[1] // BY - 1, 1.0, 0.0)
    return low, high


def side_lanes(l, tiles):
    lane = iota((BY, BZ), 1)
    x = l - XL
    if x < 0:
        a, b = lane_roll(tiles[2], 16 - 16 * l), lane_roll(tiles[2], -(64 + 16 * l))
    elif x < BX:
        a, b = lane_roll(tiles[0], 112 - 16 * x), lane_roll(tiles[1], -16 * x)
    else:
        a, b = lane_roll(tiles[3], 112 - 16 * (x - BX)), lane_roll(tiles[3], -(64 + 16 * (x - BX)))
    return jnp.where(lane >= 112, a, jnp.where(lane < 16, b, 0.0))


def assemble_own(place, own, first, second, low_early, high_early, low_late, high_late, half):
    halos = (low_early, high_early, low_late, high_late)
    for f in FINE:
        sides = strip_tiles(place, first, second, halos, f)
        for l in range(NL):
            body = fine_tile(own, halos, f, l)
            half[f, l, :, 0:BZ] = jnp.zeros((BY, BZ), F32) if body is None else body
            half[f, l, :, BZ:] = side_lanes(l, sides)


def pair_sums(e, high):
    return e + high, e + down(e, 0), e + up(e, 0), e + down(e, 1), e + up(e, 1)


def weigh(weights, values):
    return total([a * b for a, b in zip(weights, values)])


def fine_level(sizes, place, half, y_low, y_high, whole, full, middle, to_down, to_up, rows, rsum, tsum):
    keep_low, keep_high = kept(place, sizes)

    for f in FINE:
        below, above = fine_below(f), fine_above(f, 1)
        for l in FINE_LAYERS[f]:
            rows[f, l] = jnp.zeros((BY, BZ), F32)
            at = Y_DOWN[f, l]
            rows[f, l, 0:above] = y_high[at : at + above] * keep_high[:above]
            at = Y_UP[f, l]
            rows[f, l, BY - below :] = y_low[at : at + below] * keep_low[:below]
        sides = [rows[f, NL + i] for i in range(4)]
        for l in range(NL):
            whole[f, l, 0:BY] = half[f, l]
            whole[f, l, BY:, 0:BZ] = rows[f, l] if l in FINE_LAYERS[f] else jnp.zeros((BY, BZ), F32)
            whole[f, l, BY:, BZ:] = side_lanes(l, sides)

    def grid(f, l):
        return whole[f, l]

    yz = fine_mask_args(place, sizes)
    for i in range(4):
        full[i, 0] = jnp.zeros((ROWS, LANES), F32)
        full[i, NL - 1] = jnp.zeros((ROWS, LANES), F32)
    full[3, NL - 2] = jnp.zeros((ROWS, LANES), F32)

    def weights(c, l):
        e = grid(8 + c, l)
        return (e + grid(8 + c, l - 1),) + pair_sums(e, grid(8 + c, l + 1))

    def velocities(l, carry):
        good = inside(yz, place[0] * BX + l - XL, sizes[0])
        p = grid(3, l)
        for c in range(3):
            u = grid(c, l)
            us = neighbours(grid(c, l - 1), u, grid(c, l + 1))
            ks = weights(c, l)
            before = grid(3, l - 1) if c == 0 else down(p, c - 1)
            push = 1.2 * (grid(4 + c, l) - (p - before)) + 0.6 * weigh(ks, us)
            full[c, l] = jnp.where(good, 0.4 * u + push / total(ks), 0.0)
        return carry

    loop(1, NL - 1, velocities, 0)

    def outflow(l):
        v, w = full[1, l], full[2, l]
        return (full[0, l + 1] - full[0, l]) + (up(v, 0) - v) + (up(w, 1) - w)

    def pressures(l, carry):
        good = inside(yz, place[0] * BX + l - XL, sizes[0])
        ev, ew = grid(9, l), grid(10, l)
        cell = (grid(8, l) + grid(8, l + 1)) + (ev + up(ev, 0)) + (ew + up(ew, 1))
        full[3, l] = jnp.where(good, grid(3, l) - (0.5 / 6.0) * cell * (grid(7, l) + outflow(l)), 0.0)
        return carry

    loop(1, NL - 2, pressures, 0)

    def layer_residual(c, l):
        u = full[c, l]
        us = neighbours(full[c, l - 1], u, full[c, l + 1])
        ks = weights(c, l)
        p = full[3, l]
        before = full[3, l - 1] if c == 0 else down(p, c - 1)
        return grid(4 + c, l) - (p - before) - 0.5 * (total(ks) * u - weigh(ks, us))

    def residuals(m, carry):
        l = XL + 2 * m
        for c in range(3):
            rsum[c, m] = layer_residual(c, l) + layer_residual(c, l + 1)
        rsum[3, m] = (grid(7, l) + outflow(l)) + (grid(7, l + 1) + outflow(l + 1))
        return carry

    loop(0, 5, residuals, 0)
    for i in range(4):
        rsum[i, 5] = jnp.zeros((ROWS, LANES), F32)
    for c in range(3):
        for m in range(6):
            rsum[4 + c, m] = grid(8 + c, XL + 2 * m) + grid(8 + c, XL + 2 * m + 1)

    matrix = compact_matrix()
    for f in range(7):
        tsum[6 * f : 6 * f + 6] = exact_dot(rsum[f].reshape(6 * ROWS, LANES), matrix).reshape(6, ROWS, BZ)
    for f in MID:
        rows_sent = mid_above(f, 1)
        for m in range(mid_above(f, 0)):
            i = 6 * f + m
            a = tsum[i, pl.ds(0, 8, stride=2), :] + tsum[i, pl.ds(1, 8, stride=2), :]
            at = MX_DOWN[f, m]
            to_down[at : at + rows_sent] = a[:rows_sent]
            if m < 4:
                middle[f, m] = a
            if (f, m) in MX_UP:
                at = MX_UP[f, m]
                to_up[at : at + rows_sent] = a[:rows_sent]


def sizes_of(c):
    return (ROWS if c == 1 else BY), (LANES if c == 2 else BZ)


def last_terms(sizes, place, whole, fine, sums, base, inv, cells, pbase):
    fyz = fine_mask_args(place, sizes)

    def grid(f, l):
        return whole[f, l]

    for x in range(9):
        l = x + XL
        good = inside(fyz, place[0] * BX + x, sizes[0])
        p = fine[3, l]
        for c in range(3):
            u, e = fine[c, l], grid(8 + c, l)
            us = neighbours(fine[c, l - 1], u, fine[c, l + 1])
            xp, ym, yp, zm, zp = pair_sums(e, grid(8 + c, l + 1))
            ks = (e + grid(8 + c, l - 1), xp, ym, yp, zm, zp)
            before = fine[3, l - 1] if c == 0 else down(p, c - 1)
            push = 1.2 * (grid(4 + c, l) - (p - before)) + 0.6 * weigh(ks, us)
            over = 1.0 / total(ks)
            rows, lanes = sizes_of(c)
            for i, k in enumerate(ks):
                sums[c, i, x, 0:rows, 0:lanes] = (0.6 * k)[0:rows, 0:lanes]
            base[c, x, 0:rows, 0:lanes] = jnp.where(good, 0.4 * u + push * over, 0.0)[0:rows, 0:lanes]
            inv[c, x, 0:rows, 0:lanes] = jnp.where(good, over, 0.0)[0:rows, 0:lanes]
            if x < BX and c == 0:
                cell = e + grid(8, l + 1)
            elif x < BX:
                cell = cell + (yp if c == 1 else zp)
        if x < BX:
            cell = (0.5 / 6.0) * cell
            cells[x] = cell[0:BY, 0:BZ]
            pbase[x] = (p - cell * grid(7, l))[0:BY, 0:BZ]


def pack_y_mid(own, from_low, from_high, to_down, to_up, rows):
    for f in MID:
        below, above = mid_below(f), mid_above(f, 1)
        for l in range(ML):
            if l not in MID_LAYERS[f]:
                rows[f, l] = jnp.zeros((4, BZ), F32)
                continue
            m = l - 4
            if m < 0:
                at = MX_UP[f, 4 + m]
                tile = from_low[at : at + above]
            elif m < 4:
                tile = own[f, m, 0:above]
            else:
                at = MX_DOWN[f, m - 4]
                tile = from_high[at : at + above]
            at = MY_DOWN[f, l]
            to_down[at : at + above] = tile
            at = MY_UP[f, l]
            to_up[at : at + below] = tile[4 - below : 4]
            rows[f, l] = tile[0:4]


def coarse_levels(
    sizes, place, last_sums, base, inv, cells, pbase, own, y_low, y_high, out,
    mid, sums, um, over, dm, f2, e2, low, sm, twice, spread, un,
):
    keep_low, keep_high = kept(place, sizes)
    for f in MID:
        below, above = mid_below(f), mid_above(f, 1)
        for l in range(ML):
            mid[f, l] = jnp.zeros((ROWS, BZ), F32)
            mid[f, l, 0:4] = own[f, l]
            if l in MID_LAYERS[f]:
                at = MY_DOWN[f, l]
                mid[f, l, 4 : 4 + above] = y_high[at : at + above] * keep_high[:above]
                at = MY_UP[f, l]
                mid[f, l, ROWS - below :] = y_low[at : at + below] * keep_low[:below]

    shape = (ROWS, BZ)
    yz = inside_yz(place, ROWS, BZ, sizes[1] // 2, sizes[2] // 2, 10, 4, BZ // 2 + 8, 8, BY // 2, BZ // 2)
    row_even = iota(shape, 0) % 2 == 0
    lane_even = iota(shape, 1) % 2 == 0

    def mid_inside(l):
        return inside(yz, place[0] * (BX // 2) + l - 4, sizes[0] // 2)

    for c in range(3):
        sums[c, 0, 1] = mid[4 + c, 0] + mid[4 + c, 1]

    def first_velocities(l, carry):
        good = mid_inside(l)
        for c in range(3):
            xp, ym, yp, zm, zp = pair_sums(mid[4 + c, l], mid[4 + c, l + 1])
            diag = total([sums[c, 0, l], xp, ym, yp, zm, zp])
            sums[c, 0, l + 1] = xp
            sums[c, 1, l] = ym
            sums[c, 2, l] = yp
            sums[c, 3, l] = zm
            sums[c, 4, l] = zp
            dm[c, l] = diag
            inverse = 1.0 / diag
            over[c, l] = inverse
            um[c, l] = jnp.where(good, 4.8 * mid[c, l] * inverse, 0.0)
        return carry

    loop(1, 13, first_velocities, 0)

    def weights(c, l):
        return (sums[c, 0, l], sums[c, 0, l + 1]) + tuple(sums[c, i, l] for i in range(1, 5))

    def outflow(v, l):
        b, w = v[1, l], v[2, l]
        return (v[0, l + 1] - v[0, l]) + (up(b, 0) - b) + (up(w, 1) - w)

    def mid_cell(l):
        return sums[0, 0, l + 1] + sums[1, 2, l] + sums[2, 4, l]

    def first_pressures(l, carry):
        q = mid[3, l] + 0.5 * outflow(um, l)
        um[3, l] = jnp.where(mid_inside(l), (-0.5 / 6.0) * mid_cell(l) * q, 0.0)
        return carry

    loop(1, 12, first_pressures, 0)

    def expand(a):
        a = a + up(a, 0)
        a = jnp.where(row_even, a, down(a, 0))
        a = a + up(a, 1)
        return 0.125 * jnp.where(lane_even, a, down(a, 1))

    def layer_residual(c, l):
        u = um[c, l]
        us = neighbours(um[c, l - 1], u, um[c, l + 1])
        p = um[3, l]
        before = um[3, l - 1] if c == 0 else down(p, c - 1)
        return mid[c, l] - 0.5 * (p - before) - 0.125 * (dm[c, l] * u - weigh(weights(c, l), us))

    def residuals(k, carry):
        l = 2 + 2 * k
        for c in range(3):
            f2[c, k] = expand(layer_residual(c, l) + layer_residual(c, l + 1))
        f2[3, k] = expand((mid[3, l] + 0.5 * outflow(um, l)) + (mid[3, l + 1] + 0.5 * outflow(um, l + 1)))
        return carry

    loop(0, 5, residuals, 0)

    def low_viscosity(k, carry):
        for c in range(3):
            e2[c, k] = expand(mid[4 + c, 2 * k] + mid[4 + c, 2 * k + 1])
        return carry

    loop(0, 7, low_viscosity, 0)

    def low_inside(k):
        return inside(yz, place[0] * (BX // 4) + k - 1, sizes[0] // 4)

    def low_velocities(k, carry):
        good = low_inside(k)
        for c in range(3):
            e = e2[c, k + 1]
            diag = 6.0 * e + total(neighbours(e2[c, k], e, e2[c, k + 2], 2))
            low[c, k] = jnp.where(good, 19.2 * f2[c, k] / diag, 0.0)
        return carry

    loop(0, 5, low_velocities, 0)

    def low_pressures(k, carry):
        v, w, ev, ew = low[1, k], low[2, k], e2[1, k + 1], e2[2, k + 1]
        flow = (low[0, k + 1] - low[0, k]) + (up(v, 0, 2) - v) + (up(w, 1, 2) - w)
        cell = (e2[0, k + 1] + e2[0, k + 2]) + (ev + up(ev, 0, 2)) + (ew + up(ew, 1, 2))
        low[3, k] = jnp.where(low_inside(k), (-0.5 / 6.0) * cell * (f2[3, k] + 0.25 * flow), 0.0)
        return carry

    loop(0, 4, low_pressures, 0)

    def corrected(k, carry):
        for i in range(3):
            um[i, 2 * k + 2] = um[i, 2 * k + 2] + low[i, k]
            um[i, 2 * k + 3] = um[i, 2 * k + 3] + low[i, k]
        return carry

    loop(0, 5, corrected, 0)
    for k in range(4):
        um[3, 2 * k + 2] = um[3, 2 * k + 2] + low[3, k]
        um[3, 2 * k + 3] = um[3, 2 * k + 3] + low[3, k]

    def second_velocities(l, carry):
        good = mid_inside(l)
        p = um[3, l]
        for c in range(3):
            u = um[c, l]
            us = neighbours(um[c, l - 1], u, um[c, l + 1])
            before = um[3, l - 1] if c == 0 else down(p, c - 1)
            push = 4.8 * (mid[c, l] - 0.5 * (p - before)) + 0.6 * weigh(weights(c, l), us)
            sm[c, l] = jnp.where(good, 0.4 * u + push * over[c, l], 0.0)
        return carry

    loop(3, 10, second_velocities, 0)

    def second_pressures(l, carry):
        q = mid[3, l] + 0.5 * outflow(sm, l)
        sm[3, l] = jnp.where(mid_inside(l), um[3, l] - (0.5 / 6.0) * mid_cell(l) * q, 0.0)
        return carry

    loop(3, 9, second_pressures, 0)

    last_row = iota((8, BZ), 0) == 7
    for i in range(4):
        for m in range(6):
            a = sm[i, 3 + m]
            a = jnp.where(last_row, a[8:16], a[0:8])
            twice[6 * i + m, pl.ds(0, 8, stride=2), :] = a
            twice[6 * i + m, pl.ds(1, 8, stride=2), :] = a
    matrix = spread_matrix()
    for i in range(4):
        wide = exact_dot(twice[6 * i : 6 * i + 6].reshape(6 * ROWS, BZ), matrix)
        spread[i] = wide.reshape(6, ROWS, LANES)

    for m in range(1, 6):
        p = spread[3, m]
        for c in range(3):
            rows, lanes = sizes_of(c)
            z = spread[c, m]
            sides = (down(z, 0), up(z, 0), down(z, 1), up(z, 1))
            for x in (2 * m - 2, 2 * m - 1):
                if x > BX:
                    continue
                zs = (spread[c, (x + 1) // 2], spread[c, (x + 3) // 2]) + sides
                push = weigh([last_sums[c, i, x, 0:rows, 0:lanes] for i in range(6)], [v[0:rows, 0:lanes] for v in zs])
                if c > 0:
                    push = push - 1.2 * (p - down(p, c - 1))[0:rows, 0:lanes]
                elif x % 2 == 0:
                    push = push - 1.2 * (p - spread[3, m - 1])[0:rows, 0:lanes]
                u = base[c, x, 0:rows, 0:lanes] + 0.4 * z[0:rows, 0:lanes] + inv[c, x, 0:rows, 0:lanes] * push
                un[c, x, 0:rows, 0:lanes] = u
                if x < BX:
                    out[c, x] = u[0:BY, 0:BZ]

    for x in range(BX):
        v, w = un[1, x, :, 0:BZ], un[2, x, 0:BY, :]
        flow = un[0, x + 1, 0:BY, 0:BZ] - un[0, x, 0:BY, 0:BZ]
        flow = flow + (up(v, 0) - v)[0:BY] + (up(w, 1) - w)[:, 0:BZ]
        out[3, x] = pbase[x] + spread[3, (x + 2) // 2, 0:BY, 0:BZ] - cells[x] * flow


WIDE, TILE, HUGE = (ROWS, BZ), (BY, BZ), (ROWS, LANES)
HALF = (11, NL, BY, LANES)
FINE_OUT = [(11, NL) + HUGE, (4, NL) + HUGE, (7, 4) + TILE, (MX_DOWN_ROWS, BZ), (MX_UP_ROWS, BZ)]
FINE_SCRATCH = [(11, NL + 4) + TILE, (7, 6) + HUGE, (42,) + WIDE]
LAST_OUT = [(3, 6, 9) + HUGE, (3, 9) + HUGE, (3, 9) + HUGE, (BX,) + TILE, (BX,) + TILE]
COARSE_SCRATCH = [
    (7, ML) + WIDE, (3, 5, ML) + WIDE, (4, ML) + WIDE, (3, ML) + WIDE, (3, ML) + WIDE, (4, 5) + WIDE, (3, 7) + WIDE,
    (4, 5) + WIDE, (4, ML) + WIDE, (24,) + WIDE, (4, 6) + HUGE, (3, 9) + HUGE,
]


def per_device(sizes, iterate, forcing, viscosity):
    nx, ny, nz = (lax.axis_size(a) for a in ("gx", "gy", "gz"))
    at = [lax.axis_index(a) for a in ("gx", "gy", "gz")]
    place = jnp.stack([jnp.full((BY, BZ), a, jnp.int32) for a in at + [at[2] % 2]])

    def swap(a, axis, count, start):
        pairs = []
        for i in range(start, count - 1, 2):
            pairs += [(i, i + 1), (i + 1, i)]
        return lax.ppermute(a, axis, pairs)

    def around(a, axis, count, by):
        return lax.ppermute(a, axis, [(i, (i + by) % count) for i in range(count)])

    def to_next(a, axis, count):
        return lax.ppermute(a, axis, [(i, i + 1) for i in range(count - 1)])

    def to_previous(a, axis, count):
        return lax.ppermute(a, axis, [(i + 1, i) for i in range(count - 1)])

    iterate, forcing, viscosity = (
        pltpu.with_memory_space_constraint(a, pltpu.HBM) for a in (iterate, forcing, viscosity)
    )
    tile = (BY, BZ)
    own, first, second = call(
        pack_z, [(11, BX) + tile, (11,) + tile, (11,) + tile], [pltpu.SemaphoreType.DMA((3,))],
        place, iterate, forcing, viscosity, space=HBM,
    )
    first = swap(first, "gz", nz, 1)
    second = swap(second, "gz", nz, 0)

    upward, downward = call(
        pack_x_early, [(X_UP_EARLY_TILES,) + tile, (X_DOWN_EARLY_TILES,) + tile], [], own
    )
    early = (to_next(upward, "gx", nx), to_previous(downward, "gx", nx))
    upward, downward = call(
        pack_x_late, [(X_UP_LATE_TILES,) + tile, (X_DOWN_LATE_TILES,) + tile], [], place, own, first, second
    )
    halos = (*early, to_next(upward, "gx", nx), to_previous(downward, "gx", nx))

    upward, downward = call(
        pack_y, [(Y_UP_ROWS, BZ), (Y_DOWN_ROWS, BZ)], [], place, own, first, second, *halos
    )
    y_low = around(upward, "gy", ny, 1)
    y_high = around(downward, "gy", ny, -1)
    (half,) = call(assemble_own, [HALF], [], place, own, first, second, *halos)

    whole, fine, middle, downward, upward = call(
        functools.partial(fine_level, sizes), FINE_OUT, FINE_SCRATCH, place, half, y_low, y_high
    )
    x_low = to_next(upward, "gx", nx)
    x_high = to_previous(downward, "gx", nx)

    downward, upward, middle = call(
        pack_y_mid, [(MY_DOWN_ROWS, BZ), (MY_UP_ROWS, BZ), (7, ML, 4, BZ)], [], middle, x_low, x_high
    )
    y_low = around(upward, "gy", ny, 1)
    y_high = around(downward, "gy", ny, -1)

    terms = call(functools.partial(last_terms, sizes), LAST_OUT, [], place, whole, fine)
    (updated,) = call(
        functools.partial(coarse_levels, sizes), [(4, BX) + tile], COARSE_SCRATCH,
        place, *terms, middle, y_low, y_high,
    )
    return updated


def solution(mesh):
    spec = P(None, "gx", "gy", "gz")
    sizes = (mesh.shape["gx"] * BX, mesh.shape["gy"] * BY, mesh.shape["gz"] * BZ)
    return jax.shard_map(
        functools.partial(per_device, sizes), mesh=mesh, in_specs=(spec,) * 3, out_specs=spec, check_vma=False
    )
```

```python
import functools

import jax
import jax.numpy as jnp
from jax import lax
from jax.experimental import pallas as pl
from jax.experimental.pallas import tpu as pltpu
from jax.sharding import PartitionSpec as P

F32 = jnp.float32
BX, BY, BZ = 8, 8, 128
XL, XH = 2, 4
NL = BX + XL + XH
ROWS, LANES = 16, 256
ML = 14
VMEM = pl.BlockSpec(memory_space=pltpu.VMEM)
HBM = pl.BlockSpec(memory_space=pltpu.HBM)
UNROLL = True
PARAMS = pltpu.CompilerParams(vmem_limit_bytes=20 * 1024 * 1024)


def call(kernel, outs, scratch, *args, space=VMEM):
    specs = [VMEM if a.dtype == jnp.int32 else space for a in args]
    return pl.pallas_call(
        kernel,
        out_shape=[jax.ShapeDtypeStruct(s, F32) for s in outs],
        in_specs=specs,
        out_specs=[VMEM] * len(outs),
        scratch_shapes=[pltpu.VMEM(s, F32) if isinstance(s, tuple) else s for s in scratch],
        compiler_params=PARAMS,
    )(*args)


def loop(start, stop, body, carry):
    return lax.fori_loop(start, stop, body, carry, unroll=UNROLL)


def iota(shape, dim):
    return lax.broadcasted_iota(jnp.int32, shape, dim)


def up(a, dim, by=1):
    return pltpu.roll(a, a.shape[dim] - by, dim)


def down(a, dim, by=1):
    return pltpu.roll(a, by, dim)


def lane_roll(a, by):
    by = by % a.shape[1]
    return pltpu.roll(a, by, 1) if by else a


def fine_above(f, dim):
    own = f % 4 == dim and f != 3
    return (3, 2, 3)[f // 4] + own if f % 4 < 3 else (3, 2)[f // 4]


def fine_below(f):
    return 1 if 4 <= f < 8 else 2


def mid_above(f, dim):
    return (4, 5)[f // 4] + (f % 4 == dim and f != 3)


def mid_below(f):
    return (3, 4)[f // 4]


def offsets(entries, unit=8):
    table, at = {}, 0
    for key, rows in entries:
        table[key] = at
        at += rows
    return table, -(-at // unit) * unit


FINE, MID = range(11), range(7)
X_UP = [(f, x) for f in FINE for x in range(BX - fine_below(f), BX)]
X_DOWN = [(f, x) for f in FINE for x in range(fine_above(f, 0))]
EARLY_UP, EARLY_DOWN = 18, 24
FIRST_TILES = 16
X_UP_EARLY, X_UP_EARLY_TILES = offsets([(key, 1) for key in X_UP[:EARLY_UP]], 32)
X_DOWN_EARLY, X_DOWN_EARLY_TILES = offsets([(key, 1) for key in X_DOWN[:EARLY_DOWN]], 32)
X_UP_LATE, X_UP_LATE_TILES = offsets([((f, "z"), 1) for f in FINE] + [(key, 1) for key in X_UP[EARLY_UP:]], 1)
X_DOWN_LATE, X_DOWN_LATE_TILES = offsets([((f, "z"), 1) for f in FINE] + [(key, 1) for key in X_DOWN[EARLY_DOWN:]], 1)
FINE_LAYERS = {
    f: [x + XL for x in range(-fine_below(f), BX + fine_above(f, 0))] + list(range(NL, NL + 4)) for f in FINE
}
Y_UP, Y_UP_ROWS = offsets([((f, l), fine_below(f)) for f in FINE for l in FINE_LAYERS[f]])
Y_DOWN, Y_DOWN_ROWS = offsets([((f, l), fine_above(f, 1)) for f in FINE for l in FINE_LAYERS[f]])
MX_UP, MX_UP_ROWS = offsets([((f, m), mid_above(f, 1)) for f in MID for m in range(4 - mid_below(f), 4)])
MX_DOWN, MX_DOWN_ROWS = offsets([((f, m), mid_above(f, 1)) for f in MID for m in range(mid_above(f, 0))])
MID_LAYERS = {f: [m + 4 for m in range(-mid_below(f), 4 + mid_above(f, 0))] for f in MID}
MY_UP, MY_UP_ROWS = offsets([((f, l), mid_below(f)) for f in MID for l in MID_LAYERS[f]])
MY_DOWN, MY_DOWN_ROWS = offsets([((f, l), mid_above(f, 1)) for f in MID for l in MID_LAYERS[f]])


def pack_z(place, iterate, forcing, viscosity, own, first, second, sems):
    parts = ((iterate, 0, 4), (forcing, 4, 4), (viscosity, 8, 3))
    copies = [
        pltpu.make_async_copy(source, own.at[at : at + count], sems.at[i])
        for i, (source, at, count) in enumerate(parts)
    ]
    for copy in copies:
        copy.start()
    for f in range(11, FIRST_TILES):
        first[f] = jnp.zeros((BY, BZ), F32)
    lane = iota((BY, BZ), 1) // 16
    odd = place[3] == 1
    for copy, (_, at, count) in zip(copies, parts):
        copy.wait()
        for f in range(at, at + count):
            low = jnp.zeros((BY, BZ), F32)
            high = jnp.zeros((BY, BZ), F32)
            for x in range(BX):
                a = own[f, x]
                mine = lane == x
                low = jnp.where(mine, lane_roll(a, 16 * x - 112), low)
                high = jnp.where(mine, lane_roll(a, 16 * x), high)
            first[f] = jnp.where(odd, low, high)
            second[f] = jnp.where(odd, high, low)


def strips(place, first, second, f):
    odd = place[3] == 1
    a, b = first[f], second[f]
    return jnp.where(odd, b, a), jnp.where(odd, a, b)


def fill(message, table, own):
    for key, at in table.items():
        if key[1] != "z":
            message[at] = own[key]
    for at in range(len(table), message.shape[0]):
        message[at] = jnp.zeros((BY, BZ), F32)


def pack_x_early(own, to_up, to_down):
    fill(to_up, X_UP_EARLY, own)
    fill(to_down, X_DOWN_EARLY, own)


def pack_x_late(place, own, first, second, to_up, to_down):
    lane = iota((BY, BZ), 1)
    for f in FINE:
        low, high = strips(place, first, second, f)
        to_up[X_UP_LATE[f, "z"]] = jnp.where(lane >= 96, low, lane_roll(high, -32))
        to_down[X_DOWN_LATE[f, "z"]] = jnp.where(lane < 64, low, lane_roll(high, 64))
    fill(to_up, X_UP_LATE, own)
    fill(to_down, X_DOWN_LATE, own)


def fine_tile(own, halos, f, l):
    x = l - XL
    if 0 <= x < BX:
        return own[f, x]
    low_early, high_early, low_late, high_late = halos
    key = (f, BX + x) if x < 0 else (f, x - BX)
    early, late = (low_early, low_late) if x < 0 else (high_early, high_late)
    table, rest = (X_UP_EARLY, X_UP_LATE) if x < 0 else (X_DOWN_EARLY, X_DOWN_LATE)
    if key in table:
        return early[table[key]]
    return late[rest[key]] if key in rest else None


def strip_tiles(place, first, second, halos, f):
    low, high = strips(place, first, second, f)
    return [low, high, halos[2][X_UP_LATE[f, "z"]], halos[3][X_DOWN_LATE[f, "z"]]]


def pack_y(place, own, first, second, low_early, high_early, low_late, high_late, to_up, to_down):
    halos = (low_early, high_early, low_late, high_late)
    for f in FINE:
        sides = strip_tiles(place, first, second, halos, f)
        below, above = fine_below(f), fine_above(f, 1)
        for l in FINE_LAYERS[f]:
            tile = sides[l - NL] if l >= NL else fine_tile(own, halos, f, l)
            at = Y_UP[f, l]
            to_up[at : at + below] = tile[BY - below :, :]
            at = Y_DOWN[f, l]
            to_down[at : at + above] = tile[:above, :]


def widen(tile, rows, lanes):
    tile = jnp.concatenate([tile] * (rows // BY), axis=0) if rows > BY else tile
    return jnp.concatenate([tile] * (lanes // BZ), axis=1) if lanes > BZ else tile


def inside_yz(place, rows, lanes, ny, nz, end_y, low_y, end_z, low_z, by, bz):
    y = iota((rows, lanes), 0)
    z = iota((rows, lanes), 1)
    held = ((y < end_y) | (y >= rows - low_y)) & ((z < end_z) | (z >= lanes - low_z))
    y = jnp.where(y < end_y, y, y - rows) + widen(place[1] * by, rows, lanes)
    z = jnp.where(z < end_z, z, z - lanes) + widen(place[2] * bz, rows, lanes)
    return jnp.where(held & (y >= 0) & (y < ny) & (z >= 0) & (z < nz), 1, 0)


def inside(yz, x, nx):
    ok = jnp.where((x >= 0) & (x < nx), 1, 0)
    return (yz * widen(ok, *yz.shape)) != 0


def neighbours(low, mid, high, by=1):
    return (low, high, down(mid, 0, by), up(mid, 0, by), down(mid, 1, by), up(mid, 1, by))


def total(values):
    out = values[0]
    for v in values[1:]:
        out = out + v
    return out


def couple(e, es, vs):
    return e * total(vs) + total([a * b for a, b in zip(es, vs)])


def fine_mask_args(place, sizes):
    return inside_yz(place, ROWS, LANES, sizes[1], sizes[2], BY + XH, XL, BZ + 16, 16, BY, BZ)


def compact_matrix():
    a = iota((LANES, BZ), 0) // 2
    return jnp.where(a == iota((LANES, BZ), 1), 0.125, 0.0).astype(jnp.bfloat16)


def spread_matrix():
    a = iota((BZ, LANES), 1) // 2
    return jnp.where(a == iota((BZ, LANES), 0), 1.0, 0.0).astype(jnp.bfloat16)


def exact_dot(a, matrix):
    high = a.astype(jnp.bfloat16)
    rest = a - high.astype(F32)
    mid = rest.astype(jnp.bfloat16)
    low = (rest - mid.astype(F32)).astype(jnp.bfloat16)
    dot = functools.partial(jnp.dot, preferred_element_type=F32)
    return dot(high, matrix) + (dot(mid, matrix) + dot(low, matrix))


def kept(place, sizes):
    low = jnp.where(place[1] > 0, 1.0, 0.0)
    high = jnp.where(place[1] < sizes[1] // BY - 1, 1.0, 0.0)
    return low, high


def side_lanes(l, tiles):
    lane = iota((BY, BZ), 1)
    x = l - XL
    if x < 0:
        a, b = lane_roll(tiles[2], 16 - 16 * l), lane_roll(tiles[2], -(64 + 16 * l))
    elif x < BX:
        a, b = lane_roll(tiles[0], 112 - 16 * x), lane_roll(tiles[1], -16 * x)
    else:
        a, b = lane_roll(tiles[3], 112 - 16 * (x - BX)), lane_roll(tiles[3], -(64 + 16 * (x - BX)))
    return jnp.where(lane >= 112, a, jnp.where(lane < 16, b, 0.0))


def assemble_own(place, own, first, second, low_early, high_early, low_late, high_late, half):
    halos = (low_early, high_early, low_late, high_late)
    for f in FINE:
        sides = strip_tiles(place, first, second, halos, f)
        for l in range(NL):
            body = fine_tile(own, halos, f, l)
            half[f, l, :, 0:BZ] = jnp.zeros((BY, BZ), F32) if body is None else body
            half[f, l, :, BZ:] = side_lanes(l, sides)


def pair_sums(e, high):
    return e + high, e + down(e, 0), e + up(e, 0), e + down(e, 1), e + up(e, 1)


def weigh(weights, values):
    return total([a * b for a, b in zip(weights, values)])


def fine_level(sizes, place, half, y_low, y_high, whole, full, middle, to_down, to_up, rows, rsum, tsum):
    keep_low, keep_high = kept(place, sizes)

    for f in FINE:
        below, above = fine_below(f), fine_above(f, 1)
        for l in FINE_LAYERS[f]:
            rows[f, l] = jnp.zeros((BY, BZ), F32)
            at = Y_DOWN[f, l]
            rows[f, l, 0:above] = y_high[at : at + above] * keep_high[:above]
            at = Y_UP[f, l]
            rows[f, l, BY - below :] = y_low[at : at + below] * keep_low[:below]
        sides = [rows[f, NL + i] for i in range(4)]
        for l in range(NL):
            whole[f, l, 0:BY] = half[f, l]
            whole[f, l, BY:, 0:BZ] = rows[f, l] if l in FINE_LAYERS[f] else jnp.zeros((BY, BZ), F32)
            whole[f, l, BY:, BZ:] = side_lanes(l, sides)

    def grid(f, l):
        return whole[f, l]

    yz = fine_mask_args(place, sizes)
    for i in range(4):
        full[i, 0] = jnp.zeros((ROWS, LANES), F32)
        full[i, NL - 1] = jnp.zeros((ROWS, LANES), F32)
    full[3, NL - 2] = jnp.zeros((ROWS, LANES), F32)

    def weights(c, l):
        e = grid(8 + c, l)
        return (e + grid(8 + c, l - 1),) + pair_sums(e, grid(8 + c, l + 1))

    def velocities(l, carry):
        good = inside(yz, place[0] * BX + l - XL, sizes[0])
        p = grid(3, l)
        for c in range(3):
            u = grid(c, l)
            us = neighbours(grid(c, l - 1), u, grid(c, l + 1))
            ks = weights(c, l)
            before = grid(3, l - 1) if c == 0 else down(p, c - 1)
            push = 1.2 * (grid(4 + c, l) - (p - before)) + 0.6 * weigh(ks, us)
            full[c, l] = jnp.where(good, 0.4 * u + push / total(ks), 0.0)
        return carry

    loop(1, NL - 1, velocities, 0)

    def outflow(l):
        v, w = full[1, l], full[2, l]
        return (full[0, l + 1] - full[0, l]) + (up(v, 0) - v) + (up(w, 1) - w)

    def pressures(l, carry):
        good = inside(yz, place[0] * BX + l - XL, sizes[0])
        ev, ew = grid(9, l), grid(10, l)
        cell = (grid(8, l) + grid(8, l + 1)) + (ev + up(ev, 0)) + (ew + up(ew, 1))
        full[3, l] = jnp.where(good, grid(3, l) - (0.5 / 6.0) * cell * (grid(7, l) + outflow(l)), 0.0)
        return carry

    loop(1, NL - 2, pressures, 0)

    def layer_residual(c, l):
        u = full[c, l]
        us = neighbours(full[c, l - 1], u, full[c, l + 1])
        ks = weights(c, l)
        p = full[3, l]
        before = full[3, l - 1] if c == 0 else down(p, c - 1)
        return grid(4 + c, l) - (p - before) - 0.5 * (total(ks) * u - weigh(ks, us))

    def residuals(m, carry):
        l = XL + 2 * m
        for c in range(3):
            rsum[c, m] = layer_residual(c, l) + layer_residual(c, l + 1)
        rsum[3, m] = (grid(7, l) + outflow(l)) + (grid(7, l + 1) + outflow(l + 1))
        return carry

    loop(0, 5, residuals, 0)
    for i in range(4):
        rsum[i, 5] = jnp.zeros((ROWS, LANES), F32)
    for c in range(3):
        for m in range(6):
            rsum[4 + c, m] = grid(8 + c, XL + 2 * m) + grid(8 + c, XL + 2 * m + 1)

    matrix = compact_matrix()
    for f in range(7):
        tsum[6 * f : 6 * f + 6] = exact_dot(rsum[f].reshape(6 * ROWS, LANES), matrix).reshape(6, ROWS, BZ)
    for f in MID:
        rows_sent = mid_above(f, 1)
        for m in range(mid_above(f, 0)):
            i = 6 * f + m
            a = tsum[i, pl.ds(0, 8, stride=2), :] + tsum[i, pl.ds(1, 8, stride=2), :]
            at = MX_DOWN[f, m]
            to_down[at : at + rows_sent] = a[:rows_sent]
            if m < 4:
                middle[f, m] = a
            if (f, m) in MX_UP:
                at = MX_UP[f, m]
                to_up[at : at + rows_sent] = a[:rows_sent]


def sizes_of(c):
    return (ROWS if c == 1 else BY), (LANES if c == 2 else BZ)


def last_terms(sizes, place, whole, fine, sums, base, inv, cells, pbase):
    fyz = fine_mask_args(place, sizes)

    def grid(f, l):
        return whole[f, l]

    for x in range(9):
        l = x + XL
        good = inside(fyz, place[0] * BX + x, sizes[0])
        p = fine[3, l]
        for c in range(3):
            u, e = fine[c, l], grid(8 + c, l)
            us = neighbours(fine[c, l - 1], u, fine[c, l + 1])
            xp, ym, yp, zm, zp = pair_sums(e, grid(8 + c, l + 1))
            ks = (e + grid(8 + c, l - 1), xp, ym, yp, zm, zp)
            before = fine[3, l - 1] if c == 0 else down(p, c - 1)
            push = 1.2 * (grid(4 + c, l) - (p - before)) + 0.6 * weigh(ks, us)
            over = 1.0 / total(ks)
            rows, lanes = sizes_of(c)
            for i, k in enumerate(ks):
                sums[c, i, x, 0:rows, 0:lanes] = (0.6 * k)[0:rows, 0:lanes]
            base[c, x, 0:rows, 0:lanes] = jnp.where(good, 0.4 * u + push * over, 0.0)[0:rows, 0:lanes]
            inv[c, x, 0:rows, 0:lanes] = jnp.where(good, over, 0.0)[0:rows, 0:lanes]
            if x < BX and c == 0:
                cell = e + grid(8, l + 1)
            elif x < BX:
                cell = cell + (yp if c == 1 else zp)
        if x < BX:
            cell = (0.5 / 6.0) * cell
            cells[x] = cell[0:BY, 0:BZ]
            pbase[x] = (p - cell * grid(7, l))[0:BY, 0:BZ]


def pack_y_mid(own, from_low, from_high, to_down, to_up, rows):
    for f in MID:
        below, above = mid_below(f), mid_above(f, 1)
        for l in range(ML):
            if l not in MID_LAYERS[f]:
                rows[f, l] = jnp.zeros((4, BZ), F32)
                continue
            m = l - 4
            if m < 0:
                at = MX_UP[f, 4 + m]
                tile = from_low[at : at + above]
            elif m < 4:
                tile = own[f, m, 0:above]
            else:
                at = MX_DOWN[f, m - 4]
                tile = from_high[at : at + above]
            at = MY_DOWN[f, l]
            to_down[at : at + above] = tile
            at = MY_UP[f, l]
            to_up[at : at + below] = tile[4 - below : 4]
            rows[f, l] = tile[0:4]


def coarse_levels(
    sizes, place, last_sums, base, inv, cells, pbase, own, y_low, y_high, out,
    mid, sums, um, over, dm, f2, e2, low, sm, twice, spread, un,
):
    keep_low, keep_high = kept(place, sizes)
    for f in MID:
        below, above = mid_below(f), mid_above(f, 1)
        for l in range(ML):
            mid[f, l] = jnp.zeros((ROWS, BZ), F32)
            mid[f, l, 0:4] = own[f, l]
            if l in MID_LAYERS[f]:
                at = MY_DOWN[f, l]
                mid[f, l, 4 : 4 + above] = y_high[at : at + above] * keep_high[:above]
                at = MY_UP[f, l]
                mid[f, l, ROWS - below :] = y_low[at : at + below] * keep_low[:below]

    shape = (ROWS, BZ)
    yz = inside_yz(place, ROWS, BZ, sizes[1] // 2, sizes[2] // 2, 10, 4, BZ // 2 + 8, 8, BY // 2, BZ // 2)
    row_even = iota(shape, 0) % 2 == 0
    lane_even = iota(shape, 1) % 2 == 0

    def mid_inside(l):
        return inside(yz, place[0] * (BX // 2) + l - 4, sizes[0] // 2)

    for c in range(3):
        sums[c, 0, 1] = mid[4 + c, 0] + mid[4 + c, 1]

    def first_velocities(l, carry):
        good = mid_inside(l)
        for c in range(3):
            xp, ym, yp, zm, zp = pair_sums(mid[4 + c, l], mid[4 + c, l + 1])
            diag = total([sums[c, 0, l], xp, ym, yp, zm, zp])
            sums[c, 0, l + 1] = xp
            sums[c, 1, l] = ym
            sums[c, 2, l] = yp
            sums[c, 3, l] = zm
            sums[c, 4, l] = zp
            dm[c, l] = diag
            inverse = 1.0 / diag
            over[c, l] = inverse
            um[c, l] = jnp.where(good, 4.8 * mid[c, l] * inverse, 0.0)
        return carry

    loop(1, 13, first_velocities, 0)

    def weights(c, l):
        return (sums[c, 0, l], sums[c, 0, l + 1]) + tuple(sums[c, i, l] for i in range(1, 5))

    def outflow(v, l):
        b, w = v[1, l], v[2, l]
        return (v[0, l + 1] - v[0, l]) + (up(b, 0) - b) + (up(w, 1) - w)

    def mid_cell(l):
        return sums[0, 0, l + 1] + sums[1, 2, l] + sums[2, 4, l]

    def first_pressures(l, carry):
        q = mid[3, l] + 0.5 * outflow(um, l)
        um[3, l] = jnp.where(mid_inside(l), (-0.5 / 6.0) * mid_cell(l) * q, 0.0)
        return carry

    loop(1, 12, first_pressures, 0)

    def expand(a):
        a = a + up(a, 0)
        a = jnp.where(row_even, a, down(a, 0))
        a = a + up(a, 1)
        return 0.125 * jnp.where(lane_even, a, down(a, 1))

    def layer_residual(c, l):
        u = um[c, l]
        us = neighbours(um[c, l - 1], u, um[c, l + 1])
        p = um[3, l]
        before = um[3, l - 1] if c == 0 else down(p, c - 1)
        return mid[c, l] - 0.5 * (p - before) - 0.125 * (dm[c, l] * u - weigh(weights(c, l), us))

    def residuals(k, carry):
        l = 2 + 2 * k
        for c in range(3):
            f2[c, k] = expand(layer_residual(c, l) + layer_residual(c, l + 1))
        f2[3, k] = expand((mid[3, l] + 0.5 * outflow(um, l)) + (mid[3, l + 1] + 0.5 * outflow(um, l + 1)))
        return carry

    loop(0, 5, residuals, 0)

    def low_viscosity(k, carry):
        for c in range(3):
            e2[c, k] = expand(mid[4 + c, 2 * k] + mid[4 + c, 2 * k + 1])
        return carry

    loop(0, 7, low_viscosity, 0)

    def low_inside(k):
        return inside(yz, place[0] * (BX // 4) + k - 1, sizes[0] // 4)

    def low_velocities(k, carry):
        good = low_inside(k)
        for c in range(3):
            e = e2[c, k + 1]
            diag = 6.0 * e + total(neighbours(e2[c, k], e, e2[c, k + 2], 2))
            low[c, k] = jnp.where(good, 19.2 * f2[c, k] / diag, 0.0)
        return carry

    loop(0, 5, low_velocities, 0)

    def low_pressures(k, carry):
        v, w, ev, ew = low[1, k], low[2, k], e2[1, k + 1], e2[2, k + 1]
        flow = (low[0, k + 1] - low[0, k]) + (up(v, 0, 2) - v) + (up(w, 1, 2) - w)
        cell = (e2[0, k + 1] + e2[0, k + 2]) + (ev + up(ev, 0, 2)) + (ew + up(ew, 1, 2))
        low[3, k] = jnp.where(low_inside(k), (-0.5 / 6.0) * cell * (f2[3, k] + 0.25 * flow), 0.0)
        return carry

    loop(0, 4, low_pressures, 0)

    def corrected(k, carry):
        for i in range(3):
            um[i, 2 * k + 2] = um[i, 2 * k + 2] + low[i, k]
            um[i, 2 * k + 3] = um[i, 2 * k + 3] + low[i, k]
        return carry

    loop(0, 5, corrected, 0)
    for k in range(4):
        um[3, 2 * k + 2] = um[3, 2 * k + 2] + low[3, k]
        um[3, 2 * k + 3] = um[3, 2 * k + 3] + low[3, k]

    def second_velocities(l, carry):
        good = mid_inside(l)
        p = um[3, l]
        for c in range(3):
            u = um[c, l]
            us = neighbours(um[c, l - 1], u, um[c, l + 1])
            before = um[3, l - 1] if c == 0 else down(p, c - 1)
            push = 4.8 * (mid[c, l] - 0.5 * (p - before)) + 0.6 * weigh(weights(c, l), us)
            sm[c, l] = jnp.where(good, 0.4 * u + push * over[c, l], 0.0)
        return carry

    loop(3, 10, second_velocities, 0)

    def second_pressures(l, carry):
        q = mid[3, l] + 0.5 * outflow(sm, l)
        sm[3, l] = jnp.where(mid_inside(l), um[3, l] - (0.5 / 6.0) * mid_cell(l) * q, 0.0)
        return carry

    loop(3, 9, second_pressures, 0)

    last_row = iota((8, BZ), 0) == 7
    for i in range(4):
        for m in range(6):
            a = sm[i, 3 + m]
            a = jnp.where(last_row, a[8:16], a[0:8])
            twice[6 * i + m, pl.ds(0, 8, stride=2), :] = a
            twice[6 * i + m, pl.ds(1, 8, stride=2), :] = a
    matrix = spread_matrix()
    for i in range(4):
        wide = exact_dot(twice[6 * i : 6 * i + 6].reshape(6 * ROWS, BZ), matrix)
        spread[i] = wide.reshape(6, ROWS, LANES)

    for m in range(1, 6):
        p = spread[3, m]
        for c in range(3):
            rows, lanes = sizes_of(c)
            z = spread[c, m]
            sides = (down(z, 0), up(z, 0), down(z, 1), up(z, 1))
            for x in (2 * m - 2, 2 * m - 1):
                if x > BX:
                    continue
                zs = (spread[c, (x + 1) // 2], spread[c, (x + 3) // 2]) + sides
                push = weigh([last_sums[c, i, x, 0:rows, 0:lanes] for i in range(6)], [v[0:rows, 0:lanes] for v in zs])
                if c > 0:
                    push = push - 1.2 * (p - down(p, c - 1))[0:rows, 0:lanes]
                elif x % 2 == 0:
                    push = push - 1.2 * (p - spread[3, m - 1])[0:rows, 0:lanes]
                u = base[c, x, 0:rows, 0:lanes] + 0.4 * z[0:rows, 0:lanes] + inv[c, x, 0:rows, 0:lanes] * push
                un[c, x, 0:rows, 0:lanes] = u
                if x < BX:
                    out[c, x] = u[0:BY, 0:BZ]

    for x in range(BX):
        v, w = un[1, x, :, 0:BZ], un[2, x, 0:BY, :]
        flow = un[0, x + 1, 0:BY, 0:BZ] - un[0, x, 0:BY, 0:BZ]
        flow = flow + (up(v, 0) - v)[0:BY] + (up(w, 1) - w)[:, 0:BZ]
        out[3, x] = pbase[x] + spread[3, (x + 2) // 2, 0:BY, 0:BZ] - cells[x] * flow


WIDE, TILE, HUGE = (ROWS, BZ), (BY, BZ), (ROWS, LANES)
HALF = (11, NL, BY, LANES)
FINE_OUT = [(11, NL) + HUGE, (4, NL) + HUGE, (7, 4) + TILE, (MX_DOWN_ROWS, BZ), (MX_UP_ROWS, BZ)]
FINE_SCRATCH = [(11, NL + 4) + TILE, (7, 6) + HUGE, (42,) + WIDE]
LAST_OUT = [(3, 6, 9) + HUGE, (3, 9) + HUGE, (3, 9) + HUGE, (BX,) + TILE, (BX,) + TILE]
COARSE_SCRATCH = [
    (7, ML) + WIDE, (3, 5, ML) + WIDE, (4, ML) + WIDE, (3, ML) + WIDE, (3, ML) + WIDE, (4, 5) + WIDE, (3, 7) + WIDE,
    (4, 5) + WIDE, (4, ML) + WIDE, (24,) + WIDE, (4, 6) + HUGE, (3, 9) + HUGE,
]


def per_device(sizes, iterate, forcing, viscosity):
    nx, ny, nz = (lax.axis_size(a) for a in ("gx", "gy", "gz"))
    at = [lax.axis_index(a) for a in ("gx", "gy", "gz")]
    place = jnp.stack([jnp.full((BY, BZ), a, jnp.int32) for a in at + [at[2] % 2]])

    def swap(a, axis, count, start):
        pairs = []
        for i in range(start, count - 1, 2):
            pairs += [(i, i + 1), (i + 1, i)]
        return lax.ppermute(a, axis, pairs)

    def around(a, axis, count, by):
        return lax.ppermute(a, axis, [(i, (i + by) % count) for i in range(count)])

    def to_next(a, axis, count):
        return lax.ppermute(a, axis, [(i, i + 1) for i in range(count - 1)])

    def to_previous(a, axis, count):
        return lax.ppermute(a, axis, [(i + 1, i) for i in range(count - 1)])

    iterate, forcing, viscosity = (
        pltpu.with_memory_space_constraint(a, pltpu.HBM) for a in (iterate, forcing, viscosity)
    )
    tile = (BY, BZ)
    own, first, second = call(
        pack_z, [(11, BX) + tile, (FIRST_TILES,) + tile, (11,) + tile], [pltpu.SemaphoreType.DMA((3,))],
        place, iterate, forcing, viscosity, space=HBM,
    )
    first = swap(first, "gz", nz, 1)
    second = swap(second, "gz", nz, 0)

    upward, downward = call(
        pack_x_early, [(X_UP_EARLY_TILES,) + tile, (X_DOWN_EARLY_TILES,) + tile], [], own
    )
    early = (to_next(upward, "gx", nx), to_previous(downward, "gx", nx))
    upward, downward = call(
        pack_x_late, [(X_UP_LATE_TILES,) + tile, (X_DOWN_LATE_TILES,) + tile], [], place, own, first, second
    )
    halos = (*early, to_next(upward, "gx", nx), to_previous(downward, "gx", nx))

    upward, downward = call(
        pack_y, [(Y_UP_ROWS, BZ), (Y_DOWN_ROWS, BZ)], [], place, own, first, second, *halos
    )
    y_low = around(upward, "gy", ny, 1)
    y_high = around(downward, "gy", ny, -1)
    (half,) = call(assemble_own, [HALF], [], place, own, first, second, *halos)

    whole, fine, middle, downward, upward = call(
        functools.partial(fine_level, sizes), FINE_OUT, FINE_SCRATCH, place, half, y_low, y_high
    )
    x_low = to_next(upward, "gx", nx)
    x_high = to_previous(downward, "gx", nx)

    downward, upward, middle = call(
        pack_y_mid, [(MY_DOWN_ROWS, BZ), (MY_UP_ROWS, BZ), (7, ML, 4, BZ)], [], middle, x_low, x_high
    )
    y_low = around(upward, "gy", ny, 1)
    y_high = around(downward, "gy", ny, -1)

    terms = call(functools.partial(last_terms, sizes), LAST_OUT, [], place, whole, fine)
    (updated,) = call(
        functools.partial(coarse_levels, sizes), [(4, BX) + tile], COARSE_SCRATCH,
        place, *terms, middle, y_low, y_high,
    )
    return updated


def solution(mesh):
    spec = P(None, "gx", "gy", "gz")
    sizes = (mesh.shape["gx"] * BX, mesh.shape["gy"] * BY, mesh.shape["gz"] * BZ)
    return jax.shard_map(
        functools.partial(per_device, sizes), mesh=mesh, in_specs=(spec,) * 3, out_specs=spec, check_vma=False
    )
```

```python
import functools

import jax
import jax.numpy as jnp
from jax import lax
from jax.experimental import pallas as pl
from jax.experimental.pallas import tpu as pltpu
from jax.sharding import PartitionSpec as P

F32 = jnp.float32
BX, BY, BZ = 8, 8, 128
XL, XH = 2, 4
NL = BX + XL + XH
ROWS, LANES = 16, 256
ML = 14
VMEM = pl.BlockSpec(memory_space=pltpu.VMEM)
HBM = pl.BlockSpec(memory_space=pltpu.HBM)
UNROLL = True
PARAMS = pltpu.CompilerParams(vmem_limit_bytes=20 * 1024 * 1024)


def call(kernel, outs, scratch, *args, space=VMEM):
    specs = [VMEM if a.dtype == jnp.int32 else space for a in args]
    return pl.pallas_call(
        kernel,
        out_shape=[jax.ShapeDtypeStruct(s, F32) for s in outs],
        in_specs=specs,
        out_specs=[VMEM] * len(outs),
        scratch_shapes=[pltpu.VMEM(s, F32) if isinstance(s, tuple) else s for s in scratch],
        compiler_params=PARAMS,
    )(*args)


def loop(start, stop, body, carry):
    return lax.fori_loop(start, stop, body, carry, unroll=UNROLL)


def iota(shape, dim):
    return lax.broadcasted_iota(jnp.int32, shape, dim)


def up(a, dim, by=1):
    return pltpu.roll(a, a.shape[dim] - by, dim)


def down(a, dim, by=1):
    return pltpu.roll(a, by, dim)


def lane_roll(a, by):
    by = by % a.shape[1]
    return pltpu.roll(a, by, 1) if by else a


def fine_above(f, dim):
    own = f % 4 == dim and f != 3
    return (3, 2, 3)[f // 4] + own if f % 4 < 3 else (3, 2)[f // 4]


def fine_below(f):
    return 1 if 4 <= f < 8 else 2


def mid_above(f, dim):
    return (4, 5)[f // 4] + (f % 4 == dim and f != 3)


def mid_below(f):
    return (3, 4)[f // 4]


def offsets(entries):
    table, at = {}, 0
    for key, rows in entries:
        table[key] = at
        at += rows
    return table, -(-at // 8) * 8


FINE, MID = range(11), range(7)
X_UP, X_UP_TILES = offsets(
    [((f, x), 1) for f in FINE for x in range(BX - fine_below(f), BX)] + [((f, "z"), 1) for f in FINE]
)
X_DOWN, X_DOWN_TILES = offsets(
    [((f, x), 1) for f in FINE for x in range(fine_above(f, 0))] + [((f, "z"), 1) for f in FINE]
)
FINE_LAYERS = {
    f: [x + XL for x in range(-fine_below(f), BX + fine_above(f, 0))] + list(range(NL, NL + 4)) for f in FINE
}
Y_UP, Y_UP_ROWS = offsets([((f, l), fine_below(f)) for f in FINE for l in FINE_LAYERS[f]])
Y_DOWN, Y_DOWN_ROWS = offsets([((f, l), fine_above(f, 1)) for f in FINE for l in FINE_LAYERS[f]])
MX_UP, MX_UP_ROWS = offsets([((f, m), mid_above(f, 1)) for f in MID for m in range(4 - mid_below(f), 4)])
MX_DOWN, MX_DOWN_ROWS = offsets([((f, m), mid_above(f, 1)) for f in MID for m in range(mid_above(f, 0))])
MID_LAYERS = {f: [m + 4 for m in range(-mid_below(f), 4 + mid_above(f, 0))] for f in MID}
MY_UP, MY_UP_ROWS = offsets([((f, l), mid_below(f)) for f in MID for l in MID_LAYERS[f]])
MY_DOWN, MY_DOWN_ROWS = offsets([((f, l), mid_above(f, 1)) for f in MID for l in MID_LAYERS[f]])


NEAR_TILES = 16


def pack_z(place, iterate, forcing, viscosity, own, first, second, sems):
    parts = ((iterate, 0, 4), (forcing, 4, 4), (viscosity, 8, 3))
    copies = [
        pltpu.make_async_copy(source, own.at[at : at + count], sems.at[i])
        for i, (source, at, count) in enumerate(parts)
    ]
    for copy in copies:
        copy.start()
    lane = iota((BY, BZ), 1) // 16
    for f in range(11, NEAR_TILES):
        second[f] = jnp.zeros((BY, BZ), F32)
    odd = place[3] == 1
    for copy, (_, at, count) in zip(copies, parts):
        copy.wait()
        for f in range(at, at + count):
            low = jnp.zeros((BY, BZ), F32)
            high = jnp.zeros((BY, BZ), F32)
            for x in range(BX):
                a = own[f, x]
                mine = lane == x
                low = jnp.where(mine, lane_roll(a, 16 * x - 112), low)
                high = jnp.where(mine, lane_roll(a, 16 * x), high)
            first[f] = jnp.where(odd, low, high)
            second[f] = jnp.where(odd, high, low)


def strips(place, first, second, f):
    odd = place[3] == 1
    a, b = first[f], second[f]
    return jnp.where(odd, b, a), jnp.where(odd, a, b)


def pack_x(place, own, first, second, to_up, to_down):
    lane = iota((BY, BZ), 1)
    for f in FINE:
        low, high = strips(place, first, second, f)
        to_up[X_UP[f, "z"]] = jnp.where(lane >= 96, low, lane_roll(high, -32))
        to_down[X_DOWN[f, "z"]] = jnp.where(lane < 64, low, lane_roll(high, 64))
        for x in range(BX - fine_below(f), BX):
            to_up[X_UP[f, x]] = own[f, x]
        for x in range(fine_above(f, 0)):
            to_down[X_DOWN[f, x]] = own[f, x]


def fine_tile(own, from_low, from_high, f, l):
    x = l - XL
    if 0 <= x < BX:
        return own[f, x]
    if x < 0:
        return from_low[X_UP[f, BX + x]] if -x <= fine_below(f) else None
    return from_high[X_DOWN[f, x - BX]] if x - BX < fine_above(f, 0) else None


def strip_tiles(place, first, second, from_low, from_high, f):
    low, high = strips(place, first, second, f)
    return [low, high, from_low[X_UP[f, "z"]], from_high[X_DOWN[f, "z"]]]


def pack_y(place, own, first, second, from_low, from_high, to_up, to_down):
    for f in FINE:
        sides = strip_tiles(place, first, second, from_low, from_high, f)
        below, above = fine_below(f), fine_above(f, 1)
        for l in FINE_LAYERS[f]:
            tile = sides[l - NL] if l >= NL else fine_tile(own, from_low, from_high, f, l)
            at = Y_UP[f, l]
            to_up[at : at + below] = tile[BY - below :, :]
            at = Y_DOWN[f, l]
            to_down[at : at + above] = tile[:above, :]


def widen(tile, rows, lanes):
    tile = jnp.concatenate([tile] * (rows // BY), axis=0) if rows > BY else tile
    return jnp.concatenate([tile] * (lanes // BZ), axis=1) if lanes > BZ else tile


def inside_yz(place, rows, lanes, ny, nz, end_y, low_y, end_z, low_z, by, bz):
    y = iota((rows, lanes), 0)
    z = iota((rows, lanes), 1)
    held = ((y < end_y) | (y >= rows - low_y)) & ((z < end_z) | (z >= lanes - low_z))
    y = jnp.where(y < end_y, y, y - rows) + widen(place[1] * by, rows, lanes)
    z = jnp.where(z < end_z, z, z - lanes) + widen(place[2] * bz, rows, lanes)
    return jnp.where(held & (y >= 0) & (y < ny) & (z >= 0) & (z < nz), 1, 0)


def inside(yz, x, nx):
    ok = jnp.where((x >= 0) & (x < nx), 1, 0)
    return (yz * widen(ok, *yz.shape)) != 0


def neighbours(low, mid, high, by=1):
    return (low, high, down(mid, 0, by), up(mid, 0, by), down(mid, 1, by), up(mid, 1, by))


def total(values):
    out = values[0]
    for v in values[1:]:
        out = out + v
    return out


def couple(e, es, vs):
    return e * total(vs) + total([a * b for a, b in zip(es, vs)])


def fine_mask_args(place, sizes):
    return inside_yz(place, ROWS, LANES, sizes[1], sizes[2], BY + XH, XL, BZ + 16, 16, BY, BZ)


def compact_matrix():
    a = iota((LANES, BZ), 0) // 2
    return jnp.where(a == iota((LANES, BZ), 1), 0.125, 0.0).astype(jnp.bfloat16)


def spread_matrix():
    a = iota((BZ, LANES), 1) // 2
    return jnp.where(a == iota((BZ, LANES), 0), 1.0, 0.0).astype(jnp.bfloat16)


def exact_dot(a, matrix):
    high = a.astype(jnp.bfloat16)
    rest = a - high.astype(F32)
    mid = rest.astype(jnp.bfloat16)
    low = (rest - mid.astype(F32)).astype(jnp.bfloat16)
    dot = functools.partial(jnp.dot, preferred_element_type=F32)
    return dot(high, matrix) + (dot(mid, matrix) + dot(low, matrix))


def kept(place, sizes):
    low = jnp.where(place[1] > 0, 1.0, 0.0)
    high = jnp.where(place[1] < sizes[1] // BY - 1, 1.0, 0.0)
    return low, high


def side_lanes(l, tiles):
    lane = iota((BY, BZ), 1)
    x = l - XL
    if x < 0:
        a, b = lane_roll(tiles[2], 16 - 16 * l), lane_roll(tiles[2], -(64 + 16 * l))
    elif x < BX:
        a, b = lane_roll(tiles[0], 112 - 16 * x), lane_roll(tiles[1], -16 * x)
    else:
        a, b = lane_roll(tiles[3], 112 - 16 * (x - BX)), lane_roll(tiles[3], -(64 + 16 * (x - BX)))
    return jnp.where(lane >= 112, a, jnp.where(lane < 16, b, 0.0))


def assemble_own(place, own, first, second, from_low, from_high, half):
    for f in FINE:
        sides = strip_tiles(place, first, second, from_low, from_high, f)
        for l in range(NL):
            body = fine_tile(own, from_low, from_high, f, l)
            half[f, l, :, 0:BZ] = jnp.zeros((BY, BZ), F32) if body is None else body
            half[f, l, :, BZ:] = side_lanes(l, sides)


def pair_sums(e, high):
    return e + high, e + down(e, 0), e + up(e, 0), e + down(e, 1), e + up(e, 1)


def weigh(weights, values):
    return total([a * b for a, b in zip(weights, values)])


def fine_level(sizes, place, half, y_low, y_high, whole, full, middle, to_down, to_up, rows, rsum, tsum):
    keep_low, keep_high = kept(place, sizes)

    for f in FINE:
        below, above = fine_below(f), fine_above(f, 1)
        for l in FINE_LAYERS[f]:
            rows[f, l] = jnp.zeros((BY, BZ), F32)
            at = Y_DOWN[f, l]
            rows[f, l, 0:above] = y_high[at : at + above] * keep_high[:above]
            at = Y_UP[f, l]
            rows[f, l, BY - below :] = y_low[at : at + below] * keep_low[:below]
        sides = [rows[f, NL + i] for i in range(4)]
        for l in range(NL):
            whole[f, l, 0:BY] = half[f, l]
            whole[f, l, BY:, 0:BZ] = rows[f, l] if l in FINE_LAYERS[f] else jnp.zeros((BY, BZ), F32)
            whole[f, l, BY:, BZ:] = side_lanes(l, sides)

    def grid(f, l):
        return whole[f, l]

    yz = fine_mask_args(place, sizes)
    for i in range(4):
        full[i, 0] = jnp.zeros((ROWS, LANES), F32)
        full[i, NL - 1] = jnp.zeros((ROWS, LANES), F32)
    full[3, NL - 2] = jnp.zeros((ROWS, LANES), F32)

    def weights(c, l):
        e = grid(8 + c, l)
        return (e + grid(8 + c, l - 1),) + pair_sums(e, grid(8 + c, l + 1))

    def velocities(l, carry):
        good = inside(yz, place[0] * BX + l - XL, sizes[0])
        p = grid(3, l)
        for c in range(3):
            u = grid(c, l)
            us = neighbours(grid(c, l - 1), u, grid(c, l + 1))
            ks = weights(c, l)
            before = grid(3, l - 1) if c == 0 else down(p, c - 1)
            push = 1.2 * (grid(4 + c, l) - (p - before)) + 0.6 * weigh(ks, us)
            full[c, l] = jnp.where(good, 0.4 * u + push / total(ks), 0.0)
        return carry

    loop(1, NL - 1, velocities, 0)

    def outflow(l):
        v, w = full[1, l], full[2, l]
        return (full[0, l + 1] - full[0, l]) + (up(v, 0) - v) + (up(w, 1) - w)

    def pressures(l, carry):
        good = inside(yz, place[0] * BX + l - XL, sizes[0])
        ev, ew = grid(9, l), grid(10, l)
        cell = (grid(8, l) + grid(8, l + 1)) + (ev + up(ev, 0)) + (ew + up(ew, 1))
        full[3, l] = jnp.where(good, grid(3, l) - (0.5 / 6.0) * cell * (grid(7, l) + outflow(l)), 0.0)
        return carry

    loop(1, NL - 2, pressures, 0)

    def layer_residual(c, l):
        u = full[c, l]
        us = neighbours(full[c, l - 1], u, full[c, l + 1])
        ks = weights(c, l)
        p = full[3, l]
        before = full[3, l - 1] if c == 0 else down(p, c - 1)
        return grid(4 + c, l) - (p - before) - 0.5 * (total(ks) * u - weigh(ks, us))

    def residuals(m, carry):
        l = XL + 2 * m
        for c in range(3):
            rsum[c, m] = layer_residual(c, l) + layer_residual(c, l + 1)
        rsum[3, m] = (grid(7, l) + outflow(l)) + (grid(7, l + 1) + outflow(l + 1))
        return carry

    loop(0, 5, residuals, 0)
    for i in range(4):
        rsum[i, 5] = jnp.zeros((ROWS, LANES), F32)
    for c in range(3):
        for m in range(6):
            rsum[4 + c, m] = grid(8 + c, XL + 2 * m) + grid(8 + c, XL + 2 * m + 1)

    matrix = compact_matrix()
    for f in range(7):
        tsum[6 * f : 6 * f + 6] = exact_dot(rsum[f].reshape(6 * ROWS, LANES), matrix).reshape(6, ROWS, BZ)
    for f in MID:
        rows_sent = mid_above(f, 1)
        for m in range(mid_above(f, 0)):
            i = 6 * f + m
            a = tsum[i, pl.ds(0, 8, stride=2), :] + tsum[i, pl.ds(1, 8, stride=2), :]
            at = MX_DOWN[f, m]
            to_down[at : at + rows_sent] = a[:rows_sent]
            if m < 4:
                middle[f, m] = a
            if (f, m) in MX_UP:
                at = MX_UP[f, m]
                to_up[at : at + rows_sent] = a[:rows_sent]


def sizes_of(c):
    return (ROWS if c == 1 else BY), (LANES if c == 2 else BZ)


def last_terms(sizes, place, whole, fine, sums, base, inv, cells, pbase):
    fyz = fine_mask_args(place, sizes)

    def grid(f, l):
        return whole[f, l]

    for x in range(9):
        l = x + XL
        good = inside(fyz, place[0] * BX + x, sizes[0])
        p = fine[3, l]
        for c in range(3):
            u, e = fine[c, l], grid(8 + c, l)
            us = neighbours(fine[c, l - 1], u, fine[c, l + 1])
            xp, ym, yp, zm, zp = pair_sums(e, grid(8 + c, l + 1))
            ks = (e + grid(8 + c, l - 1), xp, ym, yp, zm, zp)
            before = fine[3, l - 1] if c == 0 else down(p, c - 1)
            push = 1.2 * (grid(4 + c, l) - (p - before)) + 0.6 * weigh(ks, us)
            over = 1.0 / total(ks)
            rows, lanes = sizes_of(c)
            for i, k in enumerate(ks):
                sums[c, i, x, 0:rows, 0:lanes] = (0.6 * k)[0:rows, 0:lanes]
            base[c, x, 0:rows, 0:lanes] = jnp.where(good, 0.4 * u + push * over, 0.0)[0:rows, 0:lanes]
            inv[c, x, 0:rows, 0:lanes] = jnp.where(good, over, 0.0)[0:rows, 0:lanes]
            if x < BX and c == 0:
                cell = e + grid(8, l + 1)
            elif x < BX:
                cell = cell + (yp if c == 1 else zp)
        if x < BX:
            cell = (0.5 / 6.0) * cell
            cells[x] = cell[0:BY, 0:BZ]
            pbase[x] = (p - cell * grid(7, l))[0:BY, 0:BZ]


def pack_y_mid(own, from_low, from_high, to_down, to_up, rows):
    for f in MID:
        below, above = mid_below(f), mid_above(f, 1)
        for l in range(ML):
            if l not in MID_LAYERS[f]:
                rows[f, l] = jnp.zeros((4, BZ), F32)
                continue
            m = l - 4
            if m < 0:
                at = MX_UP[f, 4 + m]
                tile = from_low[at : at + above]
            elif m < 4:
                tile = own[f, m, 0:above]
            else:
                at = MX_DOWN[f, m - 4]
                tile = from_high[at : at + above]
            at = MY_DOWN[f, l]
            to_down[at : at + above] = tile
            at = MY_UP[f, l]
            to_up[at : at + below] = tile[4 - below : 4]
            rows[f, l] = tile[0:4]


def coarse_levels(
    sizes, place, last_sums, base, inv, cells, pbase, own, y_low, y_high, out,
    mid, sums, um, over, dm, f2, e2, low, sm, twice, spread, un,
):
    keep_low, keep_high = kept(place, sizes)
    for f in MID:
        below, above = mid_below(f), mid_above(f, 1)
        for l in range(ML):
            mid[f, l] = jnp.zeros((ROWS, BZ), F32)
            mid[f, l, 0:4] = own[f, l]
            if l in MID_LAYERS[f]:
                at = MY_DOWN[f, l]
                mid[f, l, 4 : 4 + above] = y_high[at : at + above] * keep_high[:above]
                at = MY_UP[f, l]
                mid[f, l, ROWS - below :] = y_low[at : at + below] * keep_low[:below]

    shape = (ROWS, BZ)
    yz = inside_yz(place, ROWS, BZ, sizes[1] // 2, sizes[2] // 2, 10, 4, BZ // 2 + 8, 8, BY // 2, BZ // 2)
    row_even = iota(shape, 0) % 2 == 0
    lane_even = iota(shape, 1) % 2 == 0

    def mid_inside(l):
        return inside(yz, place[0] * (BX // 2) + l - 4, sizes[0] // 2)

    for c in range(3):
        sums[c, 0, 1] = mid[4 + c, 0] + mid[4 + c, 1]

    def first_velocities(l, carry):
        good = mid_inside(l)
        for c in range(3):
            xp, ym, yp, zm, zp = pair_sums(mid[4 + c, l], mid[4 + c, l + 1])
            diag = total([sums[c, 0, l], xp, ym, yp, zm, zp])
            sums[c, 0, l + 1] = xp
            sums[c, 1, l] = ym
            sums[c, 2, l] = yp
            sums[c, 3, l] = zm
            sums[c, 4, l] = zp
            dm[c, l] = diag
            inverse = 1.0 / diag
            over[c, l] = inverse
            um[c, l] = jnp.where(good, 4.8 * mid[c, l] * inverse, 0.0)
        return carry

    loop(1, 13, first_velocities, 0)

    def weights(c, l):
        return (sums[c, 0, l], sums[c, 0, l + 1]) + tuple(sums[c, i, l] for i in range(1, 5))

    def outflow(v, l):
        b, w = v[1, l], v[2, l]
        return (v[0, l + 1] - v[0, l]) + (up(b, 0) - b) + (up(w, 1) - w)

    def mid_cell(l):
        return sums[0, 0, l + 1] + sums[1, 2, l] + sums[2, 4, l]

    def first_pressures(l, carry):
        q = mid[3, l] + 0.5 * outflow(um, l)
        um[3, l] = jnp.where(mid_inside(l), (-0.5 / 6.0) * mid_cell(l) * q, 0.0)
        return carry

    loop(1, 12, first_pressures, 0)

    def expand(a):
        a = a + up(a, 0)
        a = jnp.where(row_even, a, down(a, 0))
        a = a + up(a, 1)
        return 0.125 * jnp.where(lane_even, a, down(a, 1))

    def layer_residual(c, l):
        u = um[c, l]
        us = neighbours(um[c, l - 1], u, um[c, l + 1])
        p = um[3, l]
        before = um[3, l - 1] if c == 0 else down(p, c - 1)
        return mid[c, l] - 0.5 * (p - before) - 0.125 * (dm[c, l] * u - weigh(weights(c, l), us))

    def residuals(k, carry):
        l = 2 + 2 * k
        for c in range(3):
            f2[c, k] = expand(layer_residual(c, l) + layer_residual(c, l + 1))
        f2[3, k] = expand((mid[3, l] + 0.5 * outflow(um, l)) + (mid[3, l + 1] + 0.5 * outflow(um, l + 1)))
        return carry

    loop(0, 5, residuals, 0)

    def low_viscosity(k, carry):
        for c in range(3):
            e2[c, k] = expand(mid[4 + c, 2 * k] + mid[4 + c, 2 * k + 1])
        return carry

    loop(0, 7, low_viscosity, 0)

    def low_inside(k):
        return inside(yz, place[0] * (BX // 4) + k - 1, sizes[0] // 4)

    def low_velocities(k, carry):
        good = low_inside(k)
        for c in range(3):
            e = e2[c, k + 1]
            diag = 6.0 * e + total(neighbours(e2[c, k], e, e2[c, k + 2], 2))
            low[c, k] = jnp.where(good, 19.2 * f2[c, k] / diag, 0.0)
        return carry

    loop(0, 5, low_velocities, 0)

    def low_pressures(k, carry):
        v, w, ev, ew = low[1, k], low[2, k], e2[1, k + 1], e2[2, k + 1]
        flow = (low[0, k + 1] - low[0, k]) + (up(v, 0, 2) - v) + (up(w, 1, 2) - w)
        cell = (e2[0, k + 1] + e2[0, k + 2]) + (ev + up(ev, 0, 2)) + (ew + up(ew, 1, 2))
        low[3, k] = jnp.where(low_inside(k), (-0.5 / 6.0) * cell * (f2[3, k] + 0.25 * flow), 0.0)
        return carry

    loop(0, 4, low_pressures, 0)

    def corrected(k, carry):
        for i in range(3):
            um[i, 2 * k + 2] = um[i, 2 * k + 2] + low[i, k]
            um[i, 2 * k + 3] = um[i, 2 * k + 3] + low[i, k]
        return carry

    loop(0, 5, corrected, 0)
    for k in range(4):
        um[3, 2 * k + 2] = um[3, 2 * k + 2] + low[3, k]
        um[3, 2 * k + 3] = um[3, 2 * k + 3] + low[3, k]

    def second_velocities(l, carry):
        good = mid_inside(l)
        p = um[3, l]
        for c in range(3):
            u = um[c, l]
            us = neighbours(um[c, l - 1], u, um[c, l + 1])
            before = um[3, l - 1] if c == 0 else down(p, c - 1)
            push = 4.8 * (mid[c, l] - 0.5 * (p - before)) + 0.6 * weigh(weights(c, l), us)
            sm[c, l] = jnp.where(good, 0.4 * u + push * over[c, l], 0.0)
        return carry

    loop(3, 10, second_velocities, 0)

    def second_pressures(l, carry):
        q = mid[3, l] + 0.5 * outflow(sm, l)
        sm[3, l] = jnp.where(mid_inside(l), um[3, l] - (0.5 / 6.0) * mid_cell(l) * q, 0.0)
        return carry

    loop(3, 9, second_pressures, 0)

    last_row = iota((8, BZ), 0) == 7
    for i in range(4):
        for m in range(6):
            a = sm[i, 3 + m]
            a = jnp.where(last_row, a[8:16], a[0:8])
            twice[6 * i + m, pl.ds(0, 8, stride=2), :] = a
            twice[6 * i + m, pl.ds(1, 8, stride=2), :] = a
    matrix = spread_matrix()
    for i in range(4):
        wide = exact_dot(twice[6 * i : 6 * i + 6].reshape(6 * ROWS, BZ), matrix)
        spread[i] = wide.reshape(6, ROWS, LANES)

    for m in range(1, 6):
        p = spread[3, m]
        for c in range(3):
            rows, lanes = sizes_of(c)
            z = spread[c, m]
            sides = (down(z, 0), up(z, 0), down(z, 1), up(z, 1))
            for x in (2 * m - 2, 2 * m - 1):
                if x > BX:
                    continue
                zs = (spread[c, (x + 1) // 2], spread[c, (x + 3) // 2]) + sides
                push = weigh([last_sums[c, i, x, 0:rows, 0:lanes] for i in range(6)], [v[0:rows, 0:lanes] for v in zs])
                if c > 0:
                    push = push - 1.2 * (p - down(p, c - 1))[0:rows, 0:lanes]
                elif x % 2 == 0:
                    push = push - 1.2 * (p - spread[3, m - 1])[0:rows, 0:lanes]
                u = base[c, x, 0:rows, 0:lanes] + 0.4 * z[0:rows, 0:lanes] + inv[c, x, 0:rows, 0:lanes] * push
                un[c, x, 0:rows, 0:lanes] = u
                if x < BX:
                    out[c, x] = u[0:BY, 0:BZ]

    for x in range(BX):
        v, w = un[1, x, :, 0:BZ], un[2, x, 0:BY, :]
        flow = un[0, x + 1, 0:BY, 0:BZ] - un[0, x, 0:BY, 0:BZ]
        flow = flow + (up(v, 0) - v)[0:BY] + (up(w, 1) - w)[:, 0:BZ]
        out[3, x] = pbase[x] + spread[3, (x + 2) // 2, 0:BY, 0:BZ] - cells[x] * flow


WIDE, TILE, HUGE = (ROWS, BZ), (BY, BZ), (ROWS, LANES)
HALF = (11, NL, BY, LANES)
FINE_OUT = [(11, NL) + HUGE, (4, NL) + HUGE, (7, 4) + TILE, (MX_DOWN_ROWS, BZ), (MX_UP_ROWS, BZ)]
FINE_SCRATCH = [(11, NL + 4) + TILE, (7, 6) + HUGE, (42,) + WIDE]
LAST_OUT = [(3, 6, 9) + HUGE, (3, 9) + HUGE, (3, 9) + HUGE, (BX,) + TILE, (BX,) + TILE]
COARSE_SCRATCH = [
    (7, ML) + WIDE, (3, 5, ML) + WIDE, (4, ML) + WIDE, (3, ML) + WIDE, (3, ML) + WIDE, (4, 5) + WIDE, (3, 7) + WIDE,
    (4, 5) + WIDE, (4, ML) + WIDE, (24,) + WIDE, (4, 6) + HUGE, (3, 9) + HUGE,
]


def per_device(sizes, iterate, forcing, viscosity):
    nx, ny, nz = (lax.axis_size(a) for a in ("gx", "gy", "gz"))
    at = [lax.axis_index(a) for a in ("gx", "gy", "gz")]
    place = jnp.stack([jnp.full((BY, BZ), a, jnp.int32) for a in at + [at[2] % 2]])

    def swap(a, axis, count, start):
        pairs = []
        for i in range(start, count - 1, 2):
            pairs += [(i, i + 1), (i + 1, i)]
        return lax.ppermute(a, axis, pairs)

    def around(a, axis, count, by):
        return lax.ppermute(a, axis, [(i, (i + by) % count) for i in range(count)])

    def to_next(a, axis, count):
        return lax.ppermute(a, axis, [(i, i + 1) for i in range(count - 1)])

    def to_previous(a, axis, count):
        return lax.ppermute(a, axis, [(i + 1, i) for i in range(count - 1)])

    iterate, forcing, viscosity = (
        pltpu.with_memory_space_constraint(a, pltpu.HBM) for a in (iterate, forcing, viscosity)
    )
    tile = (BY, BZ)
    own, first, second = call(
        pack_z, [(11, BX) + tile, (11,) + tile, (NEAR_TILES,) + tile], [pltpu.SemaphoreType.DMA((3,))],
        place, iterate, forcing, viscosity, space=HBM,
    )
    first = swap(first, "gz", nz, 1)
    second = swap(second, "gz", nz, 0)

    upward, downward = call(pack_x, [(X_UP_TILES,) + tile, (X_DOWN_TILES,) + tile], [], place, own, first, second)
    x_low = to_next(upward, "gx", nx)
    x_high = to_previous(downward, "gx", nx)

    upward, downward = call(
        pack_y, [(Y_UP_ROWS, BZ), (Y_DOWN_ROWS, BZ)], [], place, own, first, second, x_low, x_high
    )
    y_low = around(upward, "gy", ny, 1)
    y_high = around(downward, "gy", ny, -1)
    (half,) = call(assemble_own, [HALF], [], place, own, first, second, x_low, x_high)

    whole, fine, middle, downward, upward = call(
        functools.partial(fine_level, sizes), FINE_OUT, FINE_SCRATCH, place, half, y_low, y_high
    )
    x_low = to_next(upward, "gx", nx)
    x_high = to_previous(downward, "gx", nx)

    downward, upward, middle = call(
        pack_y_mid, [(MY_DOWN_ROWS, BZ), (MY_UP_ROWS, BZ), (7, ML, 4, BZ)], [], middle, x_low, x_high
    )
    y_low = around(upward, "gy", ny, 1)
    y_high = around(downward, "gy", ny, -1)

    terms = call(functools.partial(last_terms, sizes), LAST_OUT, [], place, whole, fine)
    (updated,) = call(
        functools.partial(coarse_levels, sizes), [(4, BX) + tile], COARSE_SCRATCH,
        place, *terms, middle, y_low, y_high,
    )
    return updated


def solution(mesh):
    spec = P(None, "gx", "gy", "gz")
    sizes = (mesh.shape["gx"] * BX, mesh.shape["gy"] * BY, mesh.shape["gz"] * BZ)
    return jax.shard_map(
        functools.partial(per_device, sizes), mesh=mesh, in_specs=(spec,) * 3, out_specs=spec, check_vma=False
    )
```

```python
import functools

import jax
import jax.numpy as jnp
from jax import lax
from jax.experimental import pallas as pl
from jax.experimental.pallas import tpu as pltpu
from jax.sharding import PartitionSpec as P

F32 = jnp.float32
BX, BY, BZ = 8, 8, 128
XL, XH = 2, 4
NL = BX + XL + XH
ROWS, LANES = 16, 256
ML = 14
VMEM = pl.BlockSpec(memory_space=pltpu.VMEM)
HBM = pl.BlockSpec(memory_space=pltpu.HBM)
UNROLL = True
PARAMS = pltpu.CompilerParams(vmem_limit_bytes=20 * 1024 * 1024)


def call(kernel, outs, scratch, *args, space=VMEM):
    specs = [VMEM if a.dtype == jnp.int32 else space for a in args]
    return pl.pallas_call(
        kernel,
        out_shape=[jax.ShapeDtypeStruct(s, F32) for s in outs],
        in_specs=specs,
        out_specs=[VMEM] * len(outs),
        scratch_shapes=[pltpu.VMEM(s, F32) if isinstance(s, tuple) else s for s in scratch],
        compiler_params=PARAMS,
    )(*args)


def loop(start, stop, body, carry):
    return lax.fori_loop(start, stop, body, carry, unroll=UNROLL)


def iota(shape, dim):
    return lax.broadcasted_iota(jnp.int32, shape, dim)


def up(a, dim, by=1):
    return pltpu.roll(a, a.shape[dim] - by, dim)


def down(a, dim, by=1):
    return pltpu.roll(a, by, dim)


def lane_roll(a, by):
    by = by % a.shape[1]
    return pltpu.roll(a, by, 1) if by else a


def fine_above(f, dim):
    own = f % 4 == dim and f != 3
    return (3, 2, 3)[f // 4] + own if f % 4 < 3 else (3, 2)[f // 4]


def fine_below(f):
    return 1 if 4 <= f < 8 else 2


def mid_above(f, dim):
    return (4, 5)[f // 4] + (f % 4 == dim and f != 3)


def mid_below(f):
    return (3, 4)[f // 4]


def offsets(entries):
    table, at = {}, 0
    for key, rows in entries:
        table[key] = at
        at += rows
    return table, -(-at // 8) * 8


FINE, MID = range(11), range(7)
X_UP, X_UP_TILES = offsets(
    [((f, x), 1) for f in FINE for x in range(BX - fine_below(f), BX)] + [((f, "z"), 1) for f in FINE]
)
X_DOWN, X_DOWN_TILES = offsets(
    [((f, x), 1) for f in FINE for x in range(fine_above(f, 0))] + [((f, "z"), 1) for f in FINE]
)
FINE_LAYERS = {
    f: [x + XL for x in range(-fine_below(f), BX + fine_above(f, 0))] + list(range(NL, NL + 4)) for f in FINE
}
Y_UP, Y_UP_ROWS = offsets([((f, l), fine_below(f)) for f in FINE for l in FINE_LAYERS[f]])
Y_DOWN, Y_DOWN_ROWS = offsets([((f, l), fine_above(f, 1)) for f in FINE for l in FINE_LAYERS[f]])
MX_UP, MX_UP_ROWS = offsets([((f, m), mid_above(f, 1)) for f in MID for m in range(4 - mid_below(f), 4)])
MX_DOWN, MX_DOWN_ROWS = offsets([((f, m), mid_above(f, 1)) for f in MID for m in range(mid_above(f, 0))])
MID_LAYERS = {f: [m + 4 for m in range(-mid_below(f), 4 + mid_above(f, 0))] for f in MID}
MY_UP, MY_UP_ROWS = offsets([((f, l), mid_below(f)) for f in MID for l in MID_LAYERS[f]])
MY_DOWN, MY_DOWN_ROWS = offsets([((f, l), mid_above(f, 1)) for f in MID for l in MID_LAYERS[f]])


def pack_z(place, iterate, forcing, viscosity, own, first, second, sems):
    parts = [(iterate, f, f) for f in range(4)] + [(forcing, f, 4 + f) for f in range(4)]
    parts += [(viscosity, f, 8 + f) for f in range(3)]
    copies = [pltpu.make_async_copy(source.at[f], own.at[at], sems.at[at]) for source, f, at in parts]
    for copy in copies:
        copy.start()
    lane = iota((BY, BZ), 1) // 16
    odd = place[3] == 1
    for copy, (_, _, at) in zip(copies, parts):
        copy.wait()
        for f in (at,):
            low = jnp.zeros((BY, BZ), F32)
            high = jnp.zeros((BY, BZ), F32)
            for x in range(BX):
                a = own[f, x]
                mine = lane == x
                low = jnp.where(mine, lane_roll(a, 16 * x - 112), low)
                high = jnp.where(mine, lane_roll(a, 16 * x), high)
            first[f] = jnp.where(odd, low, high)
            second[f] = jnp.where(odd, high, low)


def strips(place, first, second, f):
    odd = place[3] == 1
    a, b = first[f], second[f]
    return jnp.where(odd, b, a), jnp.where(odd, a, b)


def pack_x(place, own, first, second, to_up, to_down):
    lane = iota((BY, BZ), 1)
    for f in FINE:
        low, high = strips(place, first, second, f)
        to_up[X_UP[f, "z"]] = jnp.where(lane >= 96, low, lane_roll(high, -32))
        to_down[X_DOWN[f, "z"]] = jnp.where(lane < 64, low, lane_roll(high, 64))
        for x in range(BX - fine_below(f), BX):
            to_up[X_UP[f, x]] = own[f, x]
        for x in range(fine_above(f, 0)):
            to_down[X_DOWN[f, x]] = own[f, x]


def fine_tile(own, from_low, from_high, f, l):
    x = l - XL
    if 0 <= x < BX:
        return own[f, x]
    if x < 0:
        return from_low[X_UP[f, BX + x]] if -x <= fine_below(f) else None
    return from_high[X_DOWN[f, x - BX]] if x - BX < fine_above(f, 0) else None


def strip_tiles(place, first, second, from_low, from_high, f):
    low, high = strips(place, first, second, f)
    return [low, high, from_low[X_UP[f, "z"]], from_high[X_DOWN[f, "z"]]]


def pack_y(place, own, first, second, from_low, from_high, to_up, to_down):
    for f in FINE:
        sides = strip_tiles(place, first, second, from_low, from_high, f)
        below, above = fine_below(f), fine_above(f, 1)
        for l in FINE_LAYERS[f]:
            tile = sides[l - NL] if l >= NL else fine_tile(own, from_low, from_high, f, l)
            at = Y_UP[f, l]
            to_up[at : at + below] = tile[BY - below :, :]
            at = Y_DOWN[f, l]
            to_down[at : at + above] = tile[:above, :]


def widen(tile, rows, lanes):
    tile = jnp.concatenate([tile] * (rows // BY), axis=0) if rows > BY else tile
    return jnp.concatenate([tile] * (lanes // BZ), axis=1) if lanes > BZ else tile


def inside_yz(place, rows, lanes, ny, nz, end_y, low_y, end_z, low_z, by, bz):
    y = iota((rows, lanes), 0)
    z = iota((rows, lanes), 1)
    held = ((y < end_y) | (y >= rows - low_y)) & ((z < end_z) | (z >= lanes - low_z))
    y = jnp.where(y < end_y, y, y - rows) + widen(place[1] * by, rows, lanes)
    z = jnp.where(z < end_z, z, z - lanes) + widen(place[2] * bz, rows, lanes)
    return jnp.where(held & (y >= 0) & (y < ny) & (z >= 0) & (z < nz), 1, 0)


def inside(yz, x, nx):
    ok = jnp.where((x >= 0) & (x < nx), 1, 0)
    return (yz * widen(ok, *yz.shape)) != 0


def neighbours(low, mid, high, by=1):
    return (low, high, down(mid, 0, by), up(mid, 0, by), down(mid, 1, by), up(mid, 1, by))


def total(values):
    out = values[0]
    for v in values[1:]:
        out = out + v
    return out


def couple(e, es, vs):
    return e * total(vs) + total([a * b for a, b in zip(es, vs)])


def fine_mask_args(place, sizes):
    return inside_yz(place, ROWS, LANES, sizes[1], sizes[2], BY + XH, XL, BZ + 16, 16, BY, BZ)


def compact_matrix():
    a = iota((LANES, BZ), 0) // 2
    return jnp.where(a == iota((LANES, BZ), 1), 0.125, 0.0).astype(jnp.bfloat16)


def spread_matrix():
    a = iota((BZ, LANES), 1) // 2
    return jnp.where(a == iota((BZ, LANES), 0), 1.0, 0.0).astype(jnp.bfloat16)


def exact_dot(a, matrix):
    high = a.astype(jnp.bfloat16)
    rest = a - high.astype(F32)
    mid = rest.astype(jnp.bfloat16)
    low = (rest - mid.astype(F32)).astype(jnp.bfloat16)
    dot = functools.partial(jnp.dot, preferred_element_type=F32)
    return dot(high, matrix) + (dot(mid, matrix) + dot(low, matrix))


def kept(place, sizes):
    low = jnp.where(place[1] > 0, 1.0, 0.0)
    high = jnp.where(place[1] < sizes[1] // BY - 1, 1.0, 0.0)
    return low, high


def side_lanes(l, tiles):
    lane = iota((BY, BZ), 1)
    x = l - XL
    if x < 0:
        a, b = lane_roll(tiles[2], 16 - 16 * l), lane_roll(tiles[2], -(64 + 16 * l))
    elif x < BX:
        a, b = lane_roll(tiles[0], 112 - 16 * x), lane_roll(tiles[1], -16 * x)
    else:
        a, b = lane_roll(tiles[3], 112 - 16 * (x - BX)), lane_roll(tiles[3], -(64 + 16 * (x - BX)))
    return jnp.where(lane >= 112, a, jnp.where(lane < 16, b, 0.0))


def assemble_own(place, own, first, second, from_low, from_high, half):
    for f in FINE:
        sides = strip_tiles(place, first, second, from_low, from_high, f)
        for l in range(NL):
            body = fine_tile(own, from_low, from_high, f, l)
            half[f, l, :, 0:BZ] = jnp.zeros((BY, BZ), F32) if body is None else body
            half[f, l, :, BZ:] = side_lanes(l, sides)


def pair_sums(e, high):
    return e + high, e + down(e, 0), e + up(e, 0), e + down(e, 1), e + up(e, 1)


def weigh(weights, values):
    return total([a * b for a, b in zip(weights, values)])


def fine_level(sizes, place, half, y_low, y_high, whole, full, middle, to_down, to_up, rows, rsum, tsum):
    keep_low, keep_high = kept(place, sizes)

    for f in FINE:
        below, above = fine_below(f), fine_above(f, 1)
        for l in FINE_LAYERS[f]:
            rows[f, l] = jnp.zeros((BY, BZ), F32)
            at = Y_DOWN[f, l]
            rows[f, l, 0:above] = y_high[at : at + above] * keep_high[:above]
            at = Y_UP[f, l]
            rows[f, l, BY - below :] = y_low[at : at + below] * keep_low[:below]
        sides = [rows[f, NL + i] for i in range(4)]
        for l in range(NL):
            whole[f, l, 0:BY] = half[f, l]
            whole[f, l, BY:, 0:BZ] = rows[f, l] if l in FINE_LAYERS[f] else jnp.zeros((BY, BZ), F32)
            whole[f, l, BY:, BZ:] = side_lanes(l, sides)

    def grid(f, l):
        return whole[f, l]

    yz = fine_mask_args(place, sizes)
    for i in range(4):
        full[i, 0] = jnp.zeros((ROWS, LANES), F32)
        full[i, NL - 1] = jnp.zeros((ROWS, LANES), F32)
    full[3, NL - 2] = jnp.zeros((ROWS, LANES), F32)

    def weights(c, l):
        e = grid(8 + c, l)
        return (e + grid(8 + c, l - 1),) + pair_sums(e, grid(8 + c, l + 1))

    def velocities(l, carry):
        good = inside(yz, place[0] * BX + l - XL, sizes[0])
        p = grid(3, l)
        for c in range(3):
            u = grid(c, l)
            us = neighbours(grid(c, l - 1), u, grid(c, l + 1))
            ks = weights(c, l)
            before = grid(3, l - 1) if c == 0 else down(p, c - 1)
            push = 1.2 * (grid(4 + c, l) - (p - before)) + 0.6 * weigh(ks, us)
            full[c, l] = jnp.where(good, 0.4 * u + push / total(ks), 0.0)
        return carry

    loop(1, NL - 1, velocities, 0)

    def outflow(l):
        v, w = full[1, l], full[2, l]
        return (full[0, l + 1] - full[0, l]) + (up(v, 0) - v) + (up(w, 1) - w)

    def pressures(l, carry):
        good = inside(yz, place[0] * BX + l - XL, sizes[0])
        ev, ew = grid(9, l), grid(10, l)
        cell = (grid(8, l) + grid(8, l + 1)) + (ev + up(ev, 0)) + (ew + up(ew, 1))
        full[3, l] = jnp.where(good, grid(3, l) - (0.5 / 6.0) * cell * (grid(7, l) + outflow(l)), 0.0)
        return carry

    loop(1, NL - 2, pressures, 0)

    def layer_residual(c, l):
        u = full[c, l]
        us = neighbours(full[c, l - 1], u, full[c, l + 1])
        ks = weights(c, l)
        p = full[3, l]
        before = full[3, l - 1] if c == 0 else down(p, c - 1)
        return grid(4 + c, l) - (p - before) - 0.5 * (total(ks) * u - weigh(ks, us))

    def residuals(m, carry):
        l = XL + 2 * m
        for c in range(3):
            rsum[c, m] = layer_residual(c, l) + layer_residual(c, l + 1)
        rsum[3, m] = (grid(7, l) + outflow(l)) + (grid(7, l + 1) + outflow(l + 1))
        return carry

    loop(0, 5, residuals, 0)
    for i in range(4):
        rsum[i, 5] = jnp.zeros((ROWS, LANES), F32)
    for c in range(3):
        for m in range(6):
            rsum[4 + c, m] = grid(8 + c, XL + 2 * m) + grid(8 + c, XL + 2 * m + 1)

    matrix = compact_matrix()
    for f in range(7):
        tsum[6 * f : 6 * f + 6] = exact_dot(rsum[f].reshape(6 * ROWS, LANES), matrix).reshape(6, ROWS, BZ)
    for f in MID:
        rows_sent = mid_above(f, 1)
        for m in range(mid_above(f, 0)):
            i = 6 * f + m
            a = tsum[i, pl.ds(0, 8, stride=2), :] + tsum[i, pl.ds(1, 8, stride=2), :]
            at = MX_DOWN[f, m]
            to_down[at : at + rows_sent] = a[:rows_sent]
            if m < 4:
                middle[f, m] = a
            if (f, m) in MX_UP:
                at = MX_UP[f, m]
                to_up[at : at + rows_sent] = a[:rows_sent]


def sizes_of(c):
    return (ROWS if c == 1 else BY), (LANES if c == 2 else BZ)


def last_terms(sizes, place, whole, fine, sums, base, inv, cells, pbase):
    fyz = fine_mask_args(place, sizes)

    def grid(f, l):
        return whole[f, l]

    for x in range(9):
        l = x + XL
        good = inside(fyz, place[0] * BX + x, sizes[0])
        p = fine[3, l]
        for c in range(3):
            u, e = fine[c, l], grid(8 + c, l)
            us = neighbours(fine[c, l - 1], u, fine[c, l + 1])
            xp, ym, yp, zm, zp = pair_sums(e, grid(8 + c, l + 1))
            ks = (e + grid(8 + c, l - 1), xp, ym, yp, zm, zp)
            before = fine[3, l - 1] if c == 0 else down(p, c - 1)
            push = 1.2 * (grid(4 + c, l) - (p - before)) + 0.6 * weigh(ks, us)
            over = 1.0 / total(ks)
            rows, lanes = sizes_of(c)
            for i, k in enumerate(ks):
                sums[c, i, x, 0:rows, 0:lanes] = (0.6 * k)[0:rows, 0:lanes]
            base[c, x, 0:rows, 0:lanes] = jnp.where(good, 0.4 * u + push * over, 0.0)[0:rows, 0:lanes]
            inv[c, x, 0:rows, 0:lanes] = jnp.where(good, over, 0.0)[0:rows, 0:lanes]
            if x < BX and c == 0:
                cell = e + grid(8, l + 1)
            elif x < BX:
                cell = cell + (yp if c == 1 else zp)
        if x < BX:
            cell = (0.5 / 6.0) * cell
            cells[x] = cell[0:BY, 0:BZ]
            pbase[x] = (p - cell * grid(7, l))[0:BY, 0:BZ]


def pack_y_mid(own, from_low, from_high, to_down, to_up, rows):
    for f in MID:
        below, above = mid_below(f), mid_above(f, 1)
        for l in range(ML):
            if l not in MID_LAYERS[f]:
                rows[f, l] = jnp.zeros((4, BZ), F32)
                continue
            m = l - 4
            if m < 0:
                at = MX_UP[f, 4 + m]
                tile = from_low[at : at + above]
            elif m < 4:
                tile = own[f, m, 0:above]
            else:
                at = MX_DOWN[f, m - 4]
                tile = from_high[at : at + above]
            at = MY_DOWN[f, l]
            to_down[at : at + above] = tile
            at = MY_UP[f, l]
            to_up[at : at + below] = tile[4 - below : 4]
            rows[f, l] = tile[0:4]


def coarse_levels(
    sizes, place, last_sums, base, inv, cells, pbase, own, y_low, y_high, out,
    mid, sums, um, over, dm, f2, e2, low, sm, twice, spread, un,
):
    keep_low, keep_high = kept(place, sizes)
    for f in MID:
        below, above = mid_below(f), mid_above(f, 1)
        for l in range(ML):
            mid[f, l] = jnp.zeros((ROWS, BZ), F32)
            mid[f, l, 0:4] = own[f, l]
            if l in MID_LAYERS[f]:
                at = MY_DOWN[f, l]
                mid[f, l, 4 : 4 + above] = y_high[at : at + above] * keep_high[:above]
                at = MY_UP[f, l]
                mid[f, l, ROWS - below :] = y_low[at : at + below] * keep_low[:below]

    shape = (ROWS, BZ)
    yz = inside_yz(place, ROWS, BZ, sizes[1] // 2, sizes[2] // 2, 10, 4, BZ // 2 + 8, 8, BY // 2, BZ // 2)
    row_even = iota(shape, 0) % 2 == 0
    lane_even = iota(shape, 1) % 2 == 0

    def mid_inside(l):
        return inside(yz, place[0] * (BX // 2) + l - 4, sizes[0] // 2)

    for c in range(3):
        sums[c, 0, 1] = mid[4 + c, 0] + mid[4 + c, 1]

    def first_velocities(l, carry):
        good = mid_inside(l)
        for c in range(3):
            xp, ym, yp, zm, zp = pair_sums(mid[4 + c, l], mid[4 + c, l + 1])
            diag = total([sums[c, 0, l], xp, ym, yp, zm, zp])
            sums[c, 0, l + 1] = xp
            sums[c, 1, l] = ym
            sums[c, 2, l] = yp
            sums[c, 3, l] = zm
            sums[c, 4, l] = zp
            dm[c, l] = diag
            inverse = 1.0 / diag
            over[c, l] = inverse
            um[c, l] = jnp.where(good, 4.8 * mid[c, l] * inverse, 0.0)
        return carry

    loop(1, 13, first_velocities, 0)

    def weights(c, l):
        return (sums[c, 0, l], sums[c, 0, l + 1]) + tuple(sums[c, i, l] for i in range(1, 5))

    def outflow(v, l):
        b, w = v[1, l], v[2, l]
        return (v[0, l + 1] - v[0, l]) + (up(b, 0) - b) + (up(w, 1) - w)

    def mid_cell(l):
        return sums[0, 0, l + 1] + sums[1, 2, l] + sums[2, 4, l]

    def first_pressures(l, carry):
        q = mid[3, l] + 0.5 * outflow(um, l)
        um[3, l] = jnp.where(mid_inside(l), (-0.5 / 6.0) * mid_cell(l) * q, 0.0)
        return carry

    loop(1, 12, first_pressures, 0)

    def expand(a):
        a = a + up(a, 0)
        a = jnp.where(row_even, a, down(a, 0))
        a = a + up(a, 1)
        return 0.125 * jnp.where(lane_even, a, down(a, 1))

    def layer_residual(c, l):
        u = um[c, l]
        us = neighbours(um[c, l - 1], u, um[c, l + 1])
        p = um[3, l]
        before = um[3, l - 1] if c == 0 else down(p, c - 1)
        return mid[c, l] - 0.5 * (p - before) - 0.125 * (dm[c, l] * u - weigh(weights(c, l), us))

    def residuals(k, carry):
        l = 2 + 2 * k
        for c in range(3):
            f2[c, k] = expand(layer_residual(c, l) + layer_residual(c, l + 1))
        f2[3, k] = expand((mid[3, l] + 0.5 * outflow(um, l)) + (mid[3, l + 1] + 0.5 * outflow(um, l + 1)))
        return carry

    loop(0, 5, residuals, 0)

    def low_viscosity(k, carry):
        for c in range(3):
            e2[c, k] = expand(mid[4 + c, 2 * k] + mid[4 + c, 2 * k + 1])
        return carry

    loop(0, 7, low_viscosity, 0)

    def low_inside(k):
        return inside(yz, place[0] * (BX // 4) + k - 1, sizes[0] // 4)

    def low_velocities(k, carry):
        good = low_inside(k)
        for c in range(3):
            e = e2[c, k + 1]
            diag = 6.0 * e + total(neighbours(e2[c, k], e, e2[c, k + 2], 2))
            low[c, k] = jnp.where(good, 19.2 * f2[c, k] / diag, 0.0)
        return carry

    loop(0, 5, low_velocities, 0)

    def low_pressures(k, carry):
        v, w, ev, ew = low[1, k], low[2, k], e2[1, k + 1], e2[2, k + 1]
        flow = (low[0, k + 1] - low[0, k]) + (up(v, 0, 2) - v) + (up(w, 1, 2) - w)
        cell = (e2[0, k + 1] + e2[0, k + 2]) + (ev + up(ev, 0, 2)) + (ew + up(ew, 1, 2))
        low[3, k] = jnp.where(low_inside(k), (-0.5 / 6.0) * cell * (f2[3, k] + 0.25 * flow), 0.0)
        return carry

    loop(0, 4, low_pressures, 0)

    def corrected(k, carry):
        for i in range(3):
            um[i, 2 * k + 2] = um[i, 2 * k + 2] + low[i, k]
            um[i, 2 * k + 3] = um[i, 2 * k + 3] + low[i, k]
        return carry

    loop(0, 5, corrected, 0)
    for k in range(4):
        um[3, 2 * k + 2] = um[3, 2 * k + 2] + low[3, k]
        um[3, 2 * k + 3] = um[3, 2 * k + 3] + low[3, k]

    def second_velocities(l, carry):
        good = mid_inside(l)
        p = um[3, l]
        for c in range(3):
            u = um[c, l]
            us = neighbours(um[c, l - 1], u, um[c, l + 1])
            before = um[3, l - 1] if c == 0 else down(p, c - 1)
            push = 4.8 * (mid[c, l] - 0.5 * (p - before)) + 0.6 * weigh(weights(c, l), us)
            sm[c, l] = jnp.where(good, 0.4 * u + push * over[c, l], 0.0)
        return carry

    loop(3, 10, second_velocities, 0)

    def second_pressures(l, carry):
        q = mid[3, l] + 0.5 * outflow(sm, l)
        sm[3, l] = jnp.where(mid_inside(l), um[3, l] - (0.5 / 6.0) * mid_cell(l) * q, 0.0)
        return carry

    loop(3, 9, second_pressures, 0)

    last_row = iota((8, BZ), 0) == 7
    for i in range(4):
        for m in range(6):
            a = sm[i, 3 + m]
            a = jnp.where(last_row, a[8:16], a[0:8])
            twice[6 * i + m, pl.ds(0, 8, stride=2), :] = a
            twice[6 * i + m, pl.ds(1, 8, stride=2), :] = a
    matrix = spread_matrix()
    for i in range(4):
        wide = exact_dot(twice[6 * i : 6 * i + 6].reshape(6 * ROWS, BZ), matrix)
        spread[i] = wide.reshape(6, ROWS, LANES)

    for m in range(1, 6):
        p = spread[3, m]
        for c in range(3):
            rows, lanes = sizes_of(c)
            z = spread[c, m]
            sides = (down(z, 0), up(z, 0), down(z, 1), up(z, 1))
            for x in (2 * m - 2, 2 * m - 1):
                if x > BX:
                    continue
                zs = (spread[c, (x + 1) // 2], spread[c, (x + 3) // 2]) + sides
                push = weigh([last_sums[c, i, x, 0:rows, 0:lanes] for i in range(6)], [v[0:rows, 0:lanes] for v in zs])
                if c > 0:
                    push = push - 1.2 * (p - down(p, c - 1))[0:rows, 0:lanes]
                elif x % 2 == 0:
                    push = push - 1.2 * (p - spread[3, m - 1])[0:rows, 0:lanes]
                u = base[c, x, 0:rows, 0:lanes] + 0.4 * z[0:rows, 0:lanes] + inv[c, x, 0:rows, 0:lanes] * push
                un[c, x, 0:rows, 0:lanes] = u
                if x < BX:
                    out[c, x] = u[0:BY, 0:BZ]

    for x in range(BX):
        v, w = un[1, x, :, 0:BZ], un[2, x, 0:BY, :]
        flow = un[0, x + 1, 0:BY, 0:BZ] - un[0, x, 0:BY, 0:BZ]
        flow = flow + (up(v, 0) - v)[0:BY] + (up(w, 1) - w)[:, 0:BZ]
        out[3, x] = pbase[x] + spread[3, (x + 2) // 2, 0:BY, 0:BZ] - cells[x] * flow


WIDE, TILE, HUGE = (ROWS, BZ), (BY, BZ), (ROWS, LANES)
HALF = (11, NL, BY, LANES)
FINE_OUT = [(11, NL) + HUGE, (4, NL) + HUGE, (7, 4) + TILE, (MX_DOWN_ROWS, BZ), (MX_UP_ROWS, BZ)]
FINE_SCRATCH = [(11, NL + 4) + TILE, (7, 6) + HUGE, (42,) + WIDE]
LAST_OUT = [(3, 6, 9) + HUGE, (3, 9) + HUGE, (3, 9) + HUGE, (BX,) + TILE, (BX,) + TILE]
COARSE_SCRATCH = [
    (7, ML) + WIDE, (3, 5, ML) + WIDE, (4, ML) + WIDE, (3, ML) + WIDE, (3, ML) + WIDE, (4, 5) + WIDE, (3, 7) + WIDE,
    (4, 5) + WIDE, (4, ML) + WIDE, (24,) + WIDE, (4, 6) + HUGE, (3, 9) + HUGE,
]


def per_device(sizes, iterate, forcing, viscosity):
    nx, ny, nz = (lax.axis_size(a) for a in ("gx", "gy", "gz"))
    at = [lax.axis_index(a) for a in ("gx", "gy", "gz")]
    place = jnp.stack([jnp.full((BY, BZ), a, jnp.int32) for a in at + [at[2] % 2]])

    def swap(a, axis, count, start):
        pairs = []
        for i in range(start, count - 1, 2):
            pairs += [(i, i + 1), (i + 1, i)]
        return lax.ppermute(a, axis, pairs)

    def around(a, axis, count, by):
        return lax.ppermute(a, axis, [(i, (i + by) % count) for i in range(count)])

    def to_next(a, axis, count):
        return lax.ppermute(a, axis, [(i, i + 1) for i in range(count - 1)])

    def to_previous(a, axis, count):
        return lax.ppermute(a, axis, [(i + 1, i) for i in range(count - 1)])

    iterate, forcing, viscosity = (
        pltpu.with_memory_space_constraint(a, pltpu.HBM) for a in (iterate, forcing, viscosity)
    )
    tile = (BY, BZ)
    own, first, second = call(
        pack_z, [(11, BX) + tile, (11,) + tile, (11,) + tile], [pltpu.SemaphoreType.DMA((11,))],
        place, iterate, forcing, viscosity, space=HBM,
    )
    first = swap(first, "gz", nz, 1)
    second = swap(second, "gz", nz, 0)

    upward, downward = call(pack_x, [(X_UP_TILES,) + tile, (X_DOWN_TILES,) + tile], [], place, own, first, second)
    x_low = to_next(upward, "gx", nx)
    x_high = to_previous(downward, "gx", nx)

    upward, downward = call(
        pack_y, [(Y_UP_ROWS, BZ), (Y_DOWN_ROWS, BZ)], [], place, own, first, second, x_low, x_high
    )
    y_low = around(upward, "gy", ny, 1)
    y_high = around(downward, "gy", ny, -1)
    (half,) = call(assemble_own, [HALF], [], place, own, first, second, x_low, x_high)

    whole, fine, middle, downward, upward = call(
        functools.partial(fine_level, sizes), FINE_OUT, FINE_SCRATCH, place, half, y_low, y_high
    )
    x_low = to_next(upward, "gx", nx)
    x_high = to_previous(downward, "gx", nx)

    downward, upward, middle = call(
        pack_y_mid, [(MY_DOWN_ROWS, BZ), (MY_UP_ROWS, BZ), (7, ML, 4, BZ)], [], middle, x_low, x_high
    )
    y_low = around(upward, "gy", ny, 1)
    y_high = around(downward, "gy", ny, -1)

    terms = call(functools.partial(last_terms, sizes), LAST_OUT, [], place, whole, fine)
    (updated,) = call(
        functools.partial(coarse_levels, sizes), [(4, BX) + tile], COARSE_SCRATCH,
        place, *terms, middle, y_low, y_high,
    )
    return updated


def solution(mesh):
    spec = P(None, "gx", "gy", "gz")
    sizes = (mesh.shape["gx"] * BX, mesh.shape["gy"] * BY, mesh.shape["gz"] * BZ)
    return jax.shard_map(
        functools.partial(per_device, sizes), mesh=mesh, in_specs=(spec,) * 3, out_specs=spec, check_vma=False
    )
```
